32 devices in a mesh: pipe: 2 (over core), dp: 4 (over z), seq: 4 (over y, x).
Axes of the slice: x: 2, y: 2, z: 4, core: 2. Of those that a mesh axis runs over, the one named last changes fastest.
Arguments:
- inputs: bfloat16 [96, 1024, 1024], P('dp', 'seq'), may hold values from -6 to 6
- cotangent: bfloat16 [96, 1024, 1024], P('dp', 'seq'), may hold values from -6 to 6
- mask_flags: int32 [96, 1024], P('dp', 'seq'), may hold values from 0 to 1, as said below
- residue_types: int32 [96, 1024], P('dp', 'seq'), may hold values from 0 to 29
- predicted: int32 [96, 1024], P('dp', 'seq'), may hold values from 0 to 29
- outer_params: float32 [2, 3, 1024], P('pipe')
- narrow: bfloat16 [2, 1024, 512], P('pipe'), may hold values from -0.1875 to 0.1875
- dilated: bfloat16 [2, 5, 512, 512], P('pipe'), may hold values from -0.125 to 0.125
- restore: bfloat16 [2, 512, 1024], P('pipe'), may hold values from -0.25 to 0.25
- inner_params: float32 [2, 6, 512], P('pipe')
Outputs:
- block_output: bfloat16 [96, 1024, 1024], P('dp', 'seq', 'pipe')
- input_grad: bfloat16 [96, 1024, 1024], P('dp', 'seq', 'pipe')
- outer_grad: float32 [2, 3, 1024], P('pipe')
- narrow_grad: float32 [2, 1024, 512], P('pipe')
- dilated_grad: float32 [2, 5, 512, 512], P('pipe')
- restore_grad: float32 [2, 512, 1024], P('pipe')
- inner_grad: float32 [2, 6, 512], P('pipe')
- accuracy: int32 [2, 30], replicated
The draws below stay inside these ranges and needn't reach their ends.
Inputs may be any that keep to these rules, and one draw needn't show every extreme that they name: `mask_flags`: the first residue of every sequence is masked.
All inputs are finite; a program needn't handle non-finite values.
Results may differ from the reference program's by a relative error of at most 0.015.
Values may be sent and summed in bfloat16 or wider, within the bound.
A program may use at most 320 MiB of HBM per device.

```python
import math
import jax
import jax.numpy as jnp
import numpy as np
from jax import lax

D = 1024
INNER = 512
KERNEL = 5
FIRST_DILATION = 2
SECOND_DILATION = 4
TYPES = 30
LENGTH = 1024
REACH = 8
SEQS = 96


def draw_mask_flags(key, part):
    key = jax.random.fold_in(key, 5)
    base_key, roll_key = jax.random.split(key)
    base = jax.random.randint(base_key, (SEQS, 1), 4, 9)
    seq_pos = jnp.arange(SEQS, dtype=jnp.int32)[:, None]
    positions = jnp.arange(LENGTH, dtype=jnp.int32)[None, :]
    level = base * (SEQS + 2 * seq_pos) // SEQS
    level = level * (LENGTH + 2 * positions) // LENGTH
    rolled = jax.random.randint(roll_key, (SEQS, LENGTH), 0, 128)
    flags = (rolled < level) | (positions == 0)
    return flags.astype(jnp.int32)


def draw_outer_params(key, part):
    key = jax.random.fold_in(key, 21)
    gain_key, shift_key = jax.random.split(key)
    gains = 1.0 + 0.15 * jax.random.uniform(gain_key, (2, 1, D), jnp.float32, -1.0, 1.0)
    shifts = 0.3 * jax.random.normal(shift_key, (2, 2, D), jnp.float32)
    return jnp.concatenate([gains, shifts], axis=1)


def draw_inner_params(key, part):
    key = jax.random.fold_in(key, 33)
    gain_key, shift_key = jax.random.split(key)
    gains = 1.0 + 0.15 * jax.random.uniform(gain_key, (2, 6, INNER), jnp.float32, -1.0, 1.0)
    shifts = 0.3 * jax.random.normal(shift_key, (2, 6, INNER), jnp.float32)
    row_ids = jnp.arange(6, dtype=jnp.int32)
    gain_rows = (row_ids == 2) | (row_ids == 4)
    return jnp.where(gain_rows[None, :, None], gains, shifts)


def plant(values, rng, smallest, largest):
    longest = values.shape.index(max(values.shape))
    spots = []
    for shift in (0, 1):
        where = [jax.random.randint(jax.random.fold_in(rng, axis), (), 0, length) for axis, length in enumerate(values.shape)]
        where[longest] = (where[longest] + shift) % values.shape[longest]
        spots.append(tuple(where))
    return values.at[spots[0]].set(smallest).at[spots[1]].set(largest)


def level_of(key, shape, cuts, smallest, largest):
    loudness, own = 1.0, jax.random.fold_in(key, 6)
    for position, parts in cuts:
        steps = jnp.exp(jax.random.uniform(jax.random.fold_in(own, position), (parts,), jnp.float32, smallest / len(cuts), largest / len(cuts)))
        loudness = loudness * jnp.repeat(steps, shape[position] // parts).reshape([-1 if axis == position else 1 for axis in range(len(shape))])
    return loudness


def cumulative_ranks(count, skew):
    weights = [(1 << 20) // math.isqrt(standing ** skew) + 1 for standing in range(1, count + 1)]
    deviation = 1 + sum(weights) // (1 << 30)
    return np.cumsum(np.array([max(1, weight // deviation) for weight in weights]))


def ranked(key, dims, amount, skew):
    listing = cumulative_ranks(amount, skew)
    pick = jax.random.randint(jax.random.fold_in(key, 1), dims, 0, int(listing[amount - 1]))
    rank = jnp.searchsorted(jnp.asarray(listing, jnp.int32), pick, side="right")
    return jax.random.permutation(jax.random.fold_in(key, 2), amount)[rank].astype(jnp.int32)


def noise(own_key, extent, scale, most, cuts=(), held_as=jnp.bfloat16):
    values = scale * jax.random.normal(own_key, extent, jnp.float32)
    if cuts:
        values = values * level_of(own_key, extent, cuts, -0.22, 0.18)
    return jnp.clip(values, -most, most).astype(held_as)


def setup_inputs(seed: int = 0) -> dict:
    keys = jax.random.split(jax.random.key(seed), 11)
    inputs = noise(keys[0], (SEQS, LENGTH, D), 1.0, 6.0, ((0, 4), (1, 4)))
    cotangent = noise(keys[1], (SEQS, LENGTH, D), 1.0, 6.0, ((0, 4), (1, 4)))
    mask_flags = draw_mask_flags(jax.random.fold_in(keys[10], 71), 0)
    residue_types = plant(ranked(keys[3], (SEQS, LENGTH), TYPES, 2), jax.random.fold_in(keys[3], 3), 0, TYPES - 1).astype(jnp.int32)
    predicted = plant(jax.random.randint(keys[4], (SEQS, LENGTH), 0, TYPES), jax.random.fold_in(keys[4], 1), 0, TYPES - 1).astype(jnp.int32)
    outer_params = draw_outer_params(jax.random.fold_in(keys[10], 71), 0)
    narrow = noise(keys[6], (2, D, INNER), D ** -0.5, 0.1875, ((0, 2),))
    dilated = noise(keys[7], (2, KERNEL, INNER, INNER), (KERNEL * INNER) ** -0.5, 0.125, ((0, 2),))
    restore = noise(keys[8], (2, INNER, D), INNER ** -0.5, 0.25, ((0, 2),))
    inner_params = draw_inner_params(jax.random.fold_in(keys[10], 71), 0)
    return {"inputs": inputs, "cotangent": cotangent, "mask_flags": mask_flags, "residue_types": residue_types, "predicted": predicted, "outer_params": outer_params, "narrow": narrow, "dilated": dilated, "restore": restore, "inner_params": inner_params}


@jax.custom_vjp
def low(v):
    return lax.optimization_barrier(v.astype(jnp.bfloat16)).astype(jnp.float32)

@jax.custom_vjp
def low_back(v):
    return v

def low_keep(v):
    return (low(v), None)

def low_pass(kept, grad):
    return (grad,)

def back_keep(v):
    return (v, None)

def back_low(kept, grad):
    return (low(grad),)
low.defvjp(low_keep, low_pass)
low_back.defvjp(back_keep, back_low)
epsilon = 1e-05

def norm_act(values, gain_row, shift_row):
    average = lax.optimization_barrier(jnp.mean(values, axis=-1, keepdims=True))
    centered = values - average
    spread = lax.optimization_barrier(jnp.mean(centered * centered, axis=-1, keepdims=True))
    normed = centered * lax.rsqrt(spread + epsilon)
    return jax.nn.gelu(normed * gain_row + shift_row, approximate=False)

def matmul(left, right):
    return jnp.dot(left, right, precision=lax.Precision.HIGHEST, preferred_element_type=jnp.float32)

def bytenet_block(activation_flow, outer, inner, narrow_w, dilated_w, restore_w, dilation_factor):
    first_act = low(norm_act(activation_flow, outer[0], outer[1]))
    hidden = low_back(matmul(first_act, narrow_w) + inner[0])
    second_act = low(norm_act(hidden, inner[2], inner[3]))
    padded = jnp.pad(second_act, ((REACH, REACH), (0, 0)))
    pieces = []
    for offset in range(KERNEL):
        start_row = REACH + (offset - KERNEL // 2) * dilation_factor
        pieces.append(padded[start_row:start_row + LENGTH])
    windows = jnp.concatenate(pieces, axis=1)
    inner_width = dilated_w.shape[-1]
    mixed = low_back(matmul(windows, dilated_w.reshape(KERNEL * inner_width, inner_width)) + inner[1])
    third_act = low(norm_act(mixed, inner[4], inner[5]))
    return activation_flow + low_back(matmul(third_act, restore_w) + outer[2])

def reference(inputs, cotangent, mask_flags, residue_types, predicted, outer_params, narrow, dilated, restore, inner_params):
    weights = (outer_params.astype(jnp.float32), narrow.astype(jnp.float32), dilated.astype(jnp.float32), restore.astype(jnp.float32), inner_params.astype(jnp.float32))
    type_ids = jnp.arange(TYPES, dtype=jnp.int32)
    matches = residue_types[:, :, None] == type_ids
    right_flags = mask_flags * (predicted == residue_types).astype(jnp.int32)
    right_counts = lax.optimization_barrier(jnp.sum(jnp.where(matches, right_flags[:, :, None], 0), axis=(0, 1)))
    masked_counts = lax.optimization_barrier(jnp.sum(jnp.where(matches, mask_flags[:, :, None], 0), axis=(0, 1)))
    accuracy = jnp.stack([right_counts, masked_counts]).astype(jnp.int32)
    masked_count = jnp.sum(mask_flags)
    factor = jnp.float32(SEQS * LENGTH) / masked_count.astype(jnp.float32)

    def both_blocks(activation_flow, block_parameters):
        middle_activation = bytenet_block(activation_flow, block_parameters[0][0], block_parameters[4][0], block_parameters[1][0], block_parameters[2][0], block_parameters[3][0], FIRST_DILATION)
        return bytenet_block(middle_activation, block_parameters[0][1], block_parameters[4][1], block_parameters[1][1], block_parameters[2][1], block_parameters[3][1], SECOND_DILATION)

    def per_sequence(totals, items):
        source, grad_seq, flags = items
        result, pullback = jax.vjp(both_blocks, source.astype(jnp.float32), weights)
        seed_grad = grad_seq.astype(jnp.float32) * flags.astype(jnp.float32)[:, None] * factor
        grad_stream, grad_weights = pullback(seed_grad)
        totals = jax.tree.map(jnp.add, totals, grad_weights)
        return (totals, (result.astype(jnp.bfloat16), grad_stream.astype(jnp.bfloat16)))
    initial = jax.tree.map(jnp.zeros_like, weights)
    totals, outputs = lax.scan(per_sequence, initial, (inputs, cotangent, mask_flags))
    return (outputs[0], outputs[1], totals[0], totals[1], totals[2], totals[3], totals[4], accuracy)
```

```python
import functools

import jax
import jax.numpy as jnp
from jax import lax
from jax.experimental import pallas as pl
from jax.experimental.pallas import tpu as pltpu
from jax.sharding import PartitionSpec as P

KERNEL = 5
FIRST_DILATION = 2
SECOND_DILATION = 4
TYPES = 30
LENGTH = 1024
REACH = 8
EPSILON = 1e-05
VMEM_LIMIT = 60 << 20

f32 = jnp.float32
bf16 = jnp.bfloat16

ROOT_HALF = 0.7071067811865476
INV_ROOT_2PI = 0.3989422804014327
EXP2_SCALE = -0.5 * 1.4426950408889634


def normalized(v):
    scale = 1.0 / v.shape[-1]
    centered = v - jnp.sum(v, axis=-1, keepdims=True) * scale
    spread = jnp.sum(centered * centered, axis=-1, keepdims=True) * scale
    r = lax.rsqrt(spread + EPSILON)
    return centered * r, r


def upper(u):
    return 0.5 * lax.erf(u * ROOT_HALF) + 0.5


def norm_act(v, g, s):
    n, _ = normalized(v)
    u = n * g + s
    return (u * upper(u)).astype(bf16)


def fold(v):
    rows, width = v.shape
    return jnp.sum(v.reshape(rows // 8, 8, width), axis=0)


class Back:
    def __init__(self, v, g, s):
        self.n, self.r = normalized(v)
        self.g = g
        u = self.n * g + s
        phi = upper(u)
        self.act = (u * phi).astype(bf16)
        self.slope = phi + u * (INV_ROOT_2PI * jnp.exp2(u * u * EXP2_SCALE))

    def grad(self, e):
        p = e * self.slope
        pn = p * self.n
        scale = 1.0 / p.shape[-1]
        pg = p * self.g
        a = jnp.sum(pg, axis=-1, keepdims=True) * scale
        b = jnp.sum(pn * self.g, axis=-1, keepdims=True) * scale
        return self.r * (pg - a - self.n * b), fold(pn), fold(p)


def dot(a, b):
    return jnp.dot(a, b, preferred_element_type=f32)


def dot_nt(a, b):
    return lax.dot_general(a, b, (((1,), (1,)), ((), ())), preferred_element_type=f32)


def dot_tn(a, b):
    return lax.dot_general(a, b, (((0,), (0,)), ((), ())), preferred_element_type=f32)


def fill(pad, low, rows_ref, high):
    rows = rows_ref.shape[0]
    pad[0:REACH, :] = low.astype(f32)
    pad[REACH : REACH + rows, :] = rows_ref[...].astype(f32)
    pad[REACH + rows :, :] = high.astype(f32)


def taps(pad, rows, d, direction):
    pieces = []
    for k in range(KERNEL):
        start = REACH + direction * (k - KERNEL // 2) * d
        pieces.append(pad[start : start + rows, :].astype(bf16))
    return pieces


def row(ref, i):
    return ref[0, i : i + 1, :]


def first_half(seqs, x_ref, outer_ref, inner_ref, narrow_ref, hidden_ref, second_ref, edge_ref):
    rows = x_ref.shape[1]
    for i in range(seqs):
        act = norm_act(x_ref[i].astype(f32), row(outer_ref, 0), row(outer_ref, 1))
        hidden = dot(act, narrow_ref[0]) + row(inner_ref, 0)
        hidden_ref[i] = hidden
        second = norm_act(hidden, row(inner_ref, 2), row(inner_ref, 3))
        second_ref[i] = second
        edge_ref[0, i] = second[:REACH]
        edge_ref[1, i] = second[rows - REACH :]


def middle_half(
    seqs,
    d,
    x_ref,
    second_ref,
    halo_ref,
    outer_ref,
    inner_ref,
    dilated_ref,
    restore_ref,
    next_outer_ref,
    next_inner_ref,
    next_narrow_ref,
    mixed_ref,
    middle_ref,
    hidden_ref,
    next_second_ref,
    edge_ref,
    pads,
):
    rows = x_ref.shape[1]
    inner = inner_ref.shape[-1]
    for i in range(seqs):
        pad = pads.at[i]
        fill(pad, halo_ref[0, i], second_ref.at[i], halo_ref[1, i])
        windows = jnp.concatenate(taps(pad, rows, d, 1), axis=1)
        mixed = dot(windows, dilated_ref[0].reshape(KERNEL * inner, inner)) + row(inner_ref, 1)
        mixed_ref[i] = mixed
        third = norm_act(mixed, row(inner_ref, 4), row(inner_ref, 5))
        y = x_ref[i].astype(f32) + (dot(third, restore_ref[0]) + row(outer_ref, 2))
        middle_ref[i] = y
        act = norm_act(y, row(next_outer_ref, 0), row(next_outer_ref, 1))
        hidden = dot(act, next_narrow_ref[0]) + row(next_inner_ref, 0)
        hidden_ref[i] = hidden
        second = norm_act(hidden, row(next_inner_ref, 2), row(next_inner_ref, 3))
        next_second_ref[i] = second
        edge_ref[0, i] = second[:REACH]
        edge_ref[1, i] = second[rows - REACH :]


def start_sums(refs):
    @pl.when(pl.program_id(0) == 0)
    def _():
        for ref in refs:
            ref[...] = jnp.zeros_like(ref)


def column(flags):
    return jnp.transpose(jnp.broadcast_to(flags, (128, flags.shape[1])))


def seeded(cot, flags):
    col = column(flags)
    return cot.astype(f32) * jnp.concatenate([col] * (cot.shape[1] // 128), axis=1)


def turn(
    seqs,
    d,
    middle_ref,
    second_ref,
    halo_ref,
    cot_ref,
    flags_ref,
    outer_ref,
    inner_ref,
    dilated_ref,
    restore_ref,
    own_ref,
    other_ref,
    gm_ref,
    edge_ref,
    restore_sum,
    wide_sum,
    small_sum,
    pads,
):
    rows = middle_ref.shape[1]
    inner = inner_ref.shape[-1]
    half = own_ref.shape[-1]
    core = lax.axis_index("pipe")
    start_sums((restore_sum, wide_sum, small_sum))
    for i in range(seqs):
        pad = pads.at[i]
        fill(pad, halo_ref[0, i], second_ref.at[i], halo_ref[1, i])
        windows = jnp.concatenate(taps(pad, rows, d, 1), axis=1)
        mixed = dot(windows, dilated_ref[0].reshape(KERNEL * inner, inner)) + row(inner_ref, 1)
        back = Back(mixed, row(inner_ref, 4), row(inner_ref, 5))
        y = middle_ref[i] + (dot(back.act, restore_ref[0]) + row(outer_ref, 2))
        y = y.astype(bf16)
        left, right = y[:, :half], y[:, half:]
        own_ref[i] = jnp.where(core == 0, left, right)
        other_ref[i] = jnp.where(core == 0, right, left)
        grad_low = seeded(cot_ref[i], flags_ref[i]).astype(bf16)
        gm = block_out_back(back, grad_low, restore_ref, restore_sum, wide_sum, small_sum)
        gm_ref[i] = gm
        edge_ref[0, i] = gm[:REACH]
        edge_ref[1, i] = gm[rows - REACH :]


def block_out_back(back, grad_low, restore_ref, restore_sum, wide_sum, small_sum):
    restore_sum[...] += dot_tn(back.act, grad_low)
    wide_sum[...] += fold(grad_low.astype(f32))
    gv, gain, shift = back.grad(dot_nt(grad_low, restore_ref[0]))
    gm = gv.astype(bf16)
    small_sum[0:8] += fold(gm.astype(f32))
    small_sum[8:16] += gain
    small_sum[16:24] += shift
    return gm


def block_in_back(
    i,
    d,
    stream,
    grad_out,
    hidden_ref,
    second_ref,
    halo_ref,
    gm_ref,
    gm_halo_ref,
    outer_ref,
    inner_ref,
    narrow_ref,
    dilated_ref,
    narrow_sum,
    dilated_sum,
    wide_sum,
    small_sum,
    pad,
    gm_pad,
):
    rows = stream.shape[0]
    fill(gm_pad, gm_halo_ref[0, i], gm_ref.at[i], gm_halo_ref[1, i])
    grad_second = None
    for k, piece in enumerate(taps(gm_pad, rows, d, -1)):
        term = dot_nt(piece, dilated_ref[0, k])
        grad_second = term if grad_second is None else grad_second + term
    fill(pad, halo_ref[0, i], second_ref.at[i], halo_ref[1, i])
    windows = jnp.concatenate(taps(pad, rows, d, 1), axis=1)
    dilated_sum[...] += dot_tn(windows, gm_ref[i])
    back = Back(hidden_ref[i], row(inner_ref, 2), row(inner_ref, 3))
    gv, gain, shift = back.grad(grad_second)
    gh = gv.astype(bf16)
    small_sum[0:8] += fold(gh.astype(f32))
    small_sum[8:16] += gain
    small_sum[16:24] += shift
    first = Back(stream, row(outer_ref, 0), row(outer_ref, 1))
    narrow_sum[...] += dot_tn(first.act, gh)
    gx, gain, shift = first.grad(dot_nt(gh, narrow_ref[0]))
    wide_sum[0:8] += gain
    wide_sum[8:16] += shift
    return grad_out + gx


def between(
    seqs,
    d,
    middle_ref,
    cot_ref,
    flags_ref,
    hidden_ref,
    second_ref,
    halo_ref,
    gm_ref,
    gm_halo_ref,
    outer_ref,
    inner_ref,
    narrow_ref,
    dilated_ref,
    mixed_ref,
    lower_inner_ref,
    lower_restore_ref,
    gx_ref,
    lower_gm_ref,
    edge_ref,
    narrow_sum,
    dilated_sum,
    wide_sum,
    small_sum,
    lower_restore_sum,
    lower_wide_sum,
    lower_small_sum,
    pads,
    gm_pads,
):
    rows = middle_ref.shape[1]
    start_sums(
        (
            narrow_sum,
            dilated_sum,
            wide_sum,
            small_sum,
            lower_restore_sum,
            lower_wide_sum,
            lower_small_sum,
        )
    )
    for i in range(seqs):
        gx = block_in_back(
            i,
            d,
            middle_ref[i],
            seeded(cot_ref[i], flags_ref[i]),
            hidden_ref,
            second_ref,
            halo_ref,
            gm_ref,
            gm_halo_ref,
            outer_ref,
            inner_ref,
            narrow_ref,
            dilated_ref,
            narrow_sum,
            dilated_sum,
            wide_sum,
            small_sum,
            pads.at[i],
            gm_pads.at[i],
        )
        gx_ref[i] = gx
        lower = Back(mixed_ref[i], row(lower_inner_ref, 4), row(lower_inner_ref, 5))
        gm = block_out_back(
            lower,
            gx.astype(bf16),
            lower_restore_ref,
            lower_restore_sum,
            lower_wide_sum,
            lower_small_sum,
        )
        lower_gm_ref[i] = gm
        edge_ref[0, i] = gm[:REACH]
        edge_ref[1, i] = gm[rows - REACH :]


def last_half(
    seqs,
    d,
    x_ref,
    gx_ref,
    hidden_ref,
    second_ref,
    halo_ref,
    gm_ref,
    gm_halo_ref,
    outer_ref,
    inner_ref,
    narrow_ref,
    dilated_ref,
    own_ref,
    other_ref,
    narrow_sum,
    dilated_sum,
    wide_sum,
    small_sum,
    pads,
    gm_pads,
):
    half = own_ref.shape[-1]
    core = lax.axis_index("pipe")
    start_sums((narrow_sum, dilated_sum, wide_sum, small_sum))
    for i in range(seqs):
        gx = block_in_back(
            i,
            d,
            x_ref[i].astype(f32),
            gx_ref[i],
            hidden_ref,
            second_ref,
            halo_ref,
            gm_ref,
            gm_halo_ref,
            outer_ref,
            inner_ref,
            narrow_ref,
            dilated_ref,
            narrow_sum,
            dilated_sum,
            wide_sum,
            small_sum,
            pads.at[i],
            gm_pads.at[i],
        )
        gx = gx.astype(bf16)
        left, right = gx[:, :half], gx[:, half:]
        own_ref[i] = jnp.where(core == 0, left, right)
        other_ref[i] = jnp.where(core == 0, right, left)


class Caller:
    def __init__(self, name, seqs, count, base):
        self.name, self.seqs, self.count, self.base = name, seqs, count, base
        self.in_specs, self.args, self.out_specs, self.outs, self.scratch = [], [], [], [], []

    def seq(self, *arrays):
        for a in arrays:
            self.in_specs.append(pl.BlockSpec((self.seqs, *a.shape[1:]), lambda i, b: (i, 0, 0)))
            self.args.append(a)
        return self

    def own(self, *arrays):
        step = self.count // self.seqs
        for a in arrays:
            self.in_specs.append(
                pl.BlockSpec((self.seqs, *a.shape[1:]), lambda i, b: (b[0] * step + i, 0, 0))
            )
            self.args.append(a)
        return self

    def halo(self, *arrays):
        for a in arrays:
            self.in_specs.append(
                pl.BlockSpec((2, self.seqs, *a.shape[2:]), lambda i, b: (0, i, 0, 0))
            )
            self.args.append(a)
        return self

    def whole(self, *arrays):
        for a in arrays:
            zeros = (0,) * a.ndim
            self.in_specs.append(
                pl.BlockSpec(a.shape, lambda i, b, zeros=zeros: zeros, pipeline_mode=pl.Buffered(1))
            )
            self.args.append(a)
        return self

    def block(self, index, *arrays):
        for a in arrays:
            spot = (index,) + (0,) * (a.ndim - 1)
            self.in_specs.append(
                pl.BlockSpec(
                    (1, *a.shape[1:]), lambda i, b, spot=spot: spot, pipeline_mode=pl.Buffered(1)
                )
            )
            self.args.append(a)
        return self

    def out_seq(self, *shapes):
        for shape, dtype in shapes:
            self.out_specs.append(pl.BlockSpec((self.seqs, *shape), lambda i, b: (i, 0, 0)))
            self.outs.append(jax.ShapeDtypeStruct((self.count, *shape), dtype))
        return self

    def out_edge(self, width):
        self.out_specs.append(
            pl.BlockSpec((2, self.seqs, REACH, width), lambda i, b: (0, i, 0, 0))
        )
        self.outs.append(jax.ShapeDtypeStruct((2, self.count, REACH, width), bf16))
        return self

    def out_sum(self, *shapes):
        for shape in shapes:
            self.out_specs.append(pl.BlockSpec(shape, lambda i, b: (0, 0)))
            self.outs.append(jax.ShapeDtypeStruct(shape, f32))
        return self

    def pads(self, number, rows, width):
        for _ in range(number):
            self.scratch.append(pltpu.VMEM((self.seqs, rows + 2 * REACH, width), f32))
        return self

    def __call__(self, kernel):
        return pl.pallas_call(
            kernel,
            grid_spec=pltpu.PrefetchScalarGridSpec(
                num_scalar_prefetch=1,
                grid=(self.count // self.seqs,),
                in_specs=self.in_specs,
                out_specs=self.out_specs,
                scratch_shapes=self.scratch,
            ),
            out_shape=self.outs,
            compiler_params=pltpu.CompilerParams(vmem_limit_bytes=VMEM_LIMIT),
            name=self.name,
        )(self.base, *self.args)


def without_base(function, *static):
    def kernel(base_ref, *refs):
        del base_ref
        function(*static, *refs)

    return kernel


def spread(edges):
    count = lax.axis_size("seq")
    up = [(i, i + 1) for i in range(count - 1)]
    down = [(b, a) for a, b in up]
    low = lax.ppermute(edges[1], "seq", up)
    high = lax.ppermute(edges[0], "seq", down)
    return jnp.stack([low, high])


def swap(values):
    return lax.ppermute(values, "pipe", [(0, 1), (1, 0)])


def both(values):
    return lax.all_gather(values, "pipe", axis=0, tiled=True)


def shards(
    inputs,
    cotangent,
    mask_flags,
    residue_types,
    predicted,
    outer_params,
    narrow,
    dilated,
    restore,
    inner_params,
):
    core = lax.axis_index("pipe")
    base = core.astype(jnp.int32)[None]
    chip_seqs, rows, width = inputs.shape
    inner = narrow.shape[-1]
    count = chip_seqs // 2
    half = width // 2
    type_ids = jnp.arange(TYPES, dtype=jnp.int32)
    matches = residue_types[:, :, None] == type_ids
    right_flags = mask_flags * (predicted == residue_types).astype(jnp.int32)
    right_counts = jnp.sum(jnp.where(matches, right_flags[:, :, None], 0), axis=(0, 1))
    masked_counts = jnp.sum(jnp.where(matches, mask_flags[:, :, None], 0), axis=(0, 1))
    accuracy = lax.psum(jnp.stack([right_counts, masked_counts]), ("dp", "seq"))
    masked_count = jnp.sum(accuracy[1])
    factor = f32(chip_seqs * lax.axis_size("dp") * LENGTH) / masked_count.astype(f32)
    flags = (mask_flags.astype(f32) * factor)[:, None, :]

    outer2, narrow2, dilated2, restore2, inner2 = (
        both(v) for v in (outer_params, narrow, dilated, restore, inner_params)
    )

    def caller(name, seqs):
        return Caller(name, seqs, count, base)

    seqs = 1
    hidden0, second0, edge = (
        caller("first_half", seqs)
        .own(inputs)
        .block(0, outer2, inner2, narrow2)
        .out_seq(((rows, inner), f32), ((rows, inner), bf16))
        .out_edge(inner)
    )(without_base(first_half, seqs))
    halo0 = spread(edge)

    mixed0, middle, hidden1, second1, edge = (
        caller("middle_half", seqs)
        .own(inputs)
        .seq(second0)
        .halo(halo0)
        .block(0, outer2, inner2, dilated2, restore2)
        .block(1, outer2, inner2, narrow2)
        .out_seq(
            ((rows, inner), f32), ((rows, width), f32), ((rows, inner), f32), ((rows, inner), bf16)
        )
        .out_edge(inner)
        .pads(1, rows, inner)
    )(without_base(middle_half, seqs, FIRST_DILATION))
    halo1 = spread(edge)

    out_own, out_other, gm1, edge, restore_sum1, bias_sum1, upper_sum1 = (
        caller("turn", seqs)
        .seq(middle, second1)
        .halo(halo1)
        .own(cotangent, flags)
        .block(1, outer2, inner2, dilated2, restore2)
        .out_seq(((rows, half), bf16), ((rows, half), bf16), ((rows, inner), bf16))
        .out_edge(inner)
        .out_sum((inner, width), (8, width), (24, inner))
        .pads(1, rows, inner)
    )(without_base(turn, seqs, SECOND_DILATION))
    gm_halo1 = spread(edge)

    (
        gx1,
        gm0,
        edge,
        narrow_sum1,
        dilated_sum1,
        wide_sum1,
        small_sum1,
        restore_sum0,
        bias_sum0,
        upper_sum0,
    ) = (
        caller("between", seqs)
        .seq(middle)
        .own(cotangent, flags)
        .seq(hidden1, second1)
        .halo(halo1)
        .seq(gm1)
        .halo(gm_halo1)
        .block(1, outer2, inner2, narrow2, dilated2)
        .seq(mixed0)
        .block(0, inner2, restore2)
        .out_seq(((rows, width), f32), ((rows, inner), bf16))
        .out_edge(inner)
        .out_sum(
            (width, inner),
            (KERNEL * inner, inner),
            (16, width),
            (24, inner),
            (inner, width),
            (8, width),
            (24, inner),
        )
        .pads(2, rows, inner)
    )(without_base(between, seqs, SECOND_DILATION))
    gm_halo0 = spread(edge)

    in_own, in_other, narrow_sum0, dilated_sum0, wide_sum0, small_sum0 = (
        caller("last_half", seqs)
        .own(inputs)
        .seq(gx1, hidden0, second0)
        .halo(halo0)
        .seq(gm0)
        .halo(gm_halo0)
        .block(0, outer2, inner2, narrow2, dilated2)
        .out_seq(((rows, half), bf16), ((rows, half), bf16))
        .out_sum((width, inner), (KERNEL * inner, inner), (16, width), (24, inner))
        .pads(2, rows, inner)
    )(without_base(last_half, seqs, FIRST_DILATION))

    def small(bias_sum, upper_sum, wide_sum, small_sum):
        def total(v):
            return jnp.sum(v.reshape(-1, 8, v.shape[-1]), axis=1)

        outer_grad = jnp.concatenate([total(wide_sum), total(bias_sum)])
        upper_rows, lower_rows = total(upper_sum), total(small_sum)
        inner_grad = jnp.stack(
            [
                lower_rows[0],
                upper_rows[0],
                lower_rows[1],
                lower_rows[2],
                upper_rows[1],
                upper_rows[2],
            ]
        )
        return outer_grad, inner_grad

    smalls = [
        small(bias_sum0, upper_sum0, wide_sum0, small_sum0),
        small(bias_sum1, upper_sum1, wide_sum1, small_sum1),
    ]
    parts = (
        (smalls[0][0], narrow_sum0, dilated_sum0, restore_sum0, smalls[0][1]),
        (smalls[1][0], narrow_sum1, dilated_sum1, restore_sum1, smalls[1][1]),
    )
    mine = jax.tree.map(lambda a, b: jnp.where(core == 0, a, b), *parts)
    theirs = jax.tree.map(lambda a, b: jnp.where(core == 0, b, a).astype(bf16), *parts)
    mine = jax.tree.map(lambda a, b: a + swap(b).astype(f32), mine, theirs)
    totals = lax.psum(mine, ("dp", "seq"))

    def assembled(own, other):
        arrived = swap(other)
        return jnp.where(
            core == 0,
            jnp.concatenate([own, arrived]),
            jnp.concatenate([arrived, own]),
        )

    return (
        assembled(out_own, out_other),
        assembled(in_own, in_other),
        totals[0][None],
        totals[1][None],
        totals[2].reshape(1, KERNEL, inner, inner),
        totals[3][None],
        totals[4][None],
        accuracy,
    )


def solution(mesh):
    in_specs = (
        P("dp", "seq", None),
        P("dp", "seq", None),
        P("dp", "seq"),
        P("dp", "seq"),
        P("dp", "seq"),
        P("pipe", None, None),
        P("pipe", None, None),
        P("pipe", None, None, None),
        P("pipe", None, None),
        P("pipe", None, None),
    )
    out_specs = (
        P("dp", "seq", "pipe"),
        P("dp", "seq", "pipe"),
        P("pipe", None, None),
        P("pipe", None, None),
        P("pipe", None, None, None),
        P("pipe", None, None),
        P("pipe", None, None),
        P(),
    )
    return jax.shard_map(shards, mesh=mesh, in_specs=in_specs, out_specs=out_specs, check_vma=False)
```

```python
import functools

import jax
import jax.numpy as jnp
from jax import lax
from jax.experimental import pallas as pl
from jax.experimental.pallas import tpu as pltpu
from jax.sharding import PartitionSpec as P

KERNEL = 5
FIRST_DILATION = 2
SECOND_DILATION = 4
TYPES = 30
LENGTH = 1024
REACH = 8
EPSILON = 1e-05
VMEM_LIMIT = 60 << 20

f32 = jnp.float32
bf16 = jnp.bfloat16

ROOT_HALF = 0.7071067811865476
INV_ROOT_2PI = 0.3989422804014327
EXP2_SCALE = -0.5 * 1.4426950408889634


def normalized(v):
    scale = 1.0 / v.shape[-1]
    centered = v - jnp.sum(v, axis=-1, keepdims=True) * scale
    spread = jnp.sum(centered * centered, axis=-1, keepdims=True) * scale
    r = lax.rsqrt(spread + EPSILON)
    return centered * r, r


def upper(u):
    return 0.5 * lax.erf(u * ROOT_HALF) + 0.5


def norm_act(v, g, s):
    n, _ = normalized(v)
    u = n * g + s
    return (u * upper(u)).astype(bf16)


def fold(v):
    rows, width = v.shape
    return jnp.sum(v.reshape(rows // 8, 8, width), axis=0)


class Back:
    def __init__(self, v, g, s):
        self.n, self.r = normalized(v)
        self.g = g
        u = self.n * g + s
        phi = upper(u)
        self.act = (u * phi).astype(bf16)
        self.slope = phi + u * (INV_ROOT_2PI * jnp.exp2(u * u * EXP2_SCALE))

    def grad(self, e):
        p = e * self.slope
        pn = p * self.n
        scale = 1.0 / p.shape[-1]
        pg = p * self.g
        a = jnp.sum(pg, axis=-1, keepdims=True) * scale
        b = jnp.sum(pn * self.g, axis=-1, keepdims=True) * scale
        return self.r * (pg - a - self.n * b), fold(pn), fold(p)


def dot(a, b):
    return jnp.dot(a, b, preferred_element_type=f32)


def dot_nt(a, b):
    return lax.dot_general(a, b, (((1,), (1,)), ((), ())), preferred_element_type=f32)


def dot_tn(a, b):
    return lax.dot_general(a, b, (((0,), (0,)), ((), ())), preferred_element_type=f32)


def fill(pad, low, rows_ref, high):
    rows = rows_ref.shape[0]
    pad[0:REACH, :] = low.astype(f32)
    pad[REACH : REACH + rows, :] = rows_ref[...].astype(f32)
    pad[REACH + rows :, :] = high.astype(f32)


def taps(pad, rows, d, direction):
    pieces = []
    for k in range(KERNEL):
        start = REACH + direction * (k - KERNEL // 2) * d
        pieces.append(pad[start : start + rows, :].astype(bf16))
    return pieces


def row(ref, i):
    return ref[0, i : i + 1, :]


def first_half(seqs, x_ref, outer_ref, inner_ref, narrow_ref, hidden_ref, second_ref, edge_ref):
    rows = x_ref.shape[1]
    for i in range(seqs):
        act = norm_act(x_ref[i].astype(f32), row(outer_ref, 0), row(outer_ref, 1))
        hidden = dot(act, narrow_ref[0]) + row(inner_ref, 0)
        hidden_ref[i] = hidden
        second = norm_act(hidden, row(inner_ref, 2), row(inner_ref, 3))
        second_ref[i] = second
        edge_ref[0, i] = second[:REACH]
        edge_ref[1, i] = second[rows - REACH :]


def middle_half(
    seqs,
    d,
    x_ref,
    second_ref,
    halo_ref,
    outer_ref,
    inner_ref,
    dilated_ref,
    restore_ref,
    next_outer_ref,
    next_inner_ref,
    next_narrow_ref,
    mixed_ref,
    middle_ref,
    hidden_ref,
    next_second_ref,
    edge_ref,
    pads,
):
    rows = x_ref.shape[1]
    inner = inner_ref.shape[-1]
    for i in range(seqs):
        pad = pads.at[i]
        fill(pad, halo_ref[0, i], second_ref.at[i], halo_ref[1, i])
        windows = jnp.concatenate(taps(pad, rows, d, 1), axis=1)
        mixed = dot(windows, dilated_ref[0].reshape(KERNEL * inner, inner)) + row(inner_ref, 1)
        mixed_ref[i] = mixed
        third = norm_act(mixed, row(inner_ref, 4), row(inner_ref, 5))
        y = x_ref[i].astype(f32) + (dot(third, restore_ref[0]) + row(outer_ref, 2))
        middle_ref[i] = y
        act = norm_act(y, row(next_outer_ref, 0), row(next_outer_ref, 1))
        hidden = dot(act, next_narrow_ref[0]) + row(next_inner_ref, 0)
        hidden_ref[i] = hidden
        second = norm_act(hidden, row(next_inner_ref, 2), row(next_inner_ref, 3))
        next_second_ref[i] = second
        edge_ref[0, i] = second[:REACH]
        edge_ref[1, i] = second[rows - REACH :]


def last_step():
    return pl.program_id(0) == pl.num_programs(0) - 1


def write_restore(out, total):
    inner, width = total.shape
    for j in range(width // inner):
        out[j * inner : (j + 1) * inner, :] = total[:, j * inner : (j + 1) * inner].astype(bf16)


def write_joined(out, narrow_sum, dilated_sum):
    cut = narrow_sum.shape[0]
    out[:cut, :] = narrow_sum[...].astype(bf16)
    out[cut:, :] = dilated_sum[...].astype(bf16)


def start_sums(refs):
    @pl.when(pl.program_id(0) == 0)
    def _():
        for ref in refs:
            ref[...] = jnp.zeros_like(ref)


def column(flags):
    return jnp.transpose(jnp.broadcast_to(flags, (128, flags.shape[1])))


def seeded(cot, flags):
    col = column(flags)
    return cot.astype(f32) * jnp.concatenate([col] * (cot.shape[1] // 128), axis=1)


def turn(
    seqs,
    d,
    middle_ref,
    second_ref,
    halo_ref,
    cot_ref,
    flags_ref,
    outer_ref,
    inner_ref,
    dilated_ref,
    restore_ref,
    own_ref,
    other_ref,
    gm_ref,
    edge_ref,
    restore_out,
    wide_sum,
    small_sum,
    pads,
    restore_sum,
):
    rows = middle_ref.shape[1]
    inner = inner_ref.shape[-1]
    half = own_ref.shape[-1]
    core = lax.axis_index("pipe")
    start_sums((restore_sum, wide_sum, small_sum))
    for i in range(seqs):
        pad = pads.at[i]
        fill(pad, halo_ref[0, i], second_ref.at[i], halo_ref[1, i])
        windows = jnp.concatenate(taps(pad, rows, d, 1), axis=1)
        mixed = dot(windows, dilated_ref[0].reshape(KERNEL * inner, inner)) + row(inner_ref, 1)
        back = Back(mixed, row(inner_ref, 4), row(inner_ref, 5))
        y = middle_ref[i] + (dot(back.act, restore_ref[0]) + row(outer_ref, 2))
        y = y.astype(bf16)
        left, right = y[:, :half], y[:, half:]
        own_ref[i] = jnp.where(core == 0, left, right)
        other_ref[i] = jnp.where(core == 0, right, left)
        grad_low = seeded(cot_ref[i], flags_ref[i]).astype(bf16)
        gm = block_out_back(back, grad_low, restore_ref, restore_sum, wide_sum, small_sum)
        gm_ref[i] = gm
        edge_ref[0, i] = gm[:REACH]
        edge_ref[1, i] = gm[rows - REACH :]

    @pl.when(last_step())
    def _():
        write_restore(restore_out, restore_sum)


def block_out_back(back, grad_low, restore_ref, restore_sum, wide_sum, small_sum):
    restore_sum[...] += dot_tn(back.act, grad_low)
    wide_sum[...] += fold(grad_low.astype(f32))
    gv, gain, shift = back.grad(dot_nt(grad_low, restore_ref[0]))
    gm = gv.astype(bf16)
    small_sum[0:8] += fold(gm.astype(f32))
    small_sum[8:16] += gain
    small_sum[16:24] += shift
    return gm


def block_in_back(
    i,
    d,
    stream,
    grad_out,
    hidden_ref,
    second_ref,
    halo_ref,
    gm_ref,
    gm_halo_ref,
    outer_ref,
    inner_ref,
    narrow_ref,
    dilated_ref,
    narrow_sum,
    dilated_sum,
    wide_sum,
    small_sum,
    pad,
    gm_pad,
):
    rows = stream.shape[0]
    fill(gm_pad, gm_halo_ref[0, i], gm_ref.at[i], gm_halo_ref[1, i])
    grad_second = None
    for k, piece in enumerate(taps(gm_pad, rows, d, -1)):
        term = dot_nt(piece, dilated_ref[0, k])
        grad_second = term if grad_second is None else grad_second + term
    fill(pad, halo_ref[0, i], second_ref.at[i], halo_ref[1, i])
    windows = jnp.concatenate(taps(pad, rows, d, 1), axis=1)
    dilated_sum[...] += dot_tn(windows, gm_ref[i])
    back = Back(hidden_ref[i], row(inner_ref, 2), row(inner_ref, 3))
    gv, gain, shift = back.grad(grad_second)
    gh = gv.astype(bf16)
    small_sum[0:8] += fold(gh.astype(f32))
    small_sum[8:16] += gain
    small_sum[16:24] += shift
    first = Back(stream, row(outer_ref, 0), row(outer_ref, 1))
    narrow_sum[...] += dot_tn(first.act, gh)
    gx, gain, shift = first.grad(dot_nt(gh, narrow_ref[0]))
    wide_sum[0:8] += gain
    wide_sum[8:16] += shift
    return grad_out + gx


def between(
    seqs,
    d,
    middle_ref,
    cot_ref,
    flags_ref,
    hidden_ref,
    second_ref,
    halo_ref,
    gm_ref,
    gm_halo_ref,
    outer_ref,
    inner_ref,
    narrow_ref,
    dilated_ref,
    mixed_ref,
    lower_inner_ref,
    lower_restore_ref,
    gx_ref,
    lower_gm_ref,
    edge_ref,
    joined_out,
    wide_sum,
    small_sum,
    lower_restore_out,
    lower_wide_sum,
    lower_small_sum,
    pads,
    gm_pads,
    narrow_sum,
    dilated_sum,
    lower_restore_sum,
):
    rows = middle_ref.shape[1]
    start_sums(
        (
            narrow_sum,
            dilated_sum,
            wide_sum,
            small_sum,
            lower_restore_sum,
            lower_wide_sum,
            lower_small_sum,
        )
    )
    for i in range(seqs):
        gx = block_in_back(
            i,
            d,
            middle_ref[i],
            seeded(cot_ref[i], flags_ref[i]),
            hidden_ref,
            second_ref,
            halo_ref,
            gm_ref,
            gm_halo_ref,
            outer_ref,
            inner_ref,
            narrow_ref,
            dilated_ref,
            narrow_sum,
            dilated_sum,
            wide_sum,
            small_sum,
            pads.at[i],
            gm_pads.at[i],
        )
        gx_ref[i] = gx
        lower = Back(mixed_ref[i], row(lower_inner_ref, 4), row(lower_inner_ref, 5))
        gm = block_out_back(
            lower,
            gx.astype(bf16),
            lower_restore_ref,
            lower_restore_sum,
            lower_wide_sum,
            lower_small_sum,
        )
        lower_gm_ref[i] = gm
        edge_ref[0, i] = gm[:REACH]
        edge_ref[1, i] = gm[rows - REACH :]

    @pl.when(last_step())
    def _():
        write_joined(joined_out, narrow_sum, dilated_sum)
        write_restore(lower_restore_out, lower_restore_sum)


def last_half(
    seqs,
    d,
    x_ref,
    gx_ref,
    hidden_ref,
    second_ref,
    halo_ref,
    gm_ref,
    gm_halo_ref,
    outer_ref,
    inner_ref,
    narrow_ref,
    dilated_ref,
    own_ref,
    other_ref,
    joined_out,
    wide_sum,
    small_sum,
    pads,
    gm_pads,
    narrow_sum,
    dilated_sum,
):
    half = own_ref.shape[-1]
    core = lax.axis_index("pipe")
    start_sums((narrow_sum, dilated_sum, wide_sum, small_sum))
    for i in range(seqs):
        gx = block_in_back(
            i,
            d,
            x_ref[i].astype(f32),
            gx_ref[i],
            hidden_ref,
            second_ref,
            halo_ref,
            gm_ref,
            gm_halo_ref,
            outer_ref,
            inner_ref,
            narrow_ref,
            dilated_ref,
            narrow_sum,
            dilated_sum,
            wide_sum,
            small_sum,
            pads.at[i],
            gm_pads.at[i],
        )
        gx = gx.astype(bf16)
        left, right = gx[:, :half], gx[:, half:]
        own_ref[i] = jnp.where(core == 0, left, right)
        other_ref[i] = jnp.where(core == 0, right, left)

    @pl.when(last_step())
    def _():
        write_joined(joined_out, narrow_sum, dilated_sum)


MESH = pl.DeviceIdType.MESH
UNIT = 16


def bits_of(count):
    return count.bit_length() - 1


def mixed_by(core, first, second):
    return first + core * (second - first)


class Place:
    def __init__(self):
        self.core = lax.axis_index("pipe")
        self.seq = lax.axis_index("seq")
        self.dp = lax.axis_index("dp")
        seq_bits = bits_of(lax.axis_size("seq"))
        dp_bits = bits_of(lax.axis_size("dp"))
        order = list(range(seq_bits))
        cut = seq_bits // 2
        turned = order[cut:] + order[:cut]
        self.stages = [("seq", a, b) for a, b in zip(order, turned)]
        self.stages += [("dp", a, a) for a in range(dp_bits)]

    def bit(self, stage):
        axis, a, b = self.stages[stage]
        spot = self.seq if axis == "seq" else self.dp
        return mixed_by(self.core, (spot // (1 << a)) % 2, (spot // (1 << b)) % 2)

    def peer(self, stage):
        axis, a, b = self.stages[stage]
        spot = self.seq if axis == "seq" else self.dp
        hop = mixed_by(self.core, 1 << a, 1 << b) * (1 - 2 * self.bit(stage))
        return {axis: spot + hop}

    def other_core(self):
        return {"pipe": 1 - self.core}

    def greet(self):
        barrier = pltpu.get_barrier_semaphore()
        friends = [self.other_core()] + [self.peer(s) for s in range(len(self.stages))]
        for friend in friends:
            pl.semaphore_signal(barrier, inc=1, device_id=friend, device_id_type=MESH)
        pl.semaphore_wait(barrier, len(friends))


def remote(src, dst, send_sem, recv_sem, device):
    return pltpu.make_async_remote_copy(
        src_ref=src,
        dst_ref=dst,
        send_sem=send_sem,
        recv_sem=recv_sem,
        device_id=device,
        device_id_type=MESH,
    )


def group_sizes(inner, width):
    upper = KERNEL * inner // 2
    return [upper - upper // 5 * 2, upper // 5 * 2, width // 2, width // 2]


class BlockSum:
    def __init__(self, place, block, sizes, joined, restore, out, room, sems):
        self.place, self.block, self.sizes = place, block, sizes
        self.joined, self.restore, self.out = joined, restore, out
        self.own, self.theirs, self.acc, self.sbuf, self.rbuf, self.res = room
        self.core_sems, self.load_sems, self.send_sems, self.recv_sems, self.out_sems = sems
        self.levels = len(place.stages)
        self.starts = [sum(sizes[:g]) for g in range(len(sizes))]
        self.half = sum(sizes)

    @staticmethod
    def scratch(sizes, width, levels):
        rows, groups = sum(sizes), len(sizes)
        room = [
            pltpu.VMEM((rows, width), bf16),
            pltpu.VMEM((rows, width), bf16),
            pltpu.VMEM((rows, width), f32),
            pltpu.VMEM((groups, max(BlockSum.sent(n, levels) for n in sizes), width), bf16),
            pltpu.VMEM((groups, max(BlockSum.sent(n, levels) for n in sizes), width), bf16),
            pltpu.VMEM((rows, width), bf16),
        ]
        dma = pltpu.SemaphoreType.DMA
        sems = [
            dma((groups, 2)),
            dma((groups,)),
            dma((groups, 2 * levels)),
            dma((groups, 2 * levels)),
            dma((groups, 3)),
        ]
        return room, sems

    @staticmethod
    def lengths(rows, levels):
        out = [rows]
        for _ in range(levels):
            last = out[-1]
            out.append(last // 2 if last % (2 * UNIT) == 0 else last)
        return out

    @staticmethod
    def sent(rows, levels):
        return sum(BlockSum.lengths(rows, levels)[1:])

    def spots(self, g):
        lengths = self.lengths(self.sizes[g], self.levels)
        start, out = self.starts[g], []
        for s in range(self.levels):
            out.append((start, lengths[s]))
            if lengths[s + 1] < lengths[s]:
                start = start + self.place.bit(s) * lengths[s + 1]
        out.append((start, lengths[-1]))
        return out

    def source(self, g, half):
        n, at = self.sizes[g], self.starts[g] + half * self.half
        top = self.joined.shape[0]
        if at < top:
            return self.joined.at[pl.ds(at, n)]
        return self.restore.at[pl.ds(at - top, n)]

    def core_copy(self, g, half):
        at = pl.ds(self.starts[g], self.sizes[g])
        return remote(
            self.source(g, half),
            self.theirs.at[at],
            self.core_sems.at[g, 0],
            self.core_sems.at[g, 1],
            self.place.other_core(),
        )

    def load(self, g, half):
        at = pl.ds(self.starts[g], self.sizes[g])
        return pltpu.make_async_copy(self.source(g, half), self.own.at[at], self.load_sems.at[g])

    def down(self, g, s):
        lengths = self.lengths(self.sizes[g], self.levels)
        at = pl.ds(sum(lengths[1 : s + 1]), lengths[s + 1])
        return remote(
            self.sbuf.at[g, at],
            self.rbuf.at[g, at],
            self.send_sems.at[g, s],
            self.recv_sems.at[g, s],
            self.place.peer(s),
        )

    def start_down(self, g, s):
        lengths = self.lengths(self.sizes[g], self.levels)
        start, rows = self.spots(g)[s]
        to, n = sum(lengths[1 : s + 1]), lengths[s + 1]
        if n < rows:
            start = start + (1 - self.place.bit(s)) * n
        start = pl.multiple_of(start, UNIT)
        self.sbuf[g, to : to + n, :] = self.acc[pl.ds(start, n), :].astype(bf16)
        self.down(g, s).start()

    def end_down(self, g, s):
        lengths = self.lengths(self.sizes[g], self.levels)
        at, n = sum(lengths[1 : s + 1]), lengths[s + 1]
        start = pl.multiple_of(self.spots(g)[s + 1][0], UNIT)
        self.down(g, s).wait()
        kept = self.acc[pl.ds(start, n), :]
        if n == lengths[s]:
            kept = kept.astype(bf16).astype(f32)
        self.acc[pl.ds(start, n), :] = kept + self.rbuf[g, at : at + n, :].astype(f32)

    def up(self, g, s):
        lengths = self.lengths(self.sizes[g], self.levels)
        if lengths[s] == lengths[s + 1]:
            return None
        start, n = self.spots(g)[s + 1]
        at = pl.ds(pl.multiple_of(start, UNIT), n)
        return remote(
            self.res.at[at],
            self.res.at[at],
            self.send_sems.at[g, self.levels + s],
            self.recv_sems.at[g, self.levels + s],
            self.place.peer(s),
        )

    def keep(self, g, half):
        at = pl.ds(self.starts[g], self.sizes[g])
        to = pl.ds(self.starts[g] + half * self.half, self.sizes[g])
        return pltpu.make_async_copy(self.res.at[at], self.out.at[to], self.out_sems.at[g, 0])

    def give(self, g, half):
        at = pl.ds(self.starts[g], self.sizes[g])
        to = pl.ds(self.starts[g] + half * self.half, self.sizes[g])
        return remote(
            self.res.at[at],
            self.out.at[to],
            self.out_sems.at[g, 1],
            self.out_sems.at[g, 2],
            self.place.other_core(),
        )

    def steps(self):
        return 2 * self.levels + 3

    def step(self, g, t):
        core, levels = self.place.core, self.levels
        if t == 0:
            for half in (0, 1):

                @pl.when(core == half)
                def _():
                    self.core_copy(g, 1 - half).start()
                    self.load(g, half).start()

        if t == 1:
            for half in (0, 1):

                @pl.when(core == half)
                def _():
                    self.load(g, half).wait()
                    self.core_copy(g, 1 - half).wait()

            at = slice(self.starts[g], self.starts[g] + self.sizes[g])
            self.acc[at, :] = self.own[at, :].astype(f32) + self.theirs[at, :].astype(f32)
        if 2 <= t < 2 + levels:
            self.end_down(g, t - 2)
        if 1 <= t < 1 + levels:
            self.start_down(g, t - 1)
        if t == 1 + levels:
            start, n = self.spots(g)[levels]
            at = pl.ds(pl.multiple_of(start, UNIT), n)
            self.res[at, :] = self.acc[at, :].astype(bf16)
        if 2 + levels <= t < 2 + 2 * levels:
            copy = self.up(g, 2 * levels + 1 - t)
            if copy is not None:
                copy.wait()
        if 1 + levels <= t < 1 + 2 * levels:
            copy = self.up(g, 2 * levels - t)
            if copy is not None:
                copy.start()
        if t == 1 + 2 * levels:
            for half in (0, 1):

                @pl.when(core == half)
                def _():
                    if half == self.block:
                        self.keep(g, half).start()
                    else:
                        self.give(g, half).start()

        if t == 2 + 2 * levels:
            for half in (0, 1):

                @pl.when(core == half)
                def _():
                    if half == self.block:
                        self.keep(g, half).wait()
                        self.give(g, 1 - half).wait_recv()
                    else:
                        self.give(g, half).wait_send()


class SmallSum:
    def __init__(self, place, total, arrived, sems):
        self.place, self.total, self.arrived, self.sems = place, total, arrived, sems
        self.stages = len(place.stages) + 1

    @staticmethod
    def scratch(rows, width, levels):
        return [
            pltpu.VMEM((levels + 2, rows, width), f32),
            pltpu.VMEM((levels + 1, rows, width), f32),
            pltpu.SemaphoreType.DMA((levels + 1, 2)),
        ]

    def copy(self, s):
        device = self.place.other_core() if s == 0 else self.place.peer(s - 1)
        return remote(
            self.total.at[s], self.arrived.at[s], self.sems.at[s, 0], self.sems.at[s, 1], device
        )

    def start(self, s):
        self.copy(s).start()

    def end(self, s):
        self.copy(s).wait()
        self.total[s + 1] = self.total[s] + self.arrived[s]


def gather_small(total, block, bias_ref, upper_ref, wide_ref, small_ref):
    half = total.shape[-1]
    rows = []
    for ref in (wide_ref, bias_ref):
        for k in range(ref.shape[0] // 8):
            for lane in range(0, ref.shape[1], half):
                rows.append((ref, k, lane))
    for ref, k in ((small_ref, 0), (upper_ref, 0), (small_ref, 1), (small_ref, 2), (upper_ref, 1), (upper_ref, 2)):
        rows.append((ref, k, 0))
    for j, (ref, k, lane) in enumerate(rows):
        piece = ref[8 * k : 8 * k + 8, lane : lane + half]
        total[0, 16 * block + j : 16 * block + j + 1, :] = jnp.sum(piece, axis=0, keepdims=True)


def sum_all(
    sizes,
    joined0,
    restore0,
    joined1,
    restore1,
    *refs,
):
    smalls, (out, small_out), scratch = refs[:8], refs[8:10], refs[10:]
    place = Place()
    place.greet()
    levels = len(place.stages)
    sets = [
        BlockSum(place, 1, sizes, joined1, restore1, out, scratch[0:6], scratch[6:11]),
        BlockSum(place, 0, sizes, joined0, restore0, out, scratch[11:17], scratch[17:22]),
    ]
    small = SmallSum(place, *scratch[22:])
    small.total[0] = jnp.zeros_like(small.total[0])
    for block in (0, 1):
        gather_small(small.total, block, *smalls[4 * block : 4 * block + 4])
    work = [(each, g) for each in sets for g in range(len(sizes))]
    for t in range(len(work) + sets[0].steps() - 1):
        if 0 < t <= small.stages:
            small.end(t - 1)
        if t < small.stages:
            small.start(t)
        for i, (each, g) in enumerate(work):
            if 0 <= t - i < each.steps():
                each.step(g, t - i)
    small_out[...] = small.total[small.stages]


class Caller:
    def __init__(self, name, seqs, count, base):
        self.name, self.seqs, self.count, self.base = name, seqs, count, base
        self.in_specs, self.args, self.out_specs, self.outs, self.scratch = [], [], [], [], []

    def seq(self, *arrays):
        for a in arrays:
            self.in_specs.append(pl.BlockSpec((self.seqs, *a.shape[1:]), lambda i, b: (i, 0, 0)))
            self.args.append(a)
        return self

    def own(self, *arrays):
        step = self.count // self.seqs
        for a in arrays:
            self.in_specs.append(
                pl.BlockSpec((self.seqs, *a.shape[1:]), lambda i, b: (b[0] * step + i, 0, 0))
            )
            self.args.append(a)
        return self

    def halo(self, *arrays):
        for a in arrays:
            self.in_specs.append(
                pl.BlockSpec((2, self.seqs, *a.shape[2:]), lambda i, b: (0, i, 0, 0))
            )
            self.args.append(a)
        return self

    def whole(self, *arrays):
        for a in arrays:
            zeros = (0,) * a.ndim
            self.in_specs.append(
                pl.BlockSpec(a.shape, lambda i, b, zeros=zeros: zeros, pipeline_mode=pl.Buffered(1))
            )
            self.args.append(a)
        return self

    def block(self, index, *arrays):
        for a in arrays:
            spot = (index,) + (0,) * (a.ndim - 1)
            self.in_specs.append(
                pl.BlockSpec(
                    (1, *a.shape[1:]), lambda i, b, spot=spot: spot, pipeline_mode=pl.Buffered(1)
                )
            )
            self.args.append(a)
        return self

    def out_seq(self, *shapes):
        for shape, dtype in shapes:
            self.out_specs.append(pl.BlockSpec((self.seqs, *shape), lambda i, b: (i, 0, 0)))
            self.outs.append(jax.ShapeDtypeStruct((self.count, *shape), dtype))
        return self

    def out_edge(self, width):
        self.out_specs.append(
            pl.BlockSpec((2, self.seqs, REACH, width), lambda i, b: (0, i, 0, 0))
        )
        self.outs.append(jax.ShapeDtypeStruct((2, self.count, REACH, width), bf16))
        return self

    def out_sum(self, *shapes, dtype=f32):
        for shape in shapes:
            self.out_specs.append(pl.BlockSpec(shape, lambda i, b: (0, 0)))
            self.outs.append(jax.ShapeDtypeStruct(shape, dtype))
        return self

    def sums(self, *shapes):
        self.scratch += [pltpu.VMEM(shape, f32) for shape in shapes]
        return self

    def pads(self, number, rows, width):
        for _ in range(number):
            self.scratch.append(pltpu.VMEM((self.seqs, rows + 2 * REACH, width), f32))
        return self

    def __call__(self, kernel):
        return pl.pallas_call(
            kernel,
            grid_spec=pltpu.PrefetchScalarGridSpec(
                num_scalar_prefetch=1,
                grid=(self.count // self.seqs,),
                in_specs=self.in_specs,
                out_specs=self.out_specs,
                scratch_shapes=self.scratch,
            ),
            out_shape=self.outs,
            compiler_params=pltpu.CompilerParams(vmem_limit_bytes=VMEM_LIMIT),
            name=self.name,
        )(self.base, *self.args)


def without_base(function, *static):
    def kernel(base_ref, *refs):
        del base_ref
        function(*static, *refs)

    return kernel


def spread(edges):
    count = lax.axis_size("seq")
    up = [(i, i + 1) for i in range(count - 1)]
    down = [(b, a) for a, b in up]
    low = lax.ppermute(edges[1], "seq", up)
    high = lax.ppermute(edges[0], "seq", down)
    return jnp.stack([low, high])


def swap(values):
    return lax.ppermute(values, "pipe", [(0, 1), (1, 0)])


def both(values):
    return lax.all_gather(values, "pipe", axis=0, tiled=True)


def shards(
    inputs,
    cotangent,
    mask_flags,
    residue_types,
    predicted,
    outer_params,
    narrow,
    dilated,
    restore,
    inner_params,
):
    core = lax.axis_index("pipe")
    base = core.astype(jnp.int32)[None]
    chip_seqs, rows, width = inputs.shape
    inner = narrow.shape[-1]
    count = chip_seqs // 2
    half = width // 2
    type_ids = jnp.arange(TYPES, dtype=jnp.int32)
    matches = residue_types[:, :, None] == type_ids
    right_flags = mask_flags * (predicted == residue_types).astype(jnp.int32)
    right_counts = jnp.sum(jnp.where(matches, right_flags[:, :, None], 0), axis=(0, 1))
    masked_counts = jnp.sum(jnp.where(matches, mask_flags[:, :, None], 0), axis=(0, 1))
    accuracy = lax.psum(jnp.stack([right_counts, masked_counts]), ("dp", "seq"))
    masked_count = jnp.sum(accuracy[1])
    factor = f32(chip_seqs * lax.axis_size("dp") * LENGTH) / masked_count.astype(f32)
    flags = (mask_flags.astype(f32) * factor)[:, None, :]

    outer2, narrow2, dilated2, restore2, inner2 = (
        both(v) for v in (outer_params, narrow, dilated, restore, inner_params)
    )

    def caller(name, seqs):
        return Caller(name, seqs, count, base)

    seqs = 1
    hidden0, second0, edge = (
        caller("first_half", seqs)
        .own(inputs)
        .block(0, outer2, inner2, narrow2)
        .out_seq(((rows, inner), f32), ((rows, inner), bf16))
        .out_edge(inner)
    )(without_base(first_half, seqs))
    halo0 = spread(edge)

    mixed0, middle, hidden1, second1, edge = (
        caller("middle_half", seqs)
        .own(inputs)
        .seq(second0)
        .halo(halo0)
        .block(0, outer2, inner2, dilated2, restore2)
        .block(1, outer2, inner2, narrow2)
        .out_seq(
            ((rows, inner), f32), ((rows, width), f32), ((rows, inner), f32), ((rows, inner), bf16)
        )
        .out_edge(inner)
        .pads(1, rows, inner)
    )(without_base(middle_half, seqs, FIRST_DILATION))
    halo1 = spread(edge)

    joined_rows = (width + KERNEL * inner, inner)
    restore_rows = (width, inner)
    out_own, out_other, gm1, edge, restore_sum1, bias_sum1, upper_sum1 = (
        caller("turn", seqs)
        .seq(middle, second1)
        .halo(halo1)
        .own(cotangent, flags)
        .block(1, outer2, inner2, dilated2, restore2)
        .out_seq(((rows, half), bf16), ((rows, half), bf16), ((rows, inner), bf16))
        .out_edge(inner)
        .out_sum(restore_rows, dtype=bf16)
        .out_sum((8, width), (24, inner))
        .pads(1, rows, inner)
        .sums((inner, width))
    )(without_base(turn, seqs, SECOND_DILATION))
    gm_halo1 = spread(edge)

    (
        gx1,
        gm0,
        edge,
        joined1,
        wide_sum1,
        small_sum1,
        restore_sum0,
        bias_sum0,
        upper_sum0,
    ) = (
        caller("between", seqs)
        .seq(middle)
        .own(cotangent, flags)
        .seq(hidden1, second1)
        .halo(halo1)
        .seq(gm1)
        .halo(gm_halo1)
        .block(1, outer2, inner2, narrow2, dilated2)
        .seq(mixed0)
        .block(0, inner2, restore2)
        .out_seq(((rows, width), f32), ((rows, inner), bf16))
        .out_edge(inner)
        .out_sum(joined_rows, dtype=bf16)
        .out_sum((16, width), (24, inner))
        .out_sum(restore_rows, dtype=bf16)
        .out_sum((8, width), (24, inner))
        .pads(2, rows, inner)
        .sums((width, inner), (KERNEL * inner, inner), (inner, width))
    )(without_base(between, seqs, SECOND_DILATION))
    gm_halo0 = spread(edge)

    in_own, in_other, joined0, wide_sum0, small_sum0 = (
        caller("last_half", seqs)
        .own(inputs)
        .seq(gx1, hidden0, second0)
        .halo(halo0)
        .seq(gm0)
        .halo(gm_halo0)
        .block(0, outer2, inner2, narrow2, dilated2)
        .out_seq(((rows, half), bf16), ((rows, half), bf16))
        .out_sum(joined_rows, dtype=bf16)
        .out_sum((16, width), (24, inner))
        .pads(2, rows, inner)
        .sums((width, inner), (KERNEL * inner, inner))
    )(without_base(last_half, seqs, FIRST_DILATION))

    sizes = group_sizes(inner, width)
    levels = bits_of(lax.axis_size("seq")) + bits_of(lax.axis_size("dp"))
    rooms = []
    for _ in range(2):
        room, sems = BlockSum.scratch(sizes, inner, levels)
        rooms += room + sems
    rooms += SmallSum.scratch(32, inner, levels)
    anywhere, vmem = pl.BlockSpec(memory_space=pl.ANY), pl.BlockSpec(memory_space=pltpu.VMEM)
    totals, smalls = pl.pallas_call(
        functools.partial(sum_all, sizes),
        out_shape=[
            jax.ShapeDtypeStruct((2 * sum(sizes), inner), bf16),
            jax.ShapeDtypeStruct((32, inner), f32),
        ],
        in_specs=[anywhere] * 4 + [vmem] * 8,
        out_specs=[anywhere, vmem],
        scratch_shapes=rooms,
        compiler_params=pltpu.CompilerParams(
            vmem_limit_bytes=VMEM_LIMIT, collective_id=0, has_side_effects=True
        ),
        name="sum_all",
    )(
        joined0,
        restore_sum0,
        joined1,
        restore_sum1,
        *(bias_sum0, upper_sum0, wide_sum0, small_sum0),
        *(bias_sum1, upper_sum1, wide_sum1, small_sum1),
    )
    totals = totals.astype(f32)
    smalls = lax.dynamic_slice_in_dim(smalls, core * 16, 16, 0)
    narrow_total = totals[:width]
    dilated_total = totals[width : width + KERNEL * inner]
    restore_total = totals[width + KERNEL * inner :].reshape(width // inner, inner, inner)
    restore_total = jnp.concatenate(list(restore_total), axis=1)
    outer_total = smalls[: 3 * width // inner].reshape(3, width)
    inner_total = smalls[3 * width // inner :][:6]

    def assembled(own, other):
        arrived = swap(other)
        return jnp.where(
            core == 0,
            jnp.concatenate([own, arrived]),
            jnp.concatenate([arrived, own]),
        )

    return (
        assembled(out_own, out_other),
        assembled(in_own, in_other),
        outer_total[None],
        narrow_total[None],
        dilated_total.reshape(1, KERNEL, inner, inner),
        restore_total[None],
        inner_total[None],
        accuracy,
    )


def solution(mesh):
    in_specs = (
        P("dp", "seq", None),
        P("dp", "seq", None),
        P("dp", "seq"),
        P("dp", "seq"),
        P("dp", "seq"),
        P("pipe", None, None),
        P("pipe", None, None),
        P("pipe", None, None, None),
        P("pipe", None, None),
        P("pipe", None, None),
    )
    out_specs = (
        P("dp", "seq", "pipe"),
        P("dp", "seq", "pipe"),
        P("pipe", None, None),
        P("pipe", None, None),
        P("pipe", None, None, None),
        P("pipe", None, None),
        P("pipe", None, None),
        P(),
    )
    return jax.shard_map(shards, mesh=mesh, in_specs=in_specs, out_specs=out_specs, check_vma=False)
```

```python
import functools

import jax
import jax.numpy as jnp
from jax import lax
from jax.experimental import pallas as pl
from jax.experimental.pallas import tpu as pltpu
from jax.sharding import PartitionSpec as P

KERNEL = 5
FIRST_DILATION = 2
SECOND_DILATION = 4
TYPES = 30
LENGTH = 1024
REACH = 8
EPSILON = 1e-05
VMEM_LIMIT = 60 << 20

f32 = jnp.float32
bf16 = jnp.bfloat16

ROOT_HALF = 0.7071067811865476
INV_ROOT_2PI = 0.3989422804014327
EXP2_SCALE = -0.5 * 1.4426950408889634


def normalized(v):
    scale = 1.0 / v.shape[-1]
    centered = v - jnp.sum(v, axis=-1, keepdims=True) * scale
    spread = jnp.sum(centered * centered, axis=-1, keepdims=True) * scale
    r = lax.rsqrt(spread + EPSILON)
    return centered * r, r


def upper(u):
    return 0.5 * lax.erf(u * ROOT_HALF) + 0.5


def norm_act(v, g, s):
    n, _ = normalized(v)
    u = n * g + s
    return (u * upper(u)).astype(bf16)


def fold(v):
    rows, width = v.shape
    return jnp.sum(v.reshape(rows // 8, 8, width), axis=0)


class Back:
    def __init__(self, v, g, s):
        self.n, self.r = normalized(v)
        self.g = g
        u = self.n * g + s
        phi = upper(u)
        self.act = (u * phi).astype(bf16)
        self.slope = phi + u * (INV_ROOT_2PI * jnp.exp2(u * u * EXP2_SCALE))

    def grad(self, e):
        p = e * self.slope
        pn = p * self.n
        scale = 1.0 / p.shape[-1]
        pg = p * self.g
        a = jnp.sum(pg, axis=-1, keepdims=True) * scale
        b = jnp.sum(pn * self.g, axis=-1, keepdims=True) * scale
        return self.r * (pg - a - self.n * b), fold(pn), fold(p)


def dot(a, b):
    return jnp.dot(a, b, preferred_element_type=f32)


def dot_nt(a, b):
    return lax.dot_general(a, b, (((1,), (1,)), ((), ())), preferred_element_type=f32)


def dot_tn(a, b):
    return lax.dot_general(a, b, (((0,), (0,)), ((), ())), preferred_element_type=f32)


def fill(pad, low, rows_ref, high):
    rows = rows_ref.shape[0]
    pad[0:REACH, :] = low.astype(f32)
    pad[REACH : REACH + rows, :] = rows_ref[...].astype(f32)
    pad[REACH + rows :, :] = high.astype(f32)


def taps(pad, rows, d, direction):
    pieces = []
    for k in range(KERNEL):
        start = REACH + direction * (k - KERNEL // 2) * d
        pieces.append(pad[start : start + rows, :].astype(bf16))
    return pieces


def row(ref, i):
    return ref[0, i : i + 1, :]


def step_of(seqs, i):
    return pl.program_id(0) * seqs + i


def first_half(
    seqs,
    count,
    x_ref,
    counts_ref,
    outer,
    inner,
    narrow,
    dilated,
    restore,
    hidden_ref,
    second_ref,
    total_ref,
    halo_out,
    outer2,
    inner2,
    narrow2,
    dilated2,
    restore2,
    outer_s,
    inner_s,
    narrow_s,
    outer_p,
    inner_p,
    narrow_p,
    restore_s,
    dilated_s,
    param_sems,
    edges,
    zeros,
    halo_sems,
    zero_sems,
    *sum_room,
):
    place = Place()
    halo = Halo(place, count, edges, zeros, halo_out, halo_sems, zero_sems)
    small = SmallSum(place, *sum_room)
    step = pl.program_id(0)
    params = ((outer, outer2), (inner, inner2), (narrow, narrow2), (restore, restore2), (dilated, dilated2))
    shadows = (outer_s, inner_s, narrow_s)

    through = (outer_p, inner_p, narrow_p, restore_s, dilated_s)

    def local(k, passing):
        dst = params[k][1].at[pl.ds(place.core, 1)]
        return pltpu.make_async_copy(passing, dst, param_sems.at[0, k])

    def away(k):
        src, dst = params[k]
        return remote(
            src,
            dst.at[pl.ds(place.core, 1)],
            param_sems.at[1, k],
            param_sems.at[2, k],
            place.other_core(),
        )

    @pl.when(step == 0)
    def _():
        place.greet(place.line() + place.partners())
        for k in range(len(params)):
            away(k).start()
        for k, shadow in enumerate(shadows):
            load = param_sems.at[3, k]

            @pl.when(place.core == 0)
            def _():
                pltpu.make_async_copy(params[k][0], shadow, load).start()

        for k, shadow in enumerate(shadows):
            load = param_sems.at[3, k]

            @pl.when(place.core == 1)
            def _():
                away(k).wait_recv()
                pltpu.make_async_copy(params[k][1].at[0:1], shadow, load).start()

        for k in range(len(params)):
            pltpu.make_async_copy(params[k][0], through[k], param_sems.at[0, k]).start()
        for k, shadow in enumerate(shadows):
            pltpu.make_async_copy(params[k][0], shadow, param_sems.at[3, k]).wait()
        small.total[1] = counts_ref[...]
        halo.begin()

    @pl.when(step == 2)
    def _():
        for k in range(len(params)):
            pltpu.make_async_copy(params[k][0], through[k], param_sems.at[0, k]).wait()
            local(k, through[k]).start()

    for k in range(1, small.stages):

        @pl.when(step == k - 1)
        def _():
            if k > 1:
                small.end(k - 1)
            small.start(k)

    for i in range(seqs):
        at = step_of(seqs, i)
        act = norm_act(x_ref[i].astype(f32), row(outer_s, 0), row(outer_s, 1))
        hidden = dot(act, narrow_s[0]) + row(inner_s, 0)
        hidden_ref[i] = hidden
        second = norm_act(hidden, row(inner_s, 2), row(inner_s, 3))
        second_ref[i] = second
        halo.send(at, second)

    @pl.when(last_step())
    def _():
        small.end(small.stages - 1)
        total_ref[...] = small.total[small.stages]
        for k in range(len(params)):
            local(k, through[k]).wait()
            away(k).wait_send()

            if k < len(shadows):

                @pl.when(place.core == 0)
                def _():
                    away(k).wait_recv()
            else:
                away(k).wait_recv()

        halo.end()


def middle_half(
    seqs,
    count,
    d,
    x_ref,
    second_ref,
    halo_ref,
    outer_ref,
    inner_ref,
    dilated_ref,
    restore_ref,
    next_outer_ref,
    next_inner_ref,
    next_narrow_ref,
    mixed_ref,
    middle_ref,
    hidden_ref,
    next_second_ref,
    halo_out,
    pads,
    *halo_room,
):
    rows = x_ref.shape[1]
    inner = inner_ref.shape[-1]
    halo = halo_of(count, halo_out, halo_room)
    for i in range(seqs):
        pad = pads.at[i]
        fill(pad, halo_ref[0, i], second_ref.at[i], halo_ref[1, i])
        windows = jnp.concatenate(taps(pad, rows, d, 1), axis=1)
        mixed = dot(windows, dilated_ref[0].reshape(KERNEL * inner, inner)) + row(inner_ref, 1)
        mixed_ref[i] = mixed
        third = norm_act(mixed, row(inner_ref, 4), row(inner_ref, 5))
        y = x_ref[i].astype(f32) + (dot(third, restore_ref[0]) + row(outer_ref, 2))
        middle_ref[i] = y
        act = norm_act(y, row(next_outer_ref, 0), row(next_outer_ref, 1))
        hidden = dot(act, next_narrow_ref[0]) + row(next_inner_ref, 0)
        hidden_ref[i] = hidden
        second = norm_act(hidden, row(next_inner_ref, 2), row(next_inner_ref, 3))
        next_second_ref[i] = second
        halo.send(step_of(seqs, i), second)
    halo.end_last()


def last_step():
    return pl.program_id(0) == pl.num_programs(0) - 1


def write_restore(out, total):
    inner, width = total.shape
    for j in range(width // inner):
        out[j * inner : (j + 1) * inner, :] = total[:, j * inner : (j + 1) * inner].astype(bf16)


def write_joined(out, narrow_sum, dilated_sum):
    cut = narrow_sum.shape[0]
    out[:cut, :] = narrow_sum[...].astype(bf16)
    out[cut:, :] = dilated_sum[...].astype(bf16)


def start_sums(refs):
    @pl.when(pl.program_id(0) == 0)
    def _():
        for ref in refs:
            ref[...] = jnp.zeros_like(ref)


def column(flags):
    return jnp.transpose(jnp.broadcast_to(flags, (128, flags.shape[1])))


def seeded(cot, flags):
    col = column(flags)
    return cot.astype(f32) * jnp.concatenate([col] * (cot.shape[1] // 128), axis=1)


def turn(
    seqs,
    count,
    d,
    middle_ref,
    second_ref,
    halo_ref,
    cot_ref,
    flags_ref,
    outer_ref,
    inner_ref,
    dilated_ref,
    restore_ref,
    gm_ref,
    restore_out,
    wide_sum,
    small_sum,
    halo_out,
    final_out,
    pads,
    restore_sum,
    *rooms,
):
    rows = middle_ref.shape[1]
    inner = inner_ref.shape[-1]
    start_sums((restore_sum, wide_sum, small_sum))
    halo = halo_of(count, halo_out, rooms[:4], ahead=True)
    halves = Halves(halo.place, count, final_out, *rooms[4:])
    for i in range(seqs):
        pad = pads.at[i]
        fill(pad, halo_ref[0, i], second_ref.at[i], halo_ref[1, i])
        windows = jnp.concatenate(taps(pad, rows, d, 1), axis=1)
        mixed = dot(windows, dilated_ref[0].reshape(KERNEL * inner, inner)) + row(inner_ref, 1)
        back = Back(mixed, row(inner_ref, 4), row(inner_ref, 5))
        y = middle_ref[i] + (dot(back.act, restore_ref[0]) + row(outer_ref, 2))
        halves.send(step_of(seqs, i), y.astype(bf16))
        grad_low = seeded(cot_ref[i], flags_ref[i]).astype(bf16)
        gm = block_out_back(back, grad_low, restore_ref, restore_sum, wide_sum, small_sum)
        gm_ref[i] = gm
        halo.send(step_of(seqs, i), gm)

    @pl.when(last_step())
    def _():
        write_restore(restore_out, restore_sum)
        halves.end()

    halo.end_last()


def block_out_back(back, grad_low, restore_ref, restore_sum, wide_sum, small_sum):
    restore_sum[...] += dot_tn(back.act, grad_low)
    wide_sum[...] += fold(grad_low.astype(f32))
    gv, gain, shift = back.grad(dot_nt(grad_low, restore_ref[0]))
    gm = gv.astype(bf16)
    small_sum[0:8] += fold(gm.astype(f32))
    small_sum[8:16] += gain
    small_sum[16:24] += shift
    return gm


def block_in_back(
    i,
    d,
    stream,
    grad_out,
    hidden_ref,
    second_ref,
    halo_ref,
    gm_ref,
    gm_halo_ref,
    outer_ref,
    inner_ref,
    narrow_ref,
    dilated_ref,
    narrow_sum,
    dilated_sum,
    wide_sum,
    small_sum,
    pad,
    gm_pad,
):
    rows = stream.shape[0]
    fill(gm_pad, gm_halo_ref[0, i], gm_ref.at[i], gm_halo_ref[1, i])
    grad_second = None
    for k, piece in enumerate(taps(gm_pad, rows, d, -1)):
        term = dot_nt(piece, dilated_ref[0, k])
        grad_second = term if grad_second is None else grad_second + term
    fill(pad, halo_ref[0, i], second_ref.at[i], halo_ref[1, i])
    windows = jnp.concatenate(taps(pad, rows, d, 1), axis=1)
    dilated_sum[...] += dot_tn(windows, gm_ref[i])
    back = Back(hidden_ref[i], row(inner_ref, 2), row(inner_ref, 3))
    gv, gain, shift = back.grad(grad_second)
    gh = gv.astype(bf16)
    small_sum[0:8] += fold(gh.astype(f32))
    small_sum[8:16] += gain
    small_sum[16:24] += shift
    first = Back(stream, row(outer_ref, 0), row(outer_ref, 1))
    narrow_sum[...] += dot_tn(first.act, gh)
    gx, gain, shift = first.grad(dot_nt(gh, narrow_ref[0]))
    wide_sum[0:8] += gain
    wide_sum[8:16] += shift
    return grad_out + gx


def between(
    seqs,
    count,
    d,
    middle_ref,
    cot_ref,
    flags_ref,
    hidden_ref,
    second_ref,
    halo_ref,
    gm_ref,
    gm_halo_ref,
    outer_ref,
    inner_ref,
    narrow_ref,
    dilated_ref,
    mixed_ref,
    lower_inner_ref,
    lower_restore_ref,
    gx_ref,
    lower_gm_ref,
    joined_out,
    wide_sum,
    small_sum,
    lower_restore_out,
    lower_wide_sum,
    lower_small_sum,
    halo_out,
    pads,
    gm_pads,
    narrow_sum,
    dilated_sum,
    lower_restore_sum,
    *halo_room,
):
    halo = halo_of(count, halo_out, halo_room)
    start_sums(
        (
            narrow_sum,
            dilated_sum,
            wide_sum,
            small_sum,
            lower_restore_sum,
            lower_wide_sum,
            lower_small_sum,
        )
    )
    for i in range(seqs):
        gx = block_in_back(
            i,
            d,
            middle_ref[i],
            seeded(cot_ref[i], flags_ref[i]),
            hidden_ref,
            second_ref,
            halo_ref,
            gm_ref,
            gm_halo_ref,
            outer_ref,
            inner_ref,
            narrow_ref,
            dilated_ref,
            narrow_sum,
            dilated_sum,
            wide_sum,
            small_sum,
            pads.at[i],
            gm_pads.at[i],
        )
        gx_ref[i] = gx
        lower = Back(mixed_ref[i], row(lower_inner_ref, 4), row(lower_inner_ref, 5))
        gm = block_out_back(
            lower,
            gx.astype(bf16),
            lower_restore_ref,
            lower_restore_sum,
            lower_wide_sum,
            lower_small_sum,
        )
        lower_gm_ref[i] = gm
        halo.send(step_of(seqs, i), gm)

    @pl.when(last_step())
    def _():
        write_joined(joined_out, narrow_sum, dilated_sum)
        write_restore(lower_restore_out, lower_restore_sum)

    halo.end_last()


def last_half(
    seqs,
    count,
    d,
    x_ref,
    gx_ref,
    hidden_ref,
    second_ref,
    halo_ref,
    gm_ref,
    gm_halo_ref,
    outer_ref,
    inner_ref,
    narrow_ref,
    dilated_ref,
    joined_out,
    wide_sum,
    small_sum,
    final_out,
    pads,
    gm_pads,
    narrow_sum,
    dilated_sum,
    *room,
):
    place = Place()
    halves = Halves(place, count, final_out, *room)

    @pl.when(pl.program_id(0) == 0)
    def _():
        place.greet([place.other_core()])

    start_sums((narrow_sum, dilated_sum, wide_sum, small_sum))
    for i in range(seqs):
        gx = block_in_back(
            i,
            d,
            x_ref[i].astype(f32),
            gx_ref[i],
            hidden_ref,
            second_ref,
            halo_ref,
            gm_ref,
            gm_halo_ref,
            outer_ref,
            inner_ref,
            narrow_ref,
            dilated_ref,
            narrow_sum,
            dilated_sum,
            wide_sum,
            small_sum,
            pads.at[i],
            gm_pads.at[i],
        )
        halves.send(step_of(seqs, i), gx.astype(bf16))

    @pl.when(last_step())
    def _():
        write_joined(joined_out, narrow_sum, dilated_sum)
        halves.end()


MESH = pl.DeviceIdType.MESH
UNIT = 16


def bits_of(count):
    return count.bit_length() - 1


def mixed_by(core, first, second):
    return first + core * (second - first)


class Place:
    def __init__(self):
        self.core = lax.axis_index("pipe")
        self.seq = lax.axis_index("seq")
        self.dp = lax.axis_index("dp")
        seq_bits = bits_of(lax.axis_size("seq"))
        dp_bits = bits_of(lax.axis_size("dp"))
        order = list(range(seq_bits))
        cut = seq_bits // 2
        turned = order[cut:] + order[:cut]
        self.stages = [("seq", a, b) for a, b in zip(order, turned)]
        self.stages += [("dp", a, a) for a in range(dp_bits)]

    def bit(self, stage):
        axis, a, b = self.stages[stage]
        spot = self.seq if axis == "seq" else self.dp
        return mixed_by(self.core, (spot // (1 << a)) % 2, (spot // (1 << b)) % 2)

    def peer(self, stage):
        axis, a, b = self.stages[stage]
        spot = self.seq if axis == "seq" else self.dp
        hop = mixed_by(self.core, 1 << a, 1 << b) * (1 - 2 * self.bit(stage))
        return {axis: spot + hop}

    def other_core(self):
        return {"pipe": 1 - self.core}

    def partners(self):
        return [self.other_core()] + [self.peer(s) for s in range(len(self.stages))]

    def line(self):
        n = lax.axis_size("seq")
        return [{"seq": (self.seq + 1) % n}, {"seq": (self.seq + n - 1) % n}]

    def greet(self, friends):
        barrier = pltpu.get_barrier_semaphore()
        for friend in friends:
            pl.semaphore_signal(barrier, inc=1, device_id=friend, device_id_type=MESH)
        pl.semaphore_wait(barrier, len(friends))


def remote(src, dst, send_sem, recv_sem, device):
    return pltpu.make_async_remote_copy(
        src_ref=src,
        dst_ref=dst,
        send_sem=send_sem,
        recv_sem=recv_sem,
        device_id=device,
        device_id_type=MESH,
    )


class Halo:
    def __init__(self, place, count, edges, zeros, halo, sems, zero_sems):
        self.place, self.count, self.edges, self.zeros = place, count, edges, zeros
        self.halo, self.sems, self.zero_sems = halo, sems, zero_sems
        self.has_low = place.seq > 0
        self.has_high = place.seq < lax.axis_size("seq") - 1

    @staticmethod
    def scratch(count, width):
        return [
            pltpu.VMEM((2, count, REACH, width), bf16),
            pltpu.VMEM((count, REACH, width), bf16),
            pltpu.SemaphoreType.DMA((4, count)),
            pltpu.SemaphoreType.DMA((2,)),
        ]

    def up(self, i):
        device = {"seq": self.place.seq + 1}
        sems = self.sems
        return remote(self.edges.at[1, i], self.halo.at[0, i], sems.at[0, i], sems.at[1, i], device)

    def down(self, i):
        device = {"seq": self.place.seq - 1}
        sems = self.sems
        return remote(self.edges.at[0, i], self.halo.at[1, i], sems.at[2, i], sems.at[3, i], device)

    def blank(self, side):
        return pltpu.make_async_copy(self.zeros, self.halo.at[side], self.zero_sems.at[side])

    def begin(self):
        self.zeros[...] = jnp.zeros_like(self.zeros)

        @pl.when(jnp.logical_not(self.has_low))
        def _():
            self.blank(0).start()

        @pl.when(jnp.logical_not(self.has_high))
        def _():
            self.blank(1).start()

    def send(self, i, values):
        self.edges[0, i] = values[:REACH]
        self.edges[1, i] = values[values.shape[0] - REACH :]

        @pl.when(self.has_high)
        def _():
            self.up(i).start()

        @pl.when(self.has_low)
        def _():
            self.down(i).start()

    def end(self):
        @pl.when(jnp.logical_not(self.has_low))
        def _():
            self.blank(0).wait()

        @pl.when(jnp.logical_not(self.has_high))
        def _():
            self.blank(1).wait()

        @pl.when(self.has_high)
        def _():
            def body(i, carry):
                self.up(i).wait_send()
                self.down(i).wait_recv()
                return carry

            lax.fori_loop(0, self.count, body, 0)

        @pl.when(self.has_low)
        def _():
            def body(i, carry):
                self.down(i).wait_send()
                self.up(i).wait_recv()
                return carry

            lax.fori_loop(0, self.count, body, 0)

    def end_last(self):
        @pl.when(last_step())
        def _():
            self.end()


def halo_of(count, halo_out, room, ahead=False):
    place = Place()
    halo = Halo(place, count, room[0], room[1], halo_out, room[2], room[3])

    @pl.when(pl.program_id(0) == 0)
    def _():
        place.greet(place.line() + ([place.other_core()] if ahead else []))
        halo.begin()

    return halo


class Halves:
    def __init__(self, place, count, out, own, other, sems, arrivals):
        self.place, self.count, self.out = place, count, out
        self.own, self.other, self.sems, self.arrivals = own, other, sems, arrivals

    @staticmethod
    def scratch(count, rows, half):
        return [
            pltpu.VMEM((2, rows, half), bf16),
            pltpu.VMEM((2, rows, half), bf16),
            pltpu.SemaphoreType.DMA((2, 2)),
            pltpu.SemaphoreType.DMA((count,)),
        ]

    def local(self, i, slot):
        to = self.place.core * self.count + i
        return pltpu.make_async_copy(self.own.at[slot], self.out.at[to], self.sems.at[0, slot])

    def away(self, i, slot):
        to = self.place.core * self.count + i
        return remote(
            self.other.at[slot],
            self.out.at[to],
            self.sems.at[1, slot],
            self.arrivals.at[i],
            self.place.other_core(),
        )

    def release(self, i, slot):
        self.local(i, slot).wait()
        self.away(i, slot).wait_send()

    def send(self, i, values):
        slot = i % 2
        half = values.shape[1] // 2
        left, right = values[:, :half], values[:, half:]

        @pl.when(i >= 2)
        def _():
            self.release(i - 2, slot)

        first = self.place.core == 0
        self.own[slot] = jnp.where(first, left, right)
        self.other[slot] = jnp.where(first, right, left)
        self.local(i, slot).start()
        self.away(i, slot).start()

    def end(self):
        for i in range(max(0, self.count - 2), self.count):
            self.release(i, i % 2)

        def body(i, carry):
            self.away(i, 0).wait_recv()
            return carry

        lax.fori_loop(0, self.count, body, 0)


def group_sizes(inner, width):
    upper = KERNEL * inner // 2
    return [upper - upper // 5 * 2, upper // 5 * 2, width // 2, width // 2]


class BlockSum:
    def __init__(self, place, block, sizes, joined, restore, out, room, sems):
        self.place, self.block, self.sizes = place, block, sizes
        self.joined, self.restore, self.out = joined, restore, out
        self.own, self.theirs, self.acc, self.sbuf, self.rbuf, self.res = room
        self.core_sems, self.load_sems, self.send_sems, self.recv_sems, self.out_sems = sems
        self.levels = len(place.stages)
        self.starts = [sum(sizes[:g]) for g in range(len(sizes))]
        self.half = sum(sizes)

    @staticmethod
    def scratch(sizes, width, levels):
        rows, groups = sum(sizes), len(sizes)
        room = [
            pltpu.VMEM((rows, width), bf16),
            pltpu.VMEM((rows, width), bf16),
            pltpu.VMEM((rows, width), f32),
            pltpu.VMEM((groups, max(BlockSum.sent(n, levels) for n in sizes), width), bf16),
            pltpu.VMEM((groups, max(BlockSum.sent(n, levels) for n in sizes), width), bf16),
            pltpu.VMEM((rows, width), bf16),
        ]
        dma = pltpu.SemaphoreType.DMA
        sems = [
            dma((groups, 2)),
            dma((groups,)),
            dma((groups, 2 * levels)),
            dma((groups, 2 * levels)),
            dma((groups, 3)),
        ]
        return room, sems

    @staticmethod
    def lengths(rows, levels):
        out = [rows]
        for _ in range(levels):
            last = out[-1]
            out.append(last // 2 if last % (2 * UNIT) == 0 else last)
        return out

    @staticmethod
    def sent(rows, levels):
        return sum(BlockSum.lengths(rows, levels)[1:])

    def spots(self, g):
        lengths = self.lengths(self.sizes[g], self.levels)
        start, out = self.starts[g], []
        for s in range(self.levels):
            out.append((start, lengths[s]))
            if lengths[s + 1] < lengths[s]:
                start = start + self.place.bit(s) * lengths[s + 1]
        out.append((start, lengths[-1]))
        return out

    def source(self, g, half):
        n, at = self.sizes[g], self.starts[g] + half * self.half
        top = self.joined.shape[0]
        if at < top:
            return self.joined.at[pl.ds(at, n)]
        return self.restore.at[pl.ds(at - top, n)]

    def core_copy(self, g, half):
        at = pl.ds(self.starts[g], self.sizes[g])
        return remote(
            self.source(g, half),
            self.theirs.at[at],
            self.core_sems.at[g, 0],
            self.core_sems.at[g, 1],
            self.place.other_core(),
        )

    def load(self, g, half):
        at = pl.ds(self.starts[g], self.sizes[g])
        return pltpu.make_async_copy(self.source(g, half), self.own.at[at], self.load_sems.at[g])

    def down(self, g, s):
        lengths = self.lengths(self.sizes[g], self.levels)
        at = pl.ds(sum(lengths[1 : s + 1]), lengths[s + 1])
        return remote(
            self.sbuf.at[g, at],
            self.rbuf.at[g, at],
            self.send_sems.at[g, s],
            self.recv_sems.at[g, s],
            self.place.peer(s),
        )

    def start_down(self, g, s):
        lengths = self.lengths(self.sizes[g], self.levels)
        start, rows = self.spots(g)[s]
        to, n = sum(lengths[1 : s + 1]), lengths[s + 1]
        if n < rows:
            start = start + (1 - self.place.bit(s)) * n
        start = pl.multiple_of(start, UNIT)
        self.sbuf[g, to : to + n, :] = self.acc[pl.ds(start, n), :].astype(bf16)
        self.down(g, s).start()

    def end_down(self, g, s):
        lengths = self.lengths(self.sizes[g], self.levels)
        at, n = sum(lengths[1 : s + 1]), lengths[s + 1]
        start = pl.multiple_of(self.spots(g)[s + 1][0], UNIT)
        self.down(g, s).wait()
        kept = self.acc[pl.ds(start, n), :]
        if n == lengths[s]:
            kept = kept.astype(bf16).astype(f32)
        self.acc[pl.ds(start, n), :] = kept + self.rbuf[g, at : at + n, :].astype(f32)

    def up(self, g, s):
        lengths = self.lengths(self.sizes[g], self.levels)
        if lengths[s] == lengths[s + 1]:
            return None
        start, n = self.spots(g)[s + 1]
        at = pl.ds(pl.multiple_of(start, UNIT), n)
        return remote(
            self.res.at[at],
            self.res.at[at],
            self.send_sems.at[g, self.levels + s],
            self.recv_sems.at[g, self.levels + s],
            self.place.peer(s),
        )

    def target(self, g, half):
        n, at = self.sizes[g], self.starts[g] + half * self.half
        joined, restore = self.out
        top = joined.shape[0]
        if at < top:
            return joined.at[pl.ds(at, n)]
        return restore.at[:, pl.ds(at - top, n)]

    def keep(self, g, half):
        at = pl.ds(self.starts[g], self.sizes[g])
        return pltpu.make_async_copy(self.res.at[at], self.target(g, half), self.out_sems.at[g, 0])

    def give(self, g, half):
        at = pl.ds(self.starts[g], self.sizes[g])
        return remote(
            self.res.at[at],
            self.target(g, half),
            self.out_sems.at[g, 1],
            self.out_sems.at[g, 2],
            self.place.other_core(),
        )

    def steps(self):
        return 2 * self.levels + 3

    def step(self, g, t):
        core, levels = self.place.core, self.levels
        if t == 0:
            for half in (0, 1):

                @pl.when(core == half)
                def _():
                    self.core_copy(g, 1 - half).start()
                    self.load(g, half).start()

        if t == 1:
            for half in (0, 1):

                @pl.when(core == half)
                def _():
                    self.load(g, half).wait()
                    self.core_copy(g, 1 - half).wait()

            at = slice(self.starts[g], self.starts[g] + self.sizes[g])
            self.acc[at, :] = self.own[at, :].astype(f32) + self.theirs[at, :].astype(f32)
        if 2 <= t < 2 + levels:
            self.end_down(g, t - 2)
        if 1 <= t < 1 + levels:
            self.start_down(g, t - 1)
        if t == 1 + levels:
            start, n = self.spots(g)[levels]
            at = pl.ds(pl.multiple_of(start, UNIT), n)
            self.res[at, :] = self.acc[at, :].astype(bf16)
        if 2 + levels <= t < 2 + 2 * levels:
            copy = self.up(g, 2 * levels + 1 - t)
            if copy is not None:
                copy.wait()
        if 1 + levels <= t < 1 + 2 * levels:
            copy = self.up(g, 2 * levels - t)
            if copy is not None:
                copy.start()
        if t == 1 + 2 * levels:
            for half in (0, 1):

                @pl.when(core == half)
                def _():
                    if half == self.block:
                        self.keep(g, half).start()
                    else:
                        self.give(g, half).start()

        if t == 2 + 2 * levels:
            for half in (0, 1):

                @pl.when(core == half)
                def _():
                    if half == self.block:
                        self.keep(g, half).wait()
                        self.give(g, 1 - half).wait_recv()
                    else:
                        self.give(g, half).wait_send()


class SmallSum:
    def __init__(self, place, total, arrived, sems):
        self.place, self.total, self.arrived, self.sems = place, total, arrived, sems
        self.stages = len(place.stages) + 1

    @staticmethod
    def scratch(rows, width, levels):
        return [
            pltpu.VMEM((levels + 2, rows, width), f32),
            pltpu.VMEM((levels + 1, rows, width), f32),
            pltpu.SemaphoreType.DMA((levels + 1, 2)),
        ]

    def copy(self, s):
        device = self.place.other_core() if s == 0 else self.place.peer(s - 1)
        return remote(
            self.total.at[s], self.arrived.at[s], self.sems.at[s, 0], self.sems.at[s, 1], device
        )

    def start(self, s):
        self.copy(s).start()

    def end(self, s):
        self.copy(s).wait()
        self.total[s + 1] = self.total[s] + self.arrived[s]


def gather_small(total, block, bias_ref, upper_ref, wide_ref, small_ref):
    half = total.shape[-1]
    rows = []
    for ref in (wide_ref, bias_ref):
        for k in range(ref.shape[0] // 8):
            for lane in range(0, ref.shape[1], half):
                rows.append((ref, k, lane))
    for ref, k in ((small_ref, 0), (upper_ref, 0), (small_ref, 1), (small_ref, 2), (upper_ref, 1), (upper_ref, 2)):
        rows.append((ref, k, 0))
    for j, (ref, k, lane) in enumerate(rows):
        piece = ref[8 * k : 8 * k + 8, lane : lane + half]
        total[0, 16 * block + j : 16 * block + j + 1, :] = jnp.sum(piece, axis=0, keepdims=True)


def sum_all(
    sizes,
    joined0,
    restore0,
    joined1,
    restore1,
    *refs,
):
    smalls, out, small_out, scratch = refs[:8], refs[8:10], refs[10], refs[11:]
    place = Place()
    place.greet(place.partners())
    levels = len(place.stages)
    sets = [
        BlockSum(place, 1, sizes, joined1, restore1, out, scratch[0:6], scratch[6:11]),
        BlockSum(place, 0, sizes, joined0, restore0, out, scratch[11:17], scratch[17:22]),
    ]
    small = SmallSum(place, *scratch[22:])
    small.total[0] = jnp.zeros_like(small.total[0])
    for block in (0, 1):
        gather_small(small.total, block, *smalls[4 * block : 4 * block + 4])
    work = [(each, g) for each in sets for g in range(len(sizes))]
    for t in range(len(work) + sets[0].steps() - 1):
        if 0 < t <= small.stages:
            small.end(t - 1)
        if t < small.stages:
            small.start(t)
        for i, (each, g) in enumerate(work):
            if 0 <= t - i < each.steps():
                each.step(g, t - i)
    small_out[...] = small.total[small.stages]


class Caller:
    def __init__(self, name, collective, seqs, count):
        self.name, self.collective, self.seqs, self.count = name, collective, seqs, count
        self.in_specs, self.args, self.out_specs, self.outs, self.scratch = [], [], [], [], []

    def seq(self, *arrays):
        for a in arrays:
            self.in_specs.append(pl.BlockSpec((self.seqs, *a.shape[1:]), lambda i: (i, 0, 0)))
            self.args.append(a)
        return self

    def own(self, *arrays):
        steps = self.count // self.seqs
        for a in arrays:
            self.in_specs.append(
                pl.BlockSpec(
                    (self.seqs, *a.shape[1:]),
                    lambda i: (lax.axis_index("pipe") * steps + i, 0, 0),
                )
            )
            self.args.append(a)
        return self

    def halo(self, *arrays):
        for a in arrays:
            self.in_specs.append(
                pl.BlockSpec((2, self.seqs, *a.shape[2:]), lambda i: (0, i, 0, 0))
            )
            self.args.append(a)
        return self

    def whole(self, *arrays):
        for a in arrays:
            zeros = (0,) * a.ndim
            self.in_specs.append(pl.BlockSpec(a.shape, lambda i, zeros=zeros: zeros))
            self.args.append(a)
        return self

    def anywhere(self, *arrays):
        for a in arrays:
            self.in_specs.append(pl.BlockSpec(memory_space=pl.ANY))
            self.args.append(a)
        return self

    def block(self, index, *arrays):
        for a in arrays:
            spot = (index,) + (0,) * (a.ndim - 1)
            self.in_specs.append(
                pl.BlockSpec(
                    (1, *a.shape[1:]), lambda i, spot=spot: spot, pipeline_mode=pl.Buffered(1)
                )
            )
            self.args.append(a)
        return self

    def out_seq(self, *shapes):
        for shape, dtype in shapes:
            self.out_specs.append(pl.BlockSpec((self.seqs, *shape), lambda i: (i, 0, 0)))
            self.outs.append(jax.ShapeDtypeStruct((self.count, *shape), dtype))
        return self

    def out_any(self, *shapes):
        for shape, dtype in shapes:
            self.out_specs.append(pl.BlockSpec(memory_space=pl.ANY))
            self.outs.append(jax.ShapeDtypeStruct(shape, dtype))
        return self

    def out_sum(self, *shapes, dtype=f32):
        for shape in shapes:
            self.out_specs.append(pl.BlockSpec(shape, lambda i: (0, 0)))
            self.outs.append(jax.ShapeDtypeStruct(shape, dtype))
        return self

    def room(self, scratch):
        self.scratch += scratch
        return self

    def sums(self, *shapes):
        return self.room([pltpu.VMEM(shape, f32) for shape in shapes])

    def pads(self, number, rows, width):
        return self.sums(*[(self.seqs, rows + 2 * REACH, width)] * number)

    def __call__(self, kernel):
        return pl.pallas_call(
            kernel,
            grid=(self.count // self.seqs,),
            in_specs=self.in_specs,
            out_specs=self.out_specs,
            scratch_shapes=self.scratch,
            out_shape=self.outs,
            compiler_params=pltpu.CompilerParams(
                vmem_limit_bytes=VMEM_LIMIT, collective_id=self.collective, has_side_effects=True
            ),
            name=self.name,
        )(*self.args)


def shards(
    inputs,
    cotangent,
    mask_flags,
    residue_types,
    predicted,
    outer_params,
    narrow,
    dilated,
    restore,
    inner_params,
):
    core = lax.axis_index("pipe")
    chip_seqs, rows, width = inputs.shape
    inner = narrow.shape[-1]
    count = chip_seqs // 2
    half = width // 2
    levels = bits_of(lax.axis_size("seq")) + bits_of(lax.axis_size("dp"))
    type_ids = jnp.arange(TYPES, dtype=jnp.int32)
    matches = residue_types[:, :, None] == type_ids
    right_flags = mask_flags * (predicted == residue_types).astype(jnp.int32)
    right_counts = jnp.sum(jnp.where(matches, right_flags[:, :, None], 0), axis=(0, 1))
    masked_counts = jnp.sum(jnp.where(matches, mask_flags[:, :, None], 0), axis=(0, 1))
    counts = jnp.stack([right_counts, masked_counts]).astype(f32)
    counts = jnp.pad(counts, ((0, 8 - 2), (0, 128 - TYPES)))

    def caller(name, collective, seqs):
        return Caller(name, collective, seqs, count)

    def twice(a):
        return ((2, *a.shape[1:]), a.dtype)

    seqs = 1
    halo_shape = ((2, count, REACH, inner), bf16)
    halo_room = Halo.scratch(count, inner)
    halves_room = Halves.scratch(count, rows, half)
    hidden0, second0, counts, halo0, outer2, inner2, narrow2, dilated2, restore2 = (
        caller("first_half", 1, seqs)
        .own(inputs)
        .whole(counts)
        .anywhere(outer_params, inner_params, narrow, dilated, restore)
        .out_seq(((rows, inner), f32), ((rows, inner), bf16))
        .out_sum((8, 128))
        .out_any(halo_shape, *map(twice, (outer_params, inner_params, narrow, dilated, restore)))
        .room([pltpu.VMEM(a.shape, a.dtype) for a in (outer_params, inner_params, narrow) * 2])
        .room([pltpu.VMEM(a.shape, a.dtype) for a in (restore, dilated)])
        .room([pltpu.SemaphoreType.DMA((4, 5))])
        .room(halo_room)
        .room(SmallSum.scratch(8, 128, levels))
    )(functools.partial(first_half, seqs, count))
    accuracy = counts[:2, :TYPES].astype(jnp.int32)
    masked_count = jnp.sum(accuracy[1])
    factor = f32(chip_seqs * lax.axis_size("dp") * LENGTH) / masked_count.astype(f32)
    flags = (mask_flags.astype(f32) * factor)[:, None, :]

    mixed0, middle, hidden1, second1, halo1 = (
        caller("middle_half", 2, seqs)
        .own(inputs)
        .seq(second0)
        .halo(halo0)
        .block(0, outer2, inner2, dilated2, restore2)
        .block(1, outer2, inner2, narrow2)
        .out_seq(
            ((rows, inner), f32), ((rows, width), f32), ((rows, inner), f32), ((rows, inner), bf16)
        )
        .out_any(halo_shape)
        .pads(1, rows, inner)
        .room(halo_room)
    )(functools.partial(middle_half, seqs, count, FIRST_DILATION))

    joined_rows = (width + KERNEL * inner, inner)
    restore_rows = (width, inner)
    final_shape = ((chip_seqs, rows, half), bf16)
    gm1, restore_sum1, bias_sum1, upper_sum1, gm_halo1, block_output = (
        caller("turn", 3, seqs)
        .seq(middle, second1)
        .halo(halo1)
        .own(cotangent, flags)
        .block(1, outer2, inner2, dilated2, restore2)
        .out_seq(((rows, inner), bf16))
        .out_sum(restore_rows, dtype=bf16)
        .out_sum((8, width), (24, inner))
        .out_any(halo_shape, final_shape)
        .pads(1, rows, inner)
        .sums((inner, width))
        .room(halo_room + halves_room)
    )(functools.partial(turn, seqs, count, SECOND_DILATION))

    (
        gx1,
        gm0,
        joined1,
        wide_sum1,
        small_sum1,
        restore_sum0,
        bias_sum0,
        upper_sum0,
        gm_halo0,
    ) = (
        caller("between", 4, seqs)
        .seq(middle)
        .own(cotangent, flags)
        .seq(hidden1, second1)
        .halo(halo1)
        .seq(gm1)
        .halo(gm_halo1)
        .block(1, outer2, inner2, narrow2, dilated2)
        .seq(mixed0)
        .block(0, inner2, restore2)
        .out_seq(((rows, width), f32), ((rows, inner), bf16))
        .out_sum(joined_rows, dtype=bf16)
        .out_sum((16, width), (24, inner))
        .out_sum(restore_rows, dtype=bf16)
        .out_sum((8, width), (24, inner))
        .out_any(halo_shape)
        .pads(2, rows, inner)
        .sums((width, inner), (KERNEL * inner, inner), (inner, width))
        .room(halo_room)
    )(functools.partial(between, seqs, count, SECOND_DILATION))

    joined0, wide_sum0, small_sum0, input_grad = (
        caller("last_half", 5, seqs)
        .own(inputs)
        .seq(gx1, hidden0, second0)
        .halo(halo0)
        .seq(gm0)
        .halo(gm_halo0)
        .block(0, outer2, inner2, narrow2, dilated2)
        .out_sum(joined_rows, dtype=bf16)
        .out_sum((16, width), (24, inner))
        .out_any(final_shape)
        .pads(2, rows, inner)
        .sums((width, inner), (KERNEL * inner, inner))
        .room(halves_room)
    )(functools.partial(last_half, seqs, count, FIRST_DILATION))

    sizes = group_sizes(inner, width)
    rooms = []
    for _ in range(2):
        room, sems = BlockSum.scratch(sizes, inner, levels)
        rooms += room + sems
    rooms += SmallSum.scratch(32, inner, levels)
    anywhere, vmem = pl.BlockSpec(memory_space=pl.ANY), pl.BlockSpec(memory_space=pltpu.VMEM)
    joined_total, restore_total, smalls = pl.pallas_call(
        functools.partial(sum_all, sizes),
        out_shape=[
            jax.ShapeDtypeStruct(joined_rows, bf16),
            jax.ShapeDtypeStruct((inner, width), bf16),
            jax.ShapeDtypeStruct((32, inner), f32),
        ],
        in_specs=[anywhere] * 4 + [vmem] * 8,
        out_specs=[anywhere, anywhere, vmem],
        scratch_shapes=rooms,
        compiler_params=pltpu.CompilerParams(
            vmem_limit_bytes=VMEM_LIMIT, collective_id=0, has_side_effects=True
        ),
        name="sum_all",
    )(
        joined0,
        restore_sum0,
        joined1,
        restore_sum1,
        *(bias_sum0, upper_sum0, wide_sum0, small_sum0),
        *(bias_sum1, upper_sum1, wide_sum1, small_sum1),
    )
    smalls = lax.dynamic_slice_in_dim(smalls, core * 16, 16, 0)
    narrow_total = joined_total[:width].astype(f32)
    dilated_total = joined_total[width:].astype(f32)
    restore_total = restore_total.astype(f32)
    outer_total = smalls[: 3 * width // inner].reshape(3, width)
    inner_total = smalls[3 * width // inner :][:6]

    return (
        block_output,
        input_grad,
        outer_total[None],
        narrow_total[None],
        dilated_total.reshape(1, KERNEL, inner, inner),
        restore_total[None],
        inner_total[None],
        accuracy,
    )


def solution(mesh):
    in_specs = (
        P("dp", "seq", None),
        P("dp", "seq", None),
        P("dp", "seq"),
        P("dp", "seq"),
        P("dp", "seq"),
        P("pipe", None, None),
        P("pipe", None, None),
        P("pipe", None, None, None),
        P("pipe", None, None),
        P("pipe", None, None),
    )
    out_specs = (
        P("dp", "seq", "pipe"),
        P("dp", "seq", "pipe"),
        P("pipe", None, None),
        P("pipe", None, None),
        P("pipe", None, None, None),
        P("pipe", None, None),
        P("pipe", None, None),
        P(),
    )
    return jax.shard_map(shards, mesh=mesh, in_specs=in_specs, out_specs=out_specs, check_vma=False)
```

```python
import functools

import jax
import jax.numpy as jnp
from jax import lax
from jax.experimental import pallas as pl
from jax.experimental.pallas import tpu as pltpu
from jax.sharding import PartitionSpec as P

KERNEL = 5
FIRST_DILATION = 2
SECOND_DILATION = 4
TYPES = 30
LENGTH = 1024
REACH = 8
EPSILON = 1e-05
VMEM_LIMIT = 63 << 20

f32 = jnp.float32
bf16 = jnp.bfloat16
KEPT = bf16

ROOT_HALF = 0.7071067811865476
INV_ROOT_2PI = 0.3989422804014327
EXP2_SCALE = -0.5 * 1.4426950408889634


def normalized(v):
    scale = 1.0 / v.shape[-1]
    centered = v - jnp.sum(v, axis=-1, keepdims=True) * scale
    spread = jnp.sum(centered * centered, axis=-1, keepdims=True) * scale
    r = lax.rsqrt(spread + EPSILON)
    return centered * r, r


def upper(u):
    return 0.5 * lax.erf(u * ROOT_HALF) + 0.5


def norm_act(v, g, s):
    n, _ = normalized(v)
    u = n * g + s
    return (u * upper(u)).astype(bf16)


def fold(v):
    rows, width = v.shape
    return jnp.sum(v.reshape(rows // 8, 8, width), axis=0)


class Back:
    def __init__(self, v, g, s):
        self.n, self.r = normalized(v)
        self.g = g
        u = self.n * g + s
        phi = upper(u)
        self.act = (u * phi).astype(bf16)
        self.slope = phi + u * (INV_ROOT_2PI * jnp.exp2(u * u * EXP2_SCALE))

    def grad(self, e):
        p = e * self.slope
        pn = p * self.n
        scale = 1.0 / p.shape[-1]
        pg = p * self.g
        a = jnp.sum(pg, axis=-1, keepdims=True) * scale
        b = jnp.sum(pn * self.g, axis=-1, keepdims=True) * scale
        return self.r * (pg - a - self.n * b), fold(pn), fold(p)


def dot(a, b):
    return jnp.dot(a, b, preferred_element_type=f32)


def dot_nt(a, b):
    return lax.dot_general(a, b, (((1,), (1,)), ((), ())), preferred_element_type=f32)


def dot_tn(a, b):
    return lax.dot_general(a, b, (((0,), (0,)), ((), ())), preferred_element_type=f32)


def fill(pad, low, values, high):
    rows = values.shape[0]
    pad[0:REACH, :] = low.astype(f32)
    pad[REACH : REACH + rows, :] = values.astype(f32)
    pad[REACH + rows :, :] = high.astype(f32)


def taps(pad, rows, d, direction):
    pieces = []
    for k in range(KERNEL):
        start = REACH + direction * (k - KERNEL // 2) * d
        pieces.append(pad[start : start + rows, :].astype(bf16))
    return pieces


def row(ref, i):
    return ref[i : i + 1, :]


def column(flags):
    return jnp.transpose(jnp.broadcast_to(flags, (128, flags.shape[1])))


def seeded(cot, flags):
    col = column(flags)
    return cot.astype(f32) * jnp.concatenate([col] * (cot.shape[1] // 128), axis=1)


MESH = pl.DeviceIdType.MESH
UNIT = 16


def bits_of(count):
    return count.bit_length() - 1


def mixed_by(core, first, second):
    return first + core * (second - first)


class Place:
    def __init__(self):
        self.core = lax.axis_index("pipe")
        self.seq = lax.axis_index("seq")
        self.dp = lax.axis_index("dp")
        seq_bits = bits_of(lax.axis_size("seq"))
        dp_bits = bits_of(lax.axis_size("dp"))
        order = list(range(seq_bits))
        cut = seq_bits // 2
        turned = order[cut:] + order[:cut]
        self.stages = [("seq", a, b) for a, b in zip(order, turned)]
        self.stages += [("dp", a, a) for a in range(dp_bits)]

    def bit(self, stage):
        axis, a, b = self.stages[stage]
        spot = self.seq if axis == "seq" else self.dp
        return mixed_by(self.core, (spot // (1 << a)) % 2, (spot // (1 << b)) % 2)

    def peer(self, stage):
        axis, a, b = self.stages[stage]
        spot = self.seq if axis == "seq" else self.dp
        hop = mixed_by(self.core, 1 << a, 1 << b) * (1 - 2 * self.bit(stage))
        return {axis: spot + hop}

    def other_core(self):
        return {"pipe": 1 - self.core}

    def partners(self):
        return [self.other_core()] + [self.peer(s) for s in range(len(self.stages))]

    def line(self):
        n = lax.axis_size("seq")
        return [{"seq": (self.seq + 1) % n}, {"seq": (self.seq + n - 1) % n}]

    def greet(self, friends):
        barrier = pltpu.get_barrier_semaphore()
        for friend in friends:
            pl.semaphore_signal(barrier, inc=1, device_id=friend, device_id_type=MESH)
        pl.semaphore_wait(barrier, len(friends))


def remote(src, dst, send_sem, recv_sem, device):
    return pltpu.make_async_remote_copy(
        src_ref=src,
        dst_ref=dst,
        send_sem=send_sem,
        recv_sem=recv_sem,
        device_id=device,
        device_id_type=MESH,
    )


class Halo:
    def __init__(self, place, edges, halo, sems):
        self.place, self.edges, self.halo, self.sems = place, edges, halo, sems
        self.has_low = place.seq > 0
        self.has_high = place.seq < lax.axis_size("seq") - 1

    @staticmethod
    def scratch(count, width):
        return [
            pltpu.VMEM((2, count, REACH, width), bf16),
            pltpu.VMEM((2, count, REACH, width), bf16),
            pltpu.SemaphoreType.DMA((4, count)),
        ]

    def up(self, i):
        device = {"seq": self.place.seq + 1}
        sems = self.sems
        return remote(self.edges.at[1, i], self.halo.at[0, i], sems.at[0, i], sems.at[1, i], device)

    def down(self, i):
        device = {"seq": self.place.seq - 1}
        sems = self.sems
        return remote(self.edges.at[0, i], self.halo.at[1, i], sems.at[2, i], sems.at[3, i], device)

    def begin(self):
        @pl.when(jnp.logical_not(self.has_low))
        def _():
            self.halo[0] = jnp.zeros_like(self.halo[0])

        @pl.when(jnp.logical_not(self.has_high))
        def _():
            self.halo[1] = jnp.zeros_like(self.halo[1])

    def send(self, i, values):
        self.edges[0, i] = values[:REACH]
        self.edges[1, i] = values[values.shape[0] - REACH :]

        @pl.when(self.has_high)
        def _():
            self.up(i).start()

        @pl.when(self.has_low)
        def _():
            self.down(i).start()

    def take(self, i):
        @pl.when(self.has_low)
        def _():
            self.down(i).wait_send()
            self.up(i).wait_recv()

        @pl.when(self.has_high)
        def _():
            self.up(i).wait_send()
            self.down(i).wait_recv()

    def around(self, pad, i, values):
        fill(pad, self.halo[0, i], values, self.halo[1, i])


class Halves:
    def __init__(self, place, count, out, own, other, sems, arrivals):
        self.place, self.count, self.out = place, count, out
        self.own, self.other, self.sems, self.arrivals = own, other, sems, arrivals

    @staticmethod
    def scratch(count, rows, half):
        return [
            pltpu.VMEM((2, rows, half), bf16),
            pltpu.VMEM((2, rows, half), bf16),
            pltpu.SemaphoreType.DMA((2, 2)),
            pltpu.SemaphoreType.DMA((count,)),
        ]

    def local(self, i, slot):
        to = self.place.core * self.count + i
        return pltpu.make_async_copy(self.own.at[slot], self.out.at[to], self.sems.at[0, slot])

    def away(self, i, slot):
        to = self.place.core * self.count + i
        return remote(
            self.other.at[slot],
            self.out.at[to],
            self.sems.at[1, slot],
            self.arrivals.at[i],
            self.place.other_core(),
        )

    def release(self, i, slot):
        self.local(i, slot).wait()
        self.away(i, slot).wait_send()

    def send(self, i, values):
        slot = i % 2
        half = values.shape[1] // 2
        left, right = values[:, :half], values[:, half:]

        @pl.when(i >= 2)
        def _():
            self.release(i - 2, slot)

        first = self.place.core == 0
        self.own[slot] = jnp.where(first, left, right)
        self.other[slot] = jnp.where(first, right, left)
        self.local(i, slot).start()
        self.away(i, slot).start()

    def end(self):
        for i in range(max(0, self.count - 2), self.count):
            self.release(i, i % 2)

        def body(i, carry):
            self.away(i, 0).wait_recv()
            return carry

        lax.fori_loop(0, self.count, body, 0)


def group_sizes(inner, width):
    upper = KERNEL * inner // 2
    return [upper - upper // 5 * 2, upper // 5 * 2, width // 2, width // 2]


class BlockSum:
    def __init__(self, place, block, sizes, part, out, room):
        self.place, self.block, self.sizes, self.part, self.out = place, block, sizes, part, out
        self.theirs, self.sbuf, self.rbuf, self.res = room[:4]
        self.core_sems, self.send_sems, self.recv_sems, self.out_sems = room[4:]
        self.levels = len(place.stages)
        self.starts = [sum(sizes[:g]) for g in range(len(sizes))]
        self.half = sum(sizes)
        sent = [sum(self.lengths(n, self.levels)[1:]) for n in sizes]
        self.bases = [sum(sent[:g]) for g in range(len(sizes))]

    @staticmethod
    def lengths(rows, levels):
        out = [rows]
        for _ in range(levels):
            last = out[-1]
            out.append(last // 2 if last % (2 * UNIT) == 0 else last)
        return out

    @staticmethod
    def scratch(sizes, width, levels):
        rows, groups = sum(sizes), len(sizes)
        sent = sum(sum(BlockSum.lengths(n, levels)[1:]) for n in sizes)
        dma = pltpu.SemaphoreType.DMA
        return [
            pltpu.VMEM((rows, width), bf16),
            pltpu.VMEM((sent, width), bf16),
            pltpu.VMEM((sent, width), bf16),
            pltpu.VMEM((rows, width), bf16),
            dma((groups, 2)),
            dma((groups, 2 * levels)),
            dma((groups, 2 * levels)),
            dma((groups, 3)),
        ]

    def spots(self, g):
        lengths = self.lengths(self.sizes[g], self.levels)
        start, out = self.starts[g], []
        for s in range(self.levels):
            out.append((start, lengths[s]))
            if lengths[s + 1] < lengths[s]:
                start = start + self.place.bit(s) * lengths[s + 1]
        out.append((start, lengths[-1]))
        return out

    def base(self, g, s):
        return self.bases[g] + sum(self.lengths(self.sizes[g], self.levels)[1 : s + 1])

    def value(self, g, s, start, n):
        lengths, spots = self.lengths(self.sizes[g], self.levels), self.spots(g)
        terms = [(self.part, self.place.core * self.half + start), (self.theirs, start)]
        for k in range(s):
            at = self.base(g, k) + (start - spots[k + 1][0])
            if lengths[k + 1] == lengths[k]:
                terms = [(self.sbuf, at)]
            terms.append((self.rbuf, at))
        total = None
        for ref, at in terms:
            term = ref[pl.ds(pl.multiple_of(at, UNIT), n), :].astype(f32)
            total = term if total is None else total + term
        return total

    def core_copy(self, g):
        n = self.sizes[g]
        source = pl.multiple_of((1 - self.place.core) * self.half + self.starts[g], UNIT)
        return remote(
            self.part.at[pl.ds(source, n)],
            self.theirs.at[pl.ds(self.starts[g], n)],
            self.core_sems.at[g, 0],
            self.core_sems.at[g, 1],
            self.place.other_core(),
        )

    def down(self, g, s):
        n = self.lengths(self.sizes[g], self.levels)[s + 1]
        at = pl.ds(self.base(g, s), n)
        return remote(
            self.sbuf.at[at],
            self.rbuf.at[at],
            self.send_sems.at[g, s],
            self.recv_sems.at[g, s],
            self.place.peer(s),
        )

    def start_down(self, g, s):
        start, rows = self.spots(g)[s]
        n = self.lengths(self.sizes[g], self.levels)[s + 1]
        if n < rows:
            start = start + (1 - self.place.bit(s)) * n
        base = self.base(g, s)
        self.sbuf[base : base + n, :] = self.value(g, s, start, n).astype(bf16)
        self.down(g, s).start()

    def up(self, g, s):
        lengths = self.lengths(self.sizes[g], self.levels)
        if lengths[s] == lengths[s + 1]:
            return None
        start, n = self.spots(g)[s + 1]
        at = pl.ds(pl.multiple_of(start, UNIT), n)
        return remote(
            self.res.at[at],
            self.res.at[at],
            self.send_sems.at[g, self.levels + s],
            self.recv_sems.at[g, self.levels + s],
            self.place.peer(s),
        )

    def target(self, g, half):
        n, at = self.sizes[g], self.starts[g] + half * self.half
        joined, restore = self.out
        top = joined.shape[0]
        if at < top:
            return joined.at[pl.ds(at, n)]
        return restore.at[:, pl.ds(at - top, n)]

    def keep(self, g, half):
        at = pl.ds(self.starts[g], self.sizes[g])
        return pltpu.make_async_copy(self.res.at[at], self.target(g, half), self.out_sems.at[g, 0])

    def give(self, g, half):
        at = pl.ds(self.starts[g], self.sizes[g])
        return remote(
            self.res.at[at],
            self.target(g, half),
            self.out_sems.at[g, 1],
            self.out_sems.at[g, 2],
            self.place.other_core(),
        )

    def steps(self):
        return 2 * self.levels + 3

    def step(self, g, t):
        core, levels = self.place.core, self.levels
        if t == 0:
            self.core_copy(g).start()
        if t == 1:
            self.core_copy(g).wait()
        if 2 <= t < 2 + levels:
            self.down(g, t - 2).wait()
        if 1 <= t < 1 + levels:
            self.start_down(g, t - 1)
        if t == 1 + levels:
            start, n = self.spots(g)[levels]
            at = pl.ds(pl.multiple_of(start, UNIT), n)
            self.res[at, :] = self.value(g, levels, start, n).astype(bf16)
        if 2 + levels <= t < 2 + 2 * levels:
            copy = self.up(g, 2 * levels + 1 - t)
            if copy is not None:
                copy.wait()
        if 1 + levels <= t < 1 + 2 * levels:
            copy = self.up(g, 2 * levels - t)
            if copy is not None:
                copy.start()
        if t == 1 + 2 * levels:
            for half in (0, 1):

                @pl.when(core == half)
                def _():
                    if half == self.block:
                        self.keep(g, half).start()
                    else:
                        self.give(g, half).start()

        if t == 2 + 2 * levels:
            for half in (0, 1):

                @pl.when(core == half)
                def _():
                    if half == self.block:
                        self.keep(g, half).wait()
                        self.give(g, 1 - half).wait_recv()
                    else:
                        self.give(g, half).wait_send()


class SmallSum:
    def __init__(self, place, total, arrived, sems):
        self.place, self.total, self.arrived, self.sems = place, total, arrived, sems
        self.stages = len(place.stages) + 1

    @staticmethod
    def scratch(rows, width, levels):
        return [
            pltpu.VMEM((levels + 2, rows, width), f32),
            pltpu.VMEM((levels + 1, rows, width), f32),
            pltpu.SemaphoreType.DMA((levels + 1, 2)),
        ]

    def copy(self, s):
        device = self.place.other_core() if s == 0 else self.place.peer(s - 1)
        return remote(
            self.total.at[s], self.arrived.at[s], self.sems.at[s, 0], self.sems.at[s, 1], device
        )

    def start(self, s):
        self.copy(s).start()

    def end(self, s):
        self.copy(s).wait()
        self.total[s + 1] = self.total[s] + self.arrived[s]


def gather_small(total, block, bias_ref, upper_ref, wide_ref, small_ref):
    half = total.shape[-1]
    rows = []
    for ref in (wide_ref, bias_ref):
        for k in range(ref.shape[0] // 8):
            for lane in range(0, ref.shape[1], half):
                rows.append((ref, k, lane))
    for ref, k in ((small_ref, 0), (upper_ref, 0), (small_ref, 1), (small_ref, 2), (upper_ref, 1), (upper_ref, 2)):
        rows.append((ref, k, 0))
    for j, (ref, k, lane) in enumerate(rows):
        piece = ref[8 * k : 8 * k + 8, lane : lane + half]
        total[0, 16 * block + j : 16 * block + j + 1, :] = jnp.sum(piece, axis=0, keepdims=True)


def block_out_back(back, grad_low, restore, restore_sum, bias_sum, upper_sum):
    restore_sum[...] += dot_tn(back.act, grad_low)
    bias_sum[...] += fold(grad_low.astype(f32))
    gv, gain, shift = back.grad(dot_nt(grad_low, restore[...]))
    gm = gv.astype(bf16)
    upper_sum[0:8] += fold(gm.astype(f32))
    upper_sum[8:16] += gain
    upper_sum[16:24] += shift
    return gm


def block_in_back(
    d, stream, grad_out, hidden, gm, outer, inner, narrow, dilated, narrow_sum, dilated_sum, wide_sum, small_sum, pad, gm_pad
):
    rows = stream.shape[0]
    grad_second = None
    for k, piece in enumerate(taps(gm_pad, rows, d, -1)):
        term = dot_nt(piece, dilated[k])
        grad_second = term if grad_second is None else grad_second + term
    windows = jnp.concatenate(taps(pad, rows, d, 1), axis=1)
    dilated_sum[...] += dot_tn(windows, gm)
    back = Back(hidden, row(inner, 2), row(inner, 3))
    gv, gain, shift = back.grad(grad_second)
    gh = gv.astype(bf16)
    small_sum[0:8] += fold(gh.astype(f32))
    small_sum[8:16] += gain
    small_sum[16:24] += shift
    first = Back(stream, row(outer, 0), row(outer, 1))
    narrow_sum[...] += dot_tn(first.act, gh)
    gx, gain, shift = first.grad(dot_nt(gh, narrow[...]))
    wide_sum[0:8] += gain
    wide_sum[8:16] += shift
    return grad_out + gx


def clear(*refs):
    for ref in refs:
        ref[...] = jnp.zeros_like(ref)


class Refs:
    def __init__(self, names, refs):
        for name, ref in zip(names, refs, strict=True):
            setattr(self, name, ref)


def whole(names, count, sizes, residues, *refs):
    r = Refs(names, refs)
    place = Place()
    core = place.core
    rows, width = r.inputs.shape[1:]
    inner = r.narrow.shape[2]
    taps_rows = KERNEL * inner
    small_counts = SmallSum(place, *r.count_room)
    halos = [Halo(place, *room) for room in r.halo_rooms]
    outputs = Halves(place, count, r.block_output, *r.halves_room)
    grads = Halves(place, count, r.input_grad, *r.halves_room[:3], r.grad_arrivals)
    outer, inner_p, narrow, dilated, restore = r.outer_v, r.inner_v, r.narrow_v, r.dilated_v, r.restore_v
    params = ((r.outer, outer), (r.inner, inner_p), (r.narrow, narrow), (r.dilated, dilated), (r.restore, restore))
    sets = [
        BlockSum(place, block, sizes, r.parts[block], (r.joined_total, r.restore_total), r.sum_rooms[block])
        for block in (0, 1)
    ]

    def local(k):
        src, dst = params[k]
        return pltpu.make_async_copy(src, dst.at[pl.ds(core, 1)], r.param_sems.at[0, k])

    def away(k):
        src, dst = params[k]
        to = dst.at[pl.ds(core, 1)]
        return remote(src, to, r.param_sems.at[1, k], r.param_sems.at[2, k], place.other_core())

    def arrive(k, block):
        @pl.when(core == block)
        def _():
            local(k).wait()

        @pl.when(core != block)
        def _():
            away(k).wait_recv()

    def over(body, ins, outs):
        def spec(a, own):
            shape = (1, *a.shape[1:])
            if own:
                return pl.BlockSpec(shape, lambda i: (core * count + i, 0, 0))
            return pl.BlockSpec(shape, lambda i: (i, 0, 0))

        in_specs = [spec(a, a is r.inputs or a is r.cotangent) for a in ins]
        out_specs = [spec(a, False) for a in outs]
        pipe = pltpu.emit_pipeline(
            lambda *blocks: body(pl.program_id(0), *blocks),
            grid=(count,),
            in_specs=in_specs,
            out_specs=out_specs,
        )
        pipe(*ins, *outs)

    def flags_of(i):
        masked = jnp.sum(small_counts.total[small_counts.stages][1:2, :], axis=1, keepdims=True)
        return r.flags[core * count + i] * (residues / masked)

    place.greet(place.line() + place.partners())
    for k in range(len(params)):
        local(k).start()
        away(k).start()
    small_counts.total[1] = r.counts[...]
    for halo in halos:
        halo.begin()
    clear(r.narrow_sum, r.dilated_sum, r.restore_sum)
    clear(*r.wide_sums, *r.bias_sums, *r.upper_sums, *r.small_sums)
    for k in range(3):
        arrive(k, 0)

    def first(i, x, hidden_out, second_out):
        for k in range(1, small_counts.stages):

            @pl.when(i == k)
            def _():
                if k > 1:
                    small_counts.end(k - 1)
                small_counts.start(k)

        act = norm_act(x[0].astype(f32), row(outer.at[0], 0), row(outer.at[0], 1))
        hidden = dot(act, narrow[0]) + row(inner_p.at[0], 0)
        hidden_out[0] = hidden
        second = norm_act(hidden, row(inner_p.at[0], 2), row(inner_p.at[0], 3))
        second_out[0] = second
        halos[0].send(i, second)

    over(first, [r.inputs], [r.hidden0, r.second0])
    small_counts.end(small_counts.stages - 1)
    r.counts_out[...] = small_counts.total[small_counts.stages]
    for k in range(len(params)):
        away(k).wait_send()
        arrive(k, 1)
        if k >= 3:
            arrive(k, 0)

    def second(i, x, second_in, mixed_out, middle_out, hidden_out, second_out):
        halos[0].take(i)
        halos[0].around(r.pads.at[0], i, second_in[0])
        windows = jnp.concatenate(taps(r.pads.at[0], rows, FIRST_DILATION, 1), axis=1)
        mixed = dot(windows, dilated[0].reshape(taps_rows, inner)) + row(inner_p.at[0], 1)
        mixed_out[0] = mixed
        third = norm_act(mixed, row(inner_p.at[0], 4), row(inner_p.at[0], 5))
        y = x[0].astype(f32) + (dot(third, restore[0]) + row(outer.at[0], 2))
        middle_out[0] = y.astype(middle_out.dtype)
        act = norm_act(y, row(outer.at[1], 0), row(outer.at[1], 1))
        hidden = dot(act, narrow[1]) + row(inner_p.at[1], 0)
        hidden_out[0] = hidden
        second = norm_act(hidden, row(inner_p.at[1], 2), row(inner_p.at[1], 3))
        second_out[0] = second
        halos[1].send(i, second)

    over(second, [r.inputs, r.second0], [r.mixed0, r.middle, r.hidden1, r.second1])

    def turn(i, middle, second_in, cot, gm_out):
        halos[1].take(i)
        halos[1].around(r.pads.at[0], i, second_in[0])
        windows = jnp.concatenate(taps(r.pads.at[0], rows, SECOND_DILATION, 1), axis=1)
        mixed = dot(windows, dilated[1].reshape(taps_rows, inner)) + row(inner_p.at[1], 1)
        back = Back(mixed, row(inner_p.at[1], 4), row(inner_p.at[1], 5))
        y = middle[0].astype(f32) + (dot(back.act, restore[1]) + row(outer.at[1], 2))
        outputs.send(i, y.astype(bf16))
        grad_low = seeded(cot[0], flags_of(i)).astype(bf16)
        gm = block_out_back(back, grad_low, restore.at[1], r.restore_sum, r.bias_sums[1], r.upper_sums[1])
        gm_out[0] = gm
        halos[2].send(i, gm)

    over(turn, [r.middle, r.second1, r.cotangent], [r.gm1])
    outputs.end()
    write_restore(r.parts[1], r.restore_sum)
    clear(r.restore_sum)

    def between(i, middle, cot, hidden, second_in, gm, mixed, gx_out, gm_out):
        halos[2].take(i)
        halos[2].around(r.pads.at[1], i, gm[0])
        halos[1].around(r.pads.at[0], i, second_in[0])
        gx = block_in_back(
            SECOND_DILATION,
            middle[0].astype(f32),
            seeded(cot[0], flags_of(i)),
            hidden[0],
            gm[0],
            outer.at[1],
            inner_p.at[1],
            narrow.at[1],
            dilated.at[1],
            r.narrow_sum,
            r.dilated_sum,
            r.wide_sums[1],
            r.small_sums[1],
            r.pads.at[0],
            r.pads.at[1],
        )
        gx_out[0] = gx.astype(gx_out.dtype)
        back = Back(mixed[0], row(inner_p.at[0], 4), row(inner_p.at[0], 5))
        gm = block_out_back(back, gx.astype(bf16), restore.at[0], r.restore_sum, r.bias_sums[0], r.upper_sums[0])
        gm_out[0] = gm
        halos[3].send(i, gm)

    over(between, [r.middle, r.cotangent, r.hidden1, r.second1, r.gm1, r.mixed0], [r.gx1, r.gm0])
    write_joined(r.parts[1], r.narrow_sum, r.dilated_sum)
    write_restore(r.parts[0], r.restore_sum)
    clear(r.narrow_sum, r.dilated_sum)

    groups = range(len(sizes))
    steps = sets[0].steps()
    lag = [g // 2 for g in groups]

    def beside(t):
        for g in groups:
            if 0 <= t - lag[g] < steps:
                sets[1].step(g, t - lag[g])

    ticks = steps + max(lag)

    def last(i, x, gx_in, hidden, second_in, gm):
        for t in range(min(ticks, count)):

            @pl.when(i == t)
            def _():
                beside(t)

        halos[3].take(i)
        halos[3].around(r.pads.at[1], i, gm[0])
        halos[0].around(r.pads.at[0], i, second_in[0])
        gx = block_in_back(
            FIRST_DILATION,
            x[0].astype(f32),
            gx_in[0].astype(f32),
            hidden[0],
            gm[0],
            outer.at[0],
            inner_p.at[0],
            narrow.at[0],
            dilated.at[0],
            r.narrow_sum,
            r.dilated_sum,
            r.wide_sums[0],
            r.small_sums[0],
            r.pads.at[0],
            r.pads.at[1],
        )
        grads.send(i, gx.astype(bf16))

    over(last, [r.inputs, r.gx1, r.hidden0, r.second0, r.gm0], [])
    write_joined(r.parts[0], r.narrow_sum, r.dilated_sum)

    small = SmallSum(place, *r.small_room)
    small.total[0] = jnp.zeros_like(small.total[0])
    for b in (0, 1):
        gather_small(small.total, b, r.bias_sums[b], r.upper_sums[b], r.wide_sums[b], r.small_sums[b])
    for t in range(max(steps + len(sizes) - 1, small.stages + 1, ticks - count)):
        if count + t < ticks:
            beside(count + t)
        for g in groups:
            if 0 <= t - g < steps:
                sets[0].step(g, t - g)
        if 0 < t <= small.stages:
            small.end(t - 1)
        if t < small.stages:
            small.start(t)
    r.small_out[...] = small.total[small.stages]
    grads.end()


def write_restore(part, total):
    inner, wide = total.shape
    top = part.shape[0] - wide
    for j in range(wide // inner):
        at = top + j * inner
        part[at : at + inner, :] = total[:, j * inner : (j + 1) * inner].astype(bf16)


def write_joined(part, narrow_sum, dilated_sum):
    cut, deep = narrow_sum.shape[0], dilated_sum.shape[0]
    part[:cut, :] = narrow_sum[...].astype(bf16)
    part[cut : cut + deep, :] = dilated_sum[...].astype(bf16)


def shards(
    inputs,
    cotangent,
    mask_flags,
    residue_types,
    predicted,
    outer_params,
    narrow,
    dilated,
    restore,
    inner_params,
):
    core = lax.axis_index("pipe")
    chip_seqs, rows, width = inputs.shape
    inner = narrow.shape[-1]
    count = chip_seqs // 2
    half = width // 2
    levels = bits_of(lax.axis_size("seq")) + bits_of(lax.axis_size("dp"))
    type_ids = jnp.arange(TYPES, dtype=jnp.int32)
    matches = residue_types[:, :, None] == type_ids
    right_flags = mask_flags * (predicted == residue_types).astype(jnp.int32)
    right_counts = jnp.sum(jnp.where(matches, right_flags[:, :, None], 0), axis=(0, 1))
    masked_counts = jnp.sum(jnp.where(matches, mask_flags[:, :, None], 0), axis=(0, 1))
    counts = jnp.stack([right_counts, masked_counts]).astype(f32)
    counts = jnp.pad(counts, ((0, 8 - 2), (0, 128 - TYPES)))

    flags = mask_flags.astype(f32)[:, None, :]
    sizes = group_sizes(inner, width)
    residues = float(chip_seqs * lax.axis_size("dp") * LENGTH)
    deep = KERNEL * inner
    any_space, vmem = pl.BlockSpec(memory_space=pl.ANY), pl.BlockSpec(memory_space=pltpu.VMEM)
    args = [
        ("inputs", inputs, any_space),
        ("cotangent", cotangent, any_space),
        ("flags", flags, vmem),
        ("counts", counts, vmem),
        ("outer", outer_params, any_space),
        ("inner", inner_params, any_space),
        ("narrow", narrow, any_space),
        ("dilated", dilated, any_space),
        ("restore", restore, any_space),
    ]
    results = [
        ("block_output", (chip_seqs, rows, half), bf16, any_space),
        ("input_grad", (chip_seqs, rows, half), bf16, any_space),
        ("joined_total", (width + deep, inner), bf16, any_space),
        ("restore_total", (inner, width), bf16, any_space),
        ("small_out", (32, inner), f32, vmem),
        ("counts_out", (8, 128), f32, vmem),
        ("hidden0", (count, rows, inner), f32, any_space),
        ("hidden1", (count, rows, inner), f32, any_space),
        ("mixed0", (count, rows, inner), f32, any_space),
        ("middle", (count, rows, width), f32, any_space),
        ("gx1", (count, rows, width), KEPT, any_space),
        ("second0", (count, rows, inner), bf16, any_space),
        ("second1", (count, rows, inner), bf16, any_space),
        ("gm0", (count, rows, inner), bf16, any_space),
        ("gm1", (count, rows, inner), bf16, any_space),
    ]

    def twice(a):
        return pltpu.VMEM((2, *a.shape[1:]), a.dtype)

    def sums(*shape):
        return pltpu.VMEM(shape, f32)

    scratch = [
        ("outer_v", twice(outer_params)),
        ("inner_v", twice(inner_params)),
        ("narrow_v", twice(narrow)),
        ("dilated_v", twice(dilated)),
        ("restore_v", twice(restore)),
        ("param_sems", pltpu.SemaphoreType.DMA((3, 5))),
        ("count_room", SmallSum.scratch(8, 128, levels)),
        ("small_room", SmallSum.scratch(32, inner, levels)),
        ("halo_rooms", [Halo.scratch(count, inner) for _ in range(4)]),
        ("halves_room", Halves.scratch(count, rows, half)),
        ("grad_arrivals", pltpu.SemaphoreType.DMA((count,))),
        ("pads", sums(2, rows + 2 * REACH, inner)),
        ("narrow_sum", sums(width, inner)),
        ("dilated_sum", sums(deep, inner)),
        ("restore_sum", sums(inner, width)),
        ("wide_sums", [sums(16, width)] * 2),
        ("bias_sums", [sums(8, width)] * 2),
        ("upper_sums", [sums(24, inner)] * 2),
        ("small_sums", [sums(24, inner)] * 2),
        ("parts", [pltpu.VMEM((2 * width + deep, inner), bf16)] * 2),
        ("sum_rooms", [BlockSum.scratch(sizes, inner, levels) for _ in range(2)]),
    ]
    names = [a[0] for a in args] + [a[0] for a in results] + [a[0] for a in scratch]
    outs = pl.pallas_call(
        functools.partial(whole, names, count, sizes, residues),
        out_shape=[jax.ShapeDtypeStruct(shape, dtype) for _, shape, dtype, _ in results],
        in_specs=[a[2] for a in args],
        out_specs=[a[3] for a in results],
        scratch_shapes=[a[1] for a in scratch],
        compiler_params=pltpu.CompilerParams(
            vmem_limit_bytes=VMEM_LIMIT, collective_id=0, has_side_effects=True
        ),
        name="whole",
    )(*[a[1] for a in args])
    block_output, input_grad, joined_total, restore_total, smalls, counts = outs[:6]
    accuracy = counts[:2, :TYPES].astype(jnp.int32)
    smalls = lax.dynamic_slice_in_dim(smalls, core * 16, 16, 0)
    narrow_total = joined_total[:width].astype(f32)
    dilated_total = joined_total[width:].astype(f32)
    restore_total = restore_total.astype(f32)
    outer_total = smalls[: 3 * width // inner].reshape(3, width)
    inner_total = smalls[3 * width // inner :][:6]

    return (
        block_output,
        input_grad,
        outer_total[None],
        narrow_total[None],
        dilated_total.reshape(1, KERNEL, inner, inner),
        restore_total[None],
        inner_total[None],
        accuracy,
    )


def solution(mesh):
    in_specs = (
        P("dp", "seq", None),
        P("dp", "seq", None),
        P("dp", "seq"),
        P("dp", "seq"),
        P("dp", "seq"),
        P("pipe", None, None),
        P("pipe", None, None),
        P("pipe", None, None, None),
        P("pipe", None, None),
        P("pipe", None, None),
    )
    out_specs = (
        P("dp", "seq", "pipe"),
        P("dp", "seq", "pipe"),
        P("pipe", None, None),
        P("pipe", None, None),
        P("pipe", None, None, None),
        P("pipe", None, None),
        P("pipe", None, None),
        P(),
    )
    return jax.shard_map(shards, mesh=mesh, in_specs=in_specs, out_specs=out_specs, check_vma=False)
```

```python
import functools

import jax
import jax.numpy as jnp
from jax import lax
from jax.experimental import pallas as pl
from jax.experimental.pallas import tpu as pltpu
from jax.sharding import PartitionSpec as P

KERNEL = 5
FIRST_DILATION = 2
SECOND_DILATION = 4
TYPES = 30
LENGTH = 1024
REACH = 8
EPSILON = 1e-05
VMEM_LIMIT = 63 << 20

f32 = jnp.float32
bf16 = jnp.bfloat16
KEPT = bf16

ROOT_HALF = 0.7071067811865476
INV_ROOT_2PI = 0.3989422804014327
EXP2_SCALE = -0.5 * 1.4426950408889634


def normalized(v):
    scale = 1.0 / v.shape[-1]
    centered = v - jnp.sum(v, axis=-1, keepdims=True) * scale
    spread = jnp.sum(centered * centered, axis=-1, keepdims=True) * scale
    r = lax.rsqrt(spread + EPSILON)
    return centered * r, r


def upper(u):
    return 0.5 * lax.erf(u * ROOT_HALF) + 0.5


def norm_act(v, g, s):
    n, _ = normalized(v)
    u = n * g + s
    return (u * upper(u)).astype(bf16)


def fold(v):
    rows, width = v.shape
    return jnp.sum(v.reshape(rows // 8, 8, width), axis=0)


class Back:
    def __init__(self, v, g, s):
        self.n, self.r = normalized(v)
        self.g = g
        u = self.n * g + s
        phi = upper(u)
        self.act = (u * phi).astype(bf16)
        self.slope = phi + u * (INV_ROOT_2PI * jnp.exp2(u * u * EXP2_SCALE))

    def grad(self, e):
        p = e * self.slope
        pn = p * self.n
        scale = 1.0 / p.shape[-1]
        pg = p * self.g
        a = jnp.sum(pg, axis=-1, keepdims=True) * scale
        b = jnp.sum(pn * self.g, axis=-1, keepdims=True) * scale
        return self.r * (pg - a - self.n * b), fold(pn), fold(p)


def dot(a, b):
    return jnp.dot(a, b, preferred_element_type=f32)


def dot_nt(a, b):
    return lax.dot_general(a, b, (((1,), (1,)), ((), ())), preferred_element_type=f32)


def dot_tn(a, b):
    return lax.dot_general(a, b, (((0,), (0,)), ((), ())), preferred_element_type=f32)


def fill(pad, low, values, high):
    rows = values.shape[0]
    pad[0:REACH, :] = low.astype(f32)
    pad[REACH : REACH + rows, :] = values.astype(f32)
    pad[REACH + rows :, :] = high.astype(f32)


def taps(pad, rows, d, direction):
    pieces = []
    for k in range(KERNEL):
        start = REACH + direction * (k - KERNEL // 2) * d
        pieces.append(pad[start : start + rows, :].astype(bf16))
    return pieces


def row(ref, i):
    return ref[i : i + 1, :]


def column(flags):
    return jnp.transpose(jnp.broadcast_to(flags, (128, flags.shape[1])))


def seeded(cot, flags):
    col = column(flags)
    return cot.astype(f32) * jnp.concatenate([col] * (cot.shape[1] // 128), axis=1)


MESH = pl.DeviceIdType.MESH
UNIT = 16


def bits_of(count):
    return count.bit_length() - 1


def mixed_by(core, first, second):
    return first + core * (second - first)


class Place:
    def __init__(self):
        self.core = lax.axis_index("pipe")
        self.seq = lax.axis_index("seq")
        self.dp = lax.axis_index("dp")
        seq_bits = bits_of(lax.axis_size("seq"))
        dp_bits = bits_of(lax.axis_size("dp"))
        order = list(range(seq_bits))
        cut = seq_bits // 2
        turned = order[cut:] + order[:cut]
        self.stages = [("seq", a, b) for a, b in zip(order, turned)]
        self.stages += [("dp", a, a) for a in range(dp_bits)]

    def bit(self, stage):
        axis, a, b = self.stages[stage]
        spot = self.seq if axis == "seq" else self.dp
        return mixed_by(self.core, (spot // (1 << a)) % 2, (spot // (1 << b)) % 2)

    def peer(self, stage):
        axis, a, b = self.stages[stage]
        spot = self.seq if axis == "seq" else self.dp
        hop = mixed_by(self.core, 1 << a, 1 << b) * (1 - 2 * self.bit(stage))
        return {axis: spot + hop}

    def other_core(self):
        return {"pipe": 1 - self.core}

    def partners(self):
        return [self.other_core()] + [self.peer(s) for s in range(len(self.stages))]

    def line(self):
        n = lax.axis_size("seq")
        return [{"seq": (self.seq + 1) % n}, {"seq": (self.seq + n - 1) % n}]

    def greet(self, friends):
        barrier = pltpu.get_barrier_semaphore()
        for friend in friends:
            pl.semaphore_signal(barrier, inc=1, device_id=friend, device_id_type=MESH)
        pl.semaphore_wait(barrier, len(friends))


def remote(src, dst, send_sem, recv_sem, device):
    return pltpu.make_async_remote_copy(
        src_ref=src,
        dst_ref=dst,
        send_sem=send_sem,
        recv_sem=recv_sem,
        device_id=device,
        device_id_type=MESH,
    )


class Halo:
    def __init__(self, place, edges, halo, sems):
        self.place, self.edges, self.halo, self.sems = place, edges, halo, sems
        self.has_low = place.seq > 0
        self.has_high = place.seq < lax.axis_size("seq") - 1

    @staticmethod
    def scratch(count, width):
        return [
            pltpu.VMEM((2, count, REACH, width), bf16),
            pltpu.VMEM((2, count, REACH, width), bf16),
            pltpu.SemaphoreType.DMA((4, count)),
        ]

    def up(self, i):
        device = {"seq": self.place.seq + 1}
        sems = self.sems
        return remote(self.edges.at[1, i], self.halo.at[0, i], sems.at[0, i], sems.at[1, i], device)

    def down(self, i):
        device = {"seq": self.place.seq - 1}
        sems = self.sems
        return remote(self.edges.at[0, i], self.halo.at[1, i], sems.at[2, i], sems.at[3, i], device)

    def begin(self):
        @pl.when(jnp.logical_not(self.has_low))
        def _():
            self.halo[0] = jnp.zeros_like(self.halo[0])

        @pl.when(jnp.logical_not(self.has_high))
        def _():
            self.halo[1] = jnp.zeros_like(self.halo[1])

    def send(self, i, values):
        self.edges[0, i] = values[:REACH]
        self.edges[1, i] = values[values.shape[0] - REACH :]

        @pl.when(self.has_high)
        def _():
            self.up(i).start()

        @pl.when(self.has_low)
        def _():
            self.down(i).start()

    def take(self, i):
        @pl.when(self.has_low)
        def _():
            self.down(i).wait_send()
            self.up(i).wait_recv()

        @pl.when(self.has_high)
        def _():
            self.up(i).wait_send()
            self.down(i).wait_recv()

    def around(self, pad, i, values):
        fill(pad, self.halo[0, i], values, self.halo[1, i])


class Halves:
    def __init__(self, place, count, out, own, other, sems, arrivals):
        self.place, self.count, self.out = place, count, out
        self.own, self.other, self.sems, self.arrivals = own, other, sems, arrivals

    @staticmethod
    def scratch(count, rows, half):
        return [
            pltpu.VMEM((2, rows, half), bf16),
            pltpu.VMEM((2, rows, half), bf16),
            pltpu.SemaphoreType.DMA((2, 2)),
            pltpu.SemaphoreType.DMA((count,)),
        ]

    def local(self, i, slot):
        to = self.place.core * self.count + i
        return pltpu.make_async_copy(self.own.at[slot], self.out.at[to], self.sems.at[0, slot])

    def away(self, i, slot):
        to = self.place.core * self.count + i
        return remote(
            self.other.at[slot],
            self.out.at[to],
            self.sems.at[1, slot],
            self.arrivals.at[i],
            self.place.other_core(),
        )

    def release(self, i, slot):
        self.local(i, slot).wait()
        self.away(i, slot).wait_send()

    def send(self, i, values):
        slot = i % 2
        half = values.shape[1] // 2
        left, right = values[:, :half], values[:, half:]

        @pl.when(i >= 2)
        def _():
            self.release(i - 2, slot)

        first = self.place.core == 0
        self.own[slot] = jnp.where(first, left, right)
        self.other[slot] = jnp.where(first, right, left)
        self.local(i, slot).start()
        self.away(i, slot).start()

    def end(self):
        for i in range(max(0, self.count - 2), self.count):
            self.release(i, i % 2)

        def body(i, carry):
            self.away(i, 0).wait_recv()
            return carry

        lax.fori_loop(0, self.count, body, 0)


def groups_of(inner, width):
    joined = width + KERNEL * inner
    half = joined // 2
    out, at = [(width // 2, joined, width // 2)], 0
    while at < half:
        rows = min(width // 2, half - at)
        out.append((rows, at, half))
        at += rows
    return out


class BlockSum:
    def __init__(self, place, block, groups, part, out, room):
        self.place, self.block, self.part, self.out = place, block, part, out
        self.groups, sizes = groups, [g[0] for g in groups]
        self.sizes = sizes
        self.theirs, self.sbuf, self.rbuf, self.res = room[:4]
        self.core_sems, self.send_sems, self.recv_sems, self.out_sems = room[4:]
        self.levels = len(place.stages)
        self.starts = [sum(sizes[:g]) for g in range(len(sizes))]
        sent = [sum(self.lengths(n, self.levels)[1:]) for n in sizes]
        self.bases = [sum(sent[:g]) for g in range(len(sizes))]

    @staticmethod
    def lengths(rows, levels):
        out = [rows]
        for _ in range(levels):
            last = out[-1]
            out.append(last // 2 if last % (2 * UNIT) == 0 else last)
        return out

    @staticmethod
    def scratch(groups, width, levels):
        sizes = [g[0] for g in groups]
        rows, groups = sum(sizes), len(sizes)
        sent = sum(sum(BlockSum.lengths(n, levels)[1:]) for n in sizes)
        dma = pltpu.SemaphoreType.DMA
        return [
            pltpu.VMEM((rows, width), bf16),
            pltpu.VMEM((sent, width), bf16),
            pltpu.VMEM((sent, width), bf16),
            pltpu.VMEM((rows, width), bf16),
            dma((groups, 2)),
            dma((groups, 2 * levels)),
            dma((groups, 2 * levels)),
            dma((groups, 3)),
        ]

    def spots(self, g):
        lengths = self.lengths(self.sizes[g], self.levels)
        start, out = self.starts[g], []
        for s in range(self.levels):
            out.append((start, lengths[s]))
            if lengths[s + 1] < lengths[s]:
                start = start + self.place.bit(s) * lengths[s + 1]
        out.append((start, lengths[-1]))
        return out

    def base(self, g, s):
        return self.bases[g] + sum(self.lengths(self.sizes[g], self.levels)[1 : s + 1])

    def value(self, g, s, start, n):
        lengths, spots = self.lengths(self.sizes[g], self.levels), self.spots(g)
        terms = [
            (self.part, self.row(g, self.place.core) + (start - self.starts[g])),
            (self.theirs, start),
        ]
        for k in range(s):
            at = self.base(g, k) + (start - spots[k + 1][0])
            if lengths[k + 1] == lengths[k]:
                terms = [(self.sbuf, at)]
            terms.append((self.rbuf, at))
        total = None
        for ref, at in terms:
            term = ref[pl.ds(pl.multiple_of(at, UNIT), n), :].astype(f32)
            total = term if total is None else total + term
        return total

    def row(self, g, half):
        _, at, stride = self.groups[g]
        return at + half * stride

    def core_copy(self, g):
        n = self.sizes[g]
        source = pl.multiple_of(self.row(g, 1 - self.place.core), UNIT)
        return remote(
            self.part.at[pl.ds(source, n)],
            self.theirs.at[pl.ds(self.starts[g], n)],
            self.core_sems.at[g, 0],
            self.core_sems.at[g, 1],
            self.place.other_core(),
        )

    def down(self, g, s):
        n = self.lengths(self.sizes[g], self.levels)[s + 1]
        at = pl.ds(self.base(g, s), n)
        return remote(
            self.sbuf.at[at],
            self.rbuf.at[at],
            self.send_sems.at[g, s],
            self.recv_sems.at[g, s],
            self.place.peer(s),
        )

    def start_down(self, g, s):
        start, rows = self.spots(g)[s]
        n = self.lengths(self.sizes[g], self.levels)[s + 1]
        if n < rows:
            start = start + (1 - self.place.bit(s)) * n
        base = self.base(g, s)
        self.sbuf[base : base + n, :] = self.value(g, s, start, n).astype(bf16)
        self.down(g, s).start()

    def up(self, g, s):
        lengths = self.lengths(self.sizes[g], self.levels)
        if lengths[s] == lengths[s + 1]:
            return None
        start, n = self.spots(g)[s + 1]
        at = pl.ds(pl.multiple_of(start, UNIT), n)
        return remote(
            self.res.at[at],
            self.res.at[at],
            self.send_sems.at[g, self.levels + s],
            self.recv_sems.at[g, self.levels + s],
            self.place.peer(s),
        )

    def target(self, g, half):
        n, at = self.sizes[g], self.row(g, half)
        narrow, dilated, restore = self.out
        for ref in (narrow, dilated):
            if at < ref.shape[0]:
                return ref.at[pl.ds(at, n)]
            at -= ref.shape[0]
        return restore.at[:, pl.ds(at, n)]

    def keep(self, g, half):
        at = pl.ds(self.starts[g], self.sizes[g])
        return pltpu.make_async_copy(self.res.at[at], self.target(g, half), self.out_sems.at[g, 0])

    def give(self, g, half):
        at = pl.ds(self.starts[g], self.sizes[g])
        return remote(
            self.res.at[at],
            self.target(g, half),
            self.out_sems.at[g, 1],
            self.out_sems.at[g, 2],
            self.place.other_core(),
        )

    def steps(self):
        return 2 * self.levels + 3

    def step(self, g, t):
        core, levels = self.place.core, self.levels
        if t == 0:
            self.core_copy(g).start()
        if t == 1:
            self.core_copy(g).wait()
        if 2 <= t < 2 + levels:
            self.down(g, t - 2).wait()
        if 1 <= t < 1 + levels:
            self.start_down(g, t - 1)
        if t == 1 + levels:
            start, n = self.spots(g)[levels]
            at = pl.ds(pl.multiple_of(start, UNIT), n)
            self.res[at, :] = self.value(g, levels, start, n).astype(bf16)
        if 2 + levels <= t < 2 + 2 * levels:
            copy = self.up(g, 2 * levels + 1 - t)
            if copy is not None:
                copy.wait()
        if 1 + levels <= t < 1 + 2 * levels:
            copy = self.up(g, 2 * levels - t)
            if copy is not None:
                copy.start()
        if t == 1 + 2 * levels:
            for half in (0, 1):

                @pl.when(core == half)
                def _():
                    if half == self.block:
                        self.keep(g, half).start()
                    else:
                        self.give(g, half).start()

        if t == 2 + 2 * levels:
            for half in (0, 1):

                @pl.when(core == half)
                def _():
                    if half == self.block:
                        self.keep(g, half).wait()
                        self.give(g, 1 - half).wait_recv()
                    else:
                        self.give(g, half).wait_send()


STEP_TIMES = (5.0, 2.3, 2.9, 0.7)
LATENCY = 2.5
CHIP_RATE = 1.0e5
CORE_RATE = 5.0e5


def plan(place, groups, width, begins, count):
    levels = len(place.stages)
    times, now = [], 0.0
    for k in range(3 * count + 400):
        times.append(now)
        now += STEP_TIMES[min(k // count, 3)]

    def sent(g, t):
        rows = groups[g][0]
        lengths = BlockSum.lengths(rows, levels)
        size = 2 * width
        if t in (0, 2 * levels + 1):
            return "pipe", rows * size / CORE_RATE
        s = t - 1 if t <= levels else 2 * levels - t
        axis, bit, _ = place.stages[s]
        flows = 1 if axis == "seq" else 2 << bit
        if t > levels and lengths[s] == lengths[s + 1]:
            flows = 0
        return axis, lengths[s + 1] * size * flows / CHIP_RATE

    due, free = {}, {}
    ready = {(block, g): times[at] for block, g, at in begins}
    tick = dict.fromkeys(ready, 0)
    for k, now in enumerate(times):
        for key in [key for key in ready if ready[key] <= now]:
            t = tick[key]
            due.setdefault(k, []).append((*key, t))
            tick[key] += 1
            if t == 2 * levels + 2:
                del ready[key]
                continue
            link, busy = sent(key[1], t)
            free[link] = max(free.get(link, 0.0), now) + busy
            ready[key] = free[link] + LATENCY
    assert not ready
    return due


class SmallSum:
    def __init__(self, place, total, arrived, sems):
        self.place, self.total, self.arrived, self.sems = place, total, arrived, sems
        self.stages = len(place.stages) + 1

    @staticmethod
    def scratch(rows, width, levels):
        return [
            pltpu.VMEM((levels + 2, rows, width), f32),
            pltpu.VMEM((levels + 1, rows, width), f32),
            pltpu.SemaphoreType.DMA((levels + 1, 2)),
        ]

    def copy(self, s):
        device = self.place.other_core() if s == 0 else self.place.peer(s - 1)
        return remote(
            self.total.at[s], self.arrived.at[s], self.sems.at[s, 0], self.sems.at[s, 1], device
        )

    def start(self, s):
        self.copy(s).start()

    def end(self, s):
        self.copy(s).wait()
        self.total[s + 1] = self.total[s] + self.arrived[s]


def gather_small(total, block, bias_ref, upper_ref, wide_ref, small_ref):
    half = total.shape[-1]
    rows = []
    for ref in (wide_ref, bias_ref):
        for k in range(ref.shape[0] // 8):
            for lane in range(0, ref.shape[1], half):
                rows.append((ref, k, lane))
    for ref, k in ((small_ref, 0), (upper_ref, 0), (small_ref, 1), (small_ref, 2), (upper_ref, 1), (upper_ref, 2)):
        rows.append((ref, k, 0))
    for j, (ref, k, lane) in enumerate(rows):
        piece = ref[8 * k : 8 * k + 8, lane : lane + half]
        total[0, 16 * block + j : 16 * block + j + 1, :] = jnp.sum(piece, axis=0, keepdims=True)


def block_out_back(back, grad_low, restore, restore_sum, bias_sum, upper_sum):
    restore_sum[...] += dot_tn(back.act, grad_low)
    bias_sum[...] += fold(grad_low.astype(f32))
    gv, gain, shift = back.grad(dot_nt(grad_low, restore[...]))
    gm = gv.astype(bf16)
    upper_sum[0:8] += fold(gm.astype(f32))
    upper_sum[8:16] += gain
    upper_sum[16:24] += shift
    return gm


def convolution_back(d, hidden, gm, inner, dilated, dilated_sum, small_sum, pad, gm_pad):
    rows = hidden.shape[0]
    grad_second = None
    for k, piece in enumerate(taps(gm_pad, rows, d, -1)):
        term = dot_nt(piece, dilated[k])
        grad_second = term if grad_second is None else grad_second + term
    windows = jnp.concatenate(taps(pad, rows, d, 1), axis=1)
    dilated_sum[...] += dot_tn(windows, gm)
    back = Back(hidden, row(inner, 2), row(inner, 3))
    gv, gain, shift = back.grad(grad_second)
    gh = gv.astype(bf16)
    small_sum[0:8] += fold(gh.astype(f32))
    small_sum[8:16] += gain
    small_sum[16:24] += shift
    return gh


def stream_back(first, gh, narrow, wide_sum):
    gx, gain, shift = first.grad(dot_nt(gh, narrow[...]))
    wide_sum[0:8] += gain
    wide_sum[8:16] += shift
    return gx


def clear(*refs):
    for ref in refs:
        ref[...] = jnp.zeros_like(ref)


class Refs:
    def __init__(self, names, refs):
        for name, ref in zip(names, refs, strict=True):
            setattr(self, name, ref)


def whole(names, count, groups, residues, *refs):
    r = Refs(names, refs)
    place = Place()
    core = place.core
    rows, width = r.inputs.shape[1:]
    inner = r.narrow.shape[2]
    taps_rows = KERNEL * inner
    small_counts = SmallSum(place, *r.count_room)
    halos = [Halo(place, *room) for room in r.halo_rooms]
    outputs = Halves(place, count, r.block_output, *r.halves_room)
    grads = Halves(place, count, r.input_grad, *r.grads_room)
    outer, inner_p, narrow, dilated, restore = r.outer_v, r.inner_v, r.narrow_v, r.dilated_v, r.restore_v
    params = ((r.outer, outer), (r.inner, inner_p), (r.narrow, narrow), (r.dilated, dilated), (r.restore, restore))
    sets = [
        BlockSum(place, block, groups, r.parts[block], (r.narrow_total, r.dilated_total, r.restore_total), r.sum_rooms[block])
        for block in (0, 1)
    ]

    def local(k):
        src, dst = params[k]
        return pltpu.make_async_copy(src, dst.at[pl.ds(core, 1)], r.param_sems.at[0, k])

    def away(k):
        src, dst = params[k]
        to = dst.at[pl.ds(core, 1)]
        return remote(src, to, r.param_sems.at[1, k], r.param_sems.at[2, k], place.other_core())

    def arrive(k, block):
        @pl.when(core == block)
        def _():
            local(k).wait()

        @pl.when(core != block)
        def _():
            away(k).wait_recv()

    def over(body, ins, outs):
        def spec(a, own):
            shape = (1, *a.shape[1:])
            if own:
                return pl.BlockSpec(shape, lambda i: (core * count + i, 0, 0))
            return pl.BlockSpec(shape, lambda i: (i, 0, 0))

        in_specs = [spec(a, a is r.inputs or a is r.cotangent) for a in ins]
        out_specs = [spec(a, False) for a in outs]
        pipe = pltpu.emit_pipeline(
            lambda *blocks: body(pl.program_id(0), *blocks),
            grid=(count,),
            in_specs=in_specs,
            out_specs=out_specs,
        )
        pipe(*ins, *outs)

    def flags_of(i):
        masked = jnp.sum(small_counts.total[small_counts.stages][1:2, :], axis=1, keepdims=True)
        return r.flags[core * count + i] * (residues / masked)

    place.greet(place.line() + place.partners())
    for k in range(len(params)):
        local(k).start()
        away(k).start()
    small_counts.total[1] = r.counts[...]
    for halo in halos:
        halo.begin()
    clear(r.narrow_sum, r.dilated_sum, r.restore_sum)
    clear(*r.wide_sums, *r.bias_sums, *r.upper_sums, *r.small_sums)
    for k in range(3):
        arrive(k, 0)

    def first(i, x, act_out, hidden_out, second_out):
        for k in range(1, small_counts.stages):

            @pl.when(i == k)
            def _():
                if k > 1:
                    small_counts.end(k - 1)
                small_counts.start(k)

        act = norm_act(x[0].astype(f32), row(outer.at[0], 0), row(outer.at[0], 1))
        act_out[0] = act
        hidden = dot(act, narrow[0]) + row(inner_p.at[0], 0)
        hidden_out[0] = hidden
        second = norm_act(hidden, row(inner_p.at[0], 2), row(inner_p.at[0], 3))
        second_out[0] = second
        halos[0].send(i, second)

    over(first, [r.inputs], [r.first0, r.hidden0, r.second0])
    small_counts.end(small_counts.stages - 1)
    r.counts_out[...] = small_counts.total[small_counts.stages]
    for k in range(len(params)):
        away(k).wait_send()
        arrive(k, 1)
        if k >= 3:
            arrive(k, 0)

    def second(i, x, second_in, mixed_out, middle_out, hidden_out, second_out):
        halos[0].take(i)
        halos[0].around(r.pads.at[0], i, second_in[0])
        windows = jnp.concatenate(taps(r.pads.at[0], rows, FIRST_DILATION, 1), axis=1)
        mixed = dot(windows, dilated[0].reshape(taps_rows, inner)) + row(inner_p.at[0], 1)
        mixed_out[0] = mixed
        third = norm_act(mixed, row(inner_p.at[0], 4), row(inner_p.at[0], 5))
        y = x[0].astype(f32) + (dot(third, restore[0]) + row(outer.at[0], 2))
        middle_out[0] = y.astype(middle_out.dtype)
        act = norm_act(y, row(outer.at[1], 0), row(outer.at[1], 1))
        hidden = dot(act, narrow[1]) + row(inner_p.at[1], 0)
        hidden_out[0] = hidden
        second = norm_act(hidden, row(inner_p.at[1], 2), row(inner_p.at[1], 3))
        second_out[0] = second
        halos[1].send(i, second)

    over(second, [r.inputs, r.second0], [r.mixed0, r.middle, r.hidden1, r.second1])

    def turn(i, second_in, cot, third_out, gm_out):
        halos[1].take(i)
        halos[1].around(r.pads.at[0], i, second_in[0])
        windows = jnp.concatenate(taps(r.pads.at[0], rows, SECOND_DILATION, 1), axis=1)
        mixed = dot(windows, dilated[1].reshape(taps_rows, inner)) + row(inner_p.at[1], 1)
        back = Back(mixed, row(inner_p.at[1], 4), row(inner_p.at[1], 5))
        third_out[0] = back.act
        grad_low = seeded(cot[0], flags_of(i)).astype(bf16)
        gm = block_out_back(back, grad_low, restore.at[1], r.restore_sum, r.bias_sums[1], r.upper_sums[1])
        gm_out[0] = gm
        halos[2].send(i, gm)

    over(turn, [r.second1, r.cotangent], [r.third1, r.gm1])
    write_restore(r.parts[1], r.restore_sum)
    clear(r.restore_sum)

    begins = [(1, 0, 0)]
    begins += [(1, g, count) for g in range(1, len(groups))]
    begins += [(0, 0, count + 4)]
    begins += [(0, g, 2 * count) for g in range(1, len(groups))]
    due = plan(place, groups, inner, begins, count)

    def beside(base, i):
        for k in range(count):
            if base + k in due:

                @pl.when(i == k)
                def _():
                    for block, g, t in due[base + k]:
                        sets[block].step(g, t)

    def between(i, middle, cot, hidden, second_in, gm, mixed, gx_out, gm_out):
        beside(0, i)
        halos[2].take(i)
        halos[2].around(r.pads.at[1], i, gm[0])
        halos[1].around(r.pads.at[0], i, second_in[0])
        gh = convolution_back(
            SECOND_DILATION,
            hidden[0],
            gm[0],
            inner_p.at[1],
            dilated.at[1],
            r.dilated_sum,
            r.small_sums[1],
            r.pads.at[0],
            r.pads.at[1],
        )
        first = Back(middle[0].astype(f32), row(outer.at[1], 0), row(outer.at[1], 1))
        r.narrow_sum[...] += dot_tn(first.act, gh)
        gx = seeded(cot[0], flags_of(i)) + stream_back(first, gh, narrow.at[1], r.wide_sums[1])
        gx_out[0] = gx.astype(gx_out.dtype)
        back = Back(mixed[0], row(inner_p.at[0], 4), row(inner_p.at[0], 5))
        gm = block_out_back(back, gx.astype(bf16), restore.at[0], r.restore_sum, r.bias_sums[0], r.upper_sums[0])
        gm_out[0] = gm
        halos[3].send(i, gm)

    over(between, [r.middle, r.cotangent, r.hidden1, r.second1, r.gm1, r.mixed0], [r.gx1, r.gm0])
    write_joined(r.parts[1], r.narrow_sum, r.dilated_sum)
    write_restore(r.parts[0], r.restore_sum)
    clear(r.narrow_sum, r.dilated_sum)

    def inward(i, act, hidden, second_in, gm, gh_out):
        beside(count, i)
        halos[3].take(i)
        halos[3].around(r.pads.at[1], i, gm[0])
        halos[0].around(r.pads.at[0], i, second_in[0])
        gh = convolution_back(
            FIRST_DILATION,
            hidden[0],
            gm[0],
            inner_p.at[0],
            dilated.at[0],
            r.dilated_sum,
            r.small_sums[0],
            r.pads.at[0],
            r.pads.at[1],
        )
        r.narrow_sum[...] += dot_tn(act[0], gh)
        gh_out[0] = gh

    over(inward, [r.first0, r.hidden0, r.second0, r.gm0], [r.gh0])
    write_joined(r.parts[0], r.narrow_sum, r.dilated_sum)

    def last(i, x, gx_in, gh, middle, third):
        beside(2 * count, i)
        y = middle[0].astype(f32) + (dot(third[0], restore[1]) + row(outer.at[1], 2))
        outputs.send(i, y.astype(bf16))
        first = Back(x[0].astype(f32), row(outer.at[0], 0), row(outer.at[0], 1))
        gx = gx_in[0].astype(f32) + stream_back(first, gh[0], narrow.at[0], r.wide_sums[0])
        grads.send(i, gx.astype(bf16))

    over(last, [r.inputs, r.gx1, r.gh0, r.middle, r.third1], [])

    small = SmallSum(place, *r.small_room)
    small.total[0] = jnp.zeros_like(small.total[0])
    for b in (0, 1):
        gather_small(small.total, b, r.bias_sums[b], r.upper_sums[b], r.wide_sums[b], r.small_sums[b])
    after = sorted(at for at in due if at >= 3 * count)
    for t in range(max(len(after), small.stages + 1)):
        if t < len(after):
            for block, g, k in due[after[t]]:
                sets[block].step(g, k)
        if 0 < t <= small.stages:
            small.end(t - 1)
        if t < small.stages:
            small.start(t)
    r.small_out[...] = small.total[small.stages]
    outputs.end()
    grads.end()


def write_restore(part, total):
    inner, wide = total.shape
    top = part.shape[0] - wide
    for j in range(wide // inner):
        at = top + j * inner
        part[at : at + inner, :] = total[:, j * inner : (j + 1) * inner].astype(bf16)


def write_joined(part, narrow_sum, dilated_sum):
    cut, deep = narrow_sum.shape[0], dilated_sum.shape[0]
    part[:cut, :] = narrow_sum[...].astype(bf16)
    part[cut : cut + deep, :] = dilated_sum[...].astype(bf16)


def shards(
    inputs,
    cotangent,
    mask_flags,
    residue_types,
    predicted,
    outer_params,
    narrow,
    dilated,
    restore,
    inner_params,
):
    core = lax.axis_index("pipe")
    chip_seqs, rows, width = inputs.shape
    inner = narrow.shape[-1]
    count = chip_seqs // 2
    half = width // 2
    levels = bits_of(lax.axis_size("seq")) + bits_of(lax.axis_size("dp"))
    type_ids = jnp.arange(TYPES, dtype=jnp.int32)
    matches = residue_types[:, :, None] == type_ids
    right_flags = mask_flags * (predicted == residue_types).astype(jnp.int32)
    right_counts = jnp.sum(jnp.where(matches, right_flags[:, :, None], 0), axis=(0, 1))
    masked_counts = jnp.sum(jnp.where(matches, mask_flags[:, :, None], 0), axis=(0, 1))
    counts = jnp.stack([right_counts, masked_counts]).astype(f32)
    counts = jnp.pad(counts, ((0, 8 - 2), (0, 128 - TYPES)))

    flags = mask_flags.astype(f32)[:, None, :]
    groups = groups_of(inner, width)
    residues = float(chip_seqs * lax.axis_size("dp") * LENGTH)
    deep = KERNEL * inner
    any_space, vmem = pl.BlockSpec(memory_space=pl.ANY), pl.BlockSpec(memory_space=pltpu.VMEM)
    args = [
        ("inputs", inputs, any_space),
        ("cotangent", cotangent, any_space),
        ("flags", flags, vmem),
        ("counts", counts, vmem),
        ("outer", outer_params, any_space),
        ("inner", inner_params, any_space),
        ("narrow", narrow, any_space),
        ("dilated", dilated, any_space),
        ("restore", restore, any_space),
    ]
    results = [
        ("block_output", (chip_seqs, rows, half), bf16, any_space),
        ("input_grad", (chip_seqs, rows, half), bf16, any_space),
        ("narrow_total", (width, inner), bf16, any_space),
        ("dilated_total", (deep, inner), bf16, any_space),
        ("restore_total", (inner, width), bf16, any_space),
        ("small_out", (32, inner), f32, vmem),
        ("counts_out", (8, 128), f32, vmem),
        ("third1", (count, rows, inner), bf16, any_space),
        ("first0", (count, rows, width), bf16, any_space),
        ("gh0", (count, rows, inner), bf16, any_space),
        ("hidden0", (count, rows, inner), f32, any_space),
        ("hidden1", (count, rows, inner), f32, any_space),
        ("mixed0", (count, rows, inner), f32, any_space),
        ("middle", (count, rows, width), f32, any_space),
        ("gx1", (count, rows, width), KEPT, any_space),
        ("second0", (count, rows, inner), bf16, any_space),
        ("second1", (count, rows, inner), bf16, any_space),
        ("gm0", (count, rows, inner), bf16, any_space),
        ("gm1", (count, rows, inner), bf16, any_space),
    ]

    def twice(a):
        return pltpu.VMEM((2, *a.shape[1:]), a.dtype)

    def sums(*shape):
        return pltpu.VMEM(shape, f32)

    scratch = [
        ("outer_v", twice(outer_params)),
        ("inner_v", twice(inner_params)),
        ("narrow_v", twice(narrow)),
        ("dilated_v", twice(dilated)),
        ("restore_v", twice(restore)),
        ("param_sems", pltpu.SemaphoreType.DMA((3, 5))),
        ("count_room", SmallSum.scratch(8, 128, levels)),
        ("small_room", SmallSum.scratch(32, inner, levels)),
        ("halo_rooms", [Halo.scratch(count, inner) for _ in range(4)]),
        ("halves_room", Halves.scratch(count, rows, half)),
        ("grads_room", Halves.scratch(count, rows, half)),
        ("pads", sums(2, rows + 2 * REACH, inner)),
        ("narrow_sum", sums(width, inner)),
        ("dilated_sum", sums(deep, inner)),
        ("restore_sum", sums(inner, width)),
        ("wide_sums", [sums(16, width)] * 2),
        ("bias_sums", [sums(8, width)] * 2),
        ("upper_sums", [sums(24, inner)] * 2),
        ("small_sums", [sums(24, inner)] * 2),
        ("parts", [pltpu.VMEM((2 * width + deep, inner), bf16)] * 2),
        ("sum_rooms", [BlockSum.scratch(groups, inner, levels) for _ in range(2)]),
    ]
    names = [a[0] for a in args] + [a[0] for a in results] + [a[0] for a in scratch]
    outs = pl.pallas_call(
        functools.partial(whole, names, count, groups, residues),
        out_shape=[jax.ShapeDtypeStruct(shape, dtype) for _, shape, dtype, _ in results],
        in_specs=[a[2] for a in args],
        out_specs=[a[3] for a in results],
        scratch_shapes=[a[1] for a in scratch],
        compiler_params=pltpu.CompilerParams(
            vmem_limit_bytes=VMEM_LIMIT, collective_id=0, has_side_effects=True
        ),
        name="whole",
    )(*[a[1] for a in args])
    block_output, input_grad, narrow_total, dilated_total, restore_total, smalls, counts = outs[:7]
    accuracy = counts[:2, :TYPES].astype(jnp.int32)
    smalls = lax.dynamic_slice_in_dim(smalls, core * 16, 16, 0)
    narrow_total = narrow_total.astype(f32)
    dilated_total = dilated_total.astype(f32)
    restore_total = restore_total.astype(f32)
    outer_total = smalls[: 3 * width // inner].reshape(3, width)
    inner_total = smalls[3 * width // inner :][:6]

    return (
        block_output,
        input_grad,
        outer_total[None],
        narrow_total[None],
        dilated_total.reshape(1, KERNEL, inner, inner),
        restore_total[None],
        inner_total[None],
        accuracy,
    )


def solution(mesh):
    in_specs = (
        P("dp", "seq", None),
        P("dp", "seq", None),
        P("dp", "seq"),
        P("dp", "seq"),
        P("dp", "seq"),
        P("pipe", None, None),
        P("pipe", None, None),
        P("pipe", None, None, None),
        P("pipe", None, None),
        P("pipe", None, None),
    )
    out_specs = (
        P("dp", "seq", "pipe"),
        P("dp", "seq", "pipe"),
        P("pipe", None, None),
        P("pipe", None, None),
        P("pipe", None, None, None),
        P("pipe", None, None),
        P("pipe", None, None),
        P(),
    )
    return jax.shard_map(shards, mesh=mesh, in_specs=in_specs, out_specs=out_specs, check_vma=False)
```

```python
import functools

import jax
import jax.numpy as jnp
from jax import lax
from jax.experimental import pallas as pl
from jax.experimental.pallas import tpu as pltpu
from jax.sharding import PartitionSpec as P

KERNEL = 5
FIRST_DILATION = 2
SECOND_DILATION = 4
TYPES = 30
LENGTH = 1024
REACH = 8
EPSILON = 1e-05
VMEM_LIMIT = 63 << 20

f32 = jnp.float32
bf16 = jnp.bfloat16
KEPT = bf16
STEP_SEQS = (2, 2, 2, 1, 2, 2)

ROOT_HALF = 0.7071067811865476
INV_ROOT_2PI = 0.3989422804014327
EXP2_SCALE = -0.5 * 1.4426950408889634


def normalized(v):
    scale = 1.0 / v.shape[-1]
    centered = v - jnp.sum(v, axis=-1, keepdims=True) * scale
    spread = jnp.sum(centered * centered, axis=-1, keepdims=True) * scale
    r = lax.rsqrt(spread + EPSILON)
    return centered * r, r


def upper(u):
    return 0.5 * lax.erf(u * ROOT_HALF) + 0.5


def norm_act(v, g, s):
    n, _ = normalized(v)
    u = n * g + s
    return (u * upper(u)).astype(bf16)


def fold(v):
    rows, width = v.shape
    return jnp.sum(v.reshape(rows // 8, 8, width), axis=0)


class Back:
    def __init__(self, v, g, s):
        self.n, self.r = normalized(v)
        self.g = g
        u = self.n * g + s
        phi = upper(u)
        self.act = (u * phi).astype(bf16)
        self.slope = phi + u * (INV_ROOT_2PI * jnp.exp2(u * u * EXP2_SCALE))

    def grad(self, e):
        p = e * self.slope
        pn = p * self.n
        scale = 1.0 / p.shape[-1]
        pg = p * self.g
        a = jnp.sum(pg, axis=-1, keepdims=True) * scale
        b = jnp.sum(pn * self.g, axis=-1, keepdims=True) * scale
        return self.r * (pg - a - self.n * b), fold(pn), fold(p)


def dot(a, b):
    return jnp.dot(a, b, preferred_element_type=f32)


def dot_nt(a, b):
    return lax.dot_general(a, b, (((1,), (1,)), ((), ())), preferred_element_type=f32)


def dot_tn(a, b):
    return lax.dot_general(a, b, (((0,), (0,)), ((), ())), preferred_element_type=f32)


def fill(pad, low, values, high):
    rows = values.shape[0]
    pad[0:REACH, :] = low.astype(f32)
    pad[REACH : REACH + rows, :] = values.astype(f32)
    pad[REACH + rows :, :] = high.astype(f32)


def taps(pad, rows, d, direction):
    pieces = []
    for k in range(KERNEL):
        start = REACH + direction * (k - KERNEL // 2) * d
        pieces.append(pad[start : start + rows, :].astype(bf16))
    return pieces


def row(ref, i):
    return ref[i : i + 1, :]


def column(flags):
    return jnp.transpose(jnp.broadcast_to(flags, (128, flags.shape[1])))


def seeded(cot, flags):
    col = column(flags)
    return cot.astype(f32) * jnp.concatenate([col] * (cot.shape[1] // 128), axis=1)


MESH = pl.DeviceIdType.MESH
UNIT = 16


def bits_of(count):
    return count.bit_length() - 1


def mixed_by(core, first, second):
    return first + core * (second - first)


class Place:
    def __init__(self):
        self.core = lax.axis_index("pipe")
        self.seq = lax.axis_index("seq")
        self.dp = lax.axis_index("dp")
        seq_bits = bits_of(lax.axis_size("seq"))
        dp_bits = bits_of(lax.axis_size("dp"))
        order = list(range(seq_bits))
        cut = seq_bits // 2
        turned = order[cut:] + order[:cut]
        self.stages = [("seq", a, b) for a, b in zip(order, turned)]
        self.stages += [("dp", a, a) for a in range(dp_bits)]

    def bit(self, stage):
        axis, a, b = self.stages[stage]
        spot = self.seq if axis == "seq" else self.dp
        return mixed_by(self.core, (spot // (1 << a)) % 2, (spot // (1 << b)) % 2)

    def peer(self, stage):
        axis, a, b = self.stages[stage]
        spot = self.seq if axis == "seq" else self.dp
        hop = mixed_by(self.core, 1 << a, 1 << b) * (1 - 2 * self.bit(stage))
        return {axis: spot + hop}

    def other_core(self):
        return {"pipe": 1 - self.core}

    def partners(self):
        return [self.other_core()] + [self.peer(s) for s in range(len(self.stages))]

    def line(self):
        n = lax.axis_size("seq")
        return [{"seq": (self.seq + 1) % n}, {"seq": (self.seq + n - 1) % n}]

    def greet(self, friends):
        barrier = pltpu.get_barrier_semaphore()
        for friend in friends:
            pl.semaphore_signal(barrier, inc=1, device_id=friend, device_id_type=MESH)
        pl.semaphore_wait(barrier, len(friends))


def remote(src, dst, send_sem, recv_sem, device):
    return pltpu.make_async_remote_copy(
        src_ref=src,
        dst_ref=dst,
        send_sem=send_sem,
        recv_sem=recv_sem,
        device_id=device,
        device_id_type=MESH,
    )


class Halo:
    def __init__(self, place, edges, halo, sems):
        self.place, self.edges, self.halo, self.sems = place, edges, halo, sems
        self.has_low = place.seq > 0
        self.has_high = place.seq < lax.axis_size("seq") - 1

    @staticmethod
    def scratch(count, width):
        return [
            pltpu.VMEM((2, count, REACH, width), bf16),
            pltpu.VMEM((2, count, REACH, width), bf16),
            pltpu.SemaphoreType.DMA((4, count)),
        ]

    def up(self, i):
        device = {"seq": self.place.seq + 1}
        sems = self.sems
        return remote(self.edges.at[1, i], self.halo.at[0, i], sems.at[0, i], sems.at[1, i], device)

    def down(self, i):
        device = {"seq": self.place.seq - 1}
        sems = self.sems
        return remote(self.edges.at[0, i], self.halo.at[1, i], sems.at[2, i], sems.at[3, i], device)

    def begin(self):
        @pl.when(jnp.logical_not(self.has_low))
        def _():
            self.halo[0] = jnp.zeros_like(self.halo[0])

        @pl.when(jnp.logical_not(self.has_high))
        def _():
            self.halo[1] = jnp.zeros_like(self.halo[1])

    def send(self, i, values):
        self.edges[0, i] = values[:REACH]
        self.edges[1, i] = values[values.shape[0] - REACH :]

        @pl.when(self.has_high)
        def _():
            self.up(i).start()

        @pl.when(self.has_low)
        def _():
            self.down(i).start()

    def take(self, i):
        @pl.when(self.has_low)
        def _():
            self.down(i).wait_send()
            self.up(i).wait_recv()

        @pl.when(self.has_high)
        def _():
            self.up(i).wait_send()
            self.down(i).wait_recv()

    def around(self, pad, i, values):
        fill(pad, self.halo[0, i], values, self.halo[1, i])


class Halves:
    def __init__(self, place, count, out, own, other, sems, arrivals):
        self.place, self.count, self.out = place, count, out
        self.own, self.other, self.sems, self.arrivals = own, other, sems, arrivals

    @staticmethod
    def scratch(count, rows, half):
        return [
            pltpu.VMEM((2, rows, half), bf16),
            pltpu.VMEM((2, rows, half), bf16),
            pltpu.SemaphoreType.DMA((2, 2)),
            pltpu.SemaphoreType.DMA((count,)),
        ]

    def local(self, i, slot):
        to = self.place.core * self.count + i
        return pltpu.make_async_copy(self.own.at[slot], self.out.at[to], self.sems.at[0, slot])

    def away(self, i, slot):
        to = self.place.core * self.count + i
        return remote(
            self.other.at[slot],
            self.out.at[to],
            self.sems.at[1, slot],
            self.arrivals.at[i],
            self.place.other_core(),
        )

    def release(self, i, slot):
        self.local(i, slot).wait()
        self.away(i, slot).wait_send()

    def send(self, i, values):
        slot = i % 2
        half = values.shape[1] // 2
        left, right = values[:, :half], values[:, half:]

        @pl.when(i >= 2)
        def _():
            self.release(i - 2, slot)

        first = self.place.core == 0
        self.own[slot] = jnp.where(first, left, right)
        self.other[slot] = jnp.where(first, right, left)
        self.local(i, slot).start()
        self.away(i, slot).start()

    def end(self):
        for i in range(max(0, self.count - 2), self.count):
            self.release(i, i % 2)

        def body(i, carry):
            self.away(i, 0).wait_recv()
            return carry

        lax.fori_loop(0, self.count, body, 0)


def groups_of(inner, width):
    joined = width + KERNEL * inner
    half = joined // 2
    out, at = [(width // 2, 0, width // 2)], 0
    while at < half:
        rows = min(width // 2, half - at)
        out.append((rows, at, half))
        at += rows
    return out


class BlockSum:
    def __init__(self, place, block, groups, part, out, room):
        self.place, self.block, self.parts, self.out = place, block, part, out
        self.groups, sizes = groups, [g[0] for g in groups]
        self.sizes = sizes
        self.theirs, self.sbuf, self.rbuf, self.res = room[:4]
        self.core_sems, self.send_sems, self.recv_sems, self.out_sems = room[4:]
        self.levels = len(place.stages)
        self.starts = [sum(sizes[:g]) for g in range(len(sizes))]
        sent = [sum(self.lengths(n, self.levels)[1:]) for n in sizes]
        self.bases = [sum(sent[:g]) for g in range(len(sizes))]

    @staticmethod
    def lengths(rows, levels):
        out = [rows]
        for _ in range(levels):
            last = out[-1]
            out.append(last // 2 if last % (2 * UNIT) == 0 else last)
        return out

    @staticmethod
    def scratch(groups, width, levels):
        sizes = [g[0] for g in groups]
        rows, groups = sum(sizes), len(sizes)
        sent = sum(sum(BlockSum.lengths(n, levels)[1:]) for n in sizes)
        dma = pltpu.SemaphoreType.DMA
        return [
            pltpu.VMEM((rows, width), bf16),
            pltpu.VMEM((sent, width), bf16),
            pltpu.VMEM((sent, width), bf16),
            pltpu.VMEM((rows, width), bf16),
            dma((groups, 2)),
            dma((groups, 2 * levels)),
            dma((groups, 2 * levels)),
            dma((groups, 3)),
        ]

    def spots(self, g):
        lengths = self.lengths(self.sizes[g], self.levels)
        start, out = self.starts[g], []
        for s in range(self.levels):
            out.append((start, lengths[s]))
            if lengths[s + 1] < lengths[s]:
                start = start + self.place.bit(s) * lengths[s + 1]
        out.append((start, lengths[-1]))
        return out

    def base(self, g, s):
        return self.bases[g] + sum(self.lengths(self.sizes[g], self.levels)[1 : s + 1])

    def value(self, g, s, start, n):
        lengths, spots = self.lengths(self.sizes[g], self.levels), self.spots(g)
        terms = [
            (self.part(g), self.row(g, self.place.core) + (start - self.starts[g])),
            (self.theirs, start),
        ]
        for k in range(s):
            at = self.base(g, k) + (start - spots[k + 1][0])
            if lengths[k + 1] == lengths[k]:
                terms = [(self.sbuf, at)]
            terms.append((self.rbuf, at))
        total = None
        for ref, at in terms:
            term = ref[pl.ds(pl.multiple_of(at, UNIT), n), :].astype(f32)
            total = term if total is None else total + term
        return total

    def part(self, g):
        return self.parts[0 if g > 0 else 1]

    def row(self, g, half):
        _, at, stride = self.groups[g]
        return at + half * stride

    def core_copy(self, g):
        n = self.sizes[g]
        source = pl.multiple_of(self.row(g, 1 - self.place.core), UNIT)
        return remote(
            self.part(g).at[pl.ds(source, n)],
            self.theirs.at[pl.ds(self.starts[g], n)],
            self.core_sems.at[g, 0],
            self.core_sems.at[g, 1],
            self.place.other_core(),
        )

    def down(self, g, s):
        n = self.lengths(self.sizes[g], self.levels)[s + 1]
        at = pl.ds(self.base(g, s), n)
        return remote(
            self.sbuf.at[at],
            self.rbuf.at[at],
            self.send_sems.at[g, s],
            self.recv_sems.at[g, s],
            self.place.peer(s),
        )

    def start_down(self, g, s):
        start, rows = self.spots(g)[s]
        n = self.lengths(self.sizes[g], self.levels)[s + 1]
        if n < rows:
            start = start + (1 - self.place.bit(s)) * n
        base = self.base(g, s)
        self.sbuf[base : base + n, :] = self.value(g, s, start, n).astype(bf16)
        self.down(g, s).start()

    def up(self, g, s):
        lengths = self.lengths(self.sizes[g], self.levels)
        if lengths[s] == lengths[s + 1]:
            return None
        start, n = self.spots(g)[s + 1]
        at = pl.ds(pl.multiple_of(start, UNIT), n)
        return remote(
            self.res.at[at],
            self.res.at[at],
            self.send_sems.at[g, self.levels + s],
            self.recv_sems.at[g, self.levels + s],
            self.place.peer(s),
        )

    def target(self, g, half):
        n, at = self.sizes[g], self.row(g, half)
        narrow, dilated, restore = self.out
        if g == 0:
            return restore.at[:, pl.ds(at, n)]
        top = narrow.shape[0]
        return narrow.at[pl.ds(at, n)] if at < top else dilated.at[pl.ds(at - top, n)]

    def keep(self, g, half):
        at = pl.ds(self.starts[g], self.sizes[g])
        return pltpu.make_async_copy(self.res.at[at], self.target(g, half), self.out_sems.at[g, 0])

    def give(self, g, half):
        at = pl.ds(self.starts[g], self.sizes[g])
        return remote(
            self.res.at[at],
            self.target(g, half),
            self.out_sems.at[g, 1],
            self.out_sems.at[g, 2],
            self.place.other_core(),
        )

    def steps(self):
        return 2 * self.levels + 3

    def step(self, g, t):
        core, levels = self.place.core, self.levels
        if t == 0:
            self.core_copy(g).start()
        if t == 1:
            self.core_copy(g).wait()
        if 2 <= t < 2 + levels:
            self.down(g, t - 2).wait()
        if 1 <= t < 1 + levels:
            self.start_down(g, t - 1)
        if t == 1 + levels:
            start, n = self.spots(g)[levels]
            at = pl.ds(pl.multiple_of(start, UNIT), n)
            self.res[at, :] = self.value(g, levels, start, n).astype(bf16)
        if 2 + levels <= t < 2 + 2 * levels:
            copy = self.up(g, 2 * levels + 1 - t)
            if copy is not None:
                copy.wait()
        if 1 + levels <= t < 1 + 2 * levels:
            copy = self.up(g, 2 * levels - t)
            if copy is not None:
                copy.start()
        if t == 1 + 2 * levels:
            for half in (0, 1):

                @pl.when(core == half)
                def _():
                    if half == self.block:
                        self.keep(g, half).start()
                    else:
                        self.give(g, half).start()

        if t == 2 + 2 * levels:
            for half in (0, 1):

                @pl.when(core == half)
                def _():
                    if half == self.block:
                        self.keep(g, half).wait()
                        self.give(g, 1 - half).wait_recv()
                    else:
                        self.give(g, half).wait_send()


SEQ_TIMES = (5.0, 2.1, 2.5)
AFTER_TIME = 0.7
LATENCY = 2.5
CHIP_RATE = 1.0e5
CORE_RATE = 5.0e5


def plan(place, groups, width, begins, spans):
    levels = len(place.stages)
    times, now = [], 0.0
    for steps, length in (*spans, (400, AFTER_TIME)):
        for _ in range(steps):
            times.append(now)
            now += length

    def sent(g, t):
        rows = groups[g][0]
        lengths = BlockSum.lengths(rows, levels)
        size = 2 * width
        if t in (0, 2 * levels + 1):
            return "pipe", rows * size / CORE_RATE
        s = t - 1 if t <= levels else 2 * levels - t
        axis, bit, _ = place.stages[s]
        flows = 1 if axis == "seq" else 2 << bit
        if t > levels and lengths[s] == lengths[s + 1]:
            flows = 0
        return axis, lengths[s + 1] * size * flows / CHIP_RATE

    due, free = {}, {}
    ready = {(block, g): times[at] for block, g, at in begins}
    tick = dict.fromkeys(ready, 0)
    for k, now in enumerate(times):
        for key in [key for key in ready if ready[key] <= now]:
            t = tick[key]
            due.setdefault(k, []).append((*key, t))
            tick[key] += 1
            if t == 2 * levels + 2:
                del ready[key]
                continue
            link, busy = sent(key[1], t)
            free[link] = max(free.get(link, 0.0), now) + busy
            ready[key] = free[link] + LATENCY
    assert not ready
    return due


class SmallSum:
    def __init__(self, place, total, arrived, sems):
        self.place, self.total, self.arrived, self.sems = place, total, arrived, sems
        self.stages = len(place.stages) + 1

    @staticmethod
    def scratch(rows, width, levels):
        return [
            pltpu.VMEM((levels + 2, rows, width), f32),
            pltpu.VMEM((levels + 1, rows, width), f32),
            pltpu.SemaphoreType.DMA((levels + 1, 2)),
        ]

    def copy(self, s):
        device = self.place.other_core() if s == 0 else self.place.peer(s - 1)
        return remote(
            self.total.at[s], self.arrived.at[s], self.sems.at[s, 0], self.sems.at[s, 1], device
        )

    def start(self, s):
        self.copy(s).start()

    def end(self, s):
        self.copy(s).wait()
        self.total[s + 1] = self.total[s] + self.arrived[s]


def gather_small(total, block, bias_ref, upper_ref, wide_ref, small_ref):
    half = total.shape[-1]
    rows = []
    for ref in (wide_ref, bias_ref):
        for k in range(ref.shape[0] // 8):
            for lane in range(0, ref.shape[1], half):
                rows.append((ref, k, lane))
    for ref, k in ((small_ref, 0), (upper_ref, 0), (small_ref, 1), (small_ref, 2), (upper_ref, 1), (upper_ref, 2)):
        rows.append((ref, k, 0))
    for j, (ref, k, lane) in enumerate(rows):
        piece = ref[8 * k : 8 * k + 8, lane : lane + half]
        total[0, 16 * block + j : 16 * block + j + 1, :] = jnp.sum(piece, axis=0, keepdims=True)


def block_out_back(back, grad_low, restore, restore_sum, bias_sum, upper_sum):
    restore_sum[...] += dot_tn(back.act, grad_low)
    bias_sum[...] += fold(grad_low.astype(f32))
    gv, gain, shift = back.grad(dot_nt(grad_low, restore[...]))
    gm = gv.astype(bf16)
    upper_sum[0:8] += fold(gm.astype(f32))
    upper_sum[8:16] += gain
    upper_sum[16:24] += shift
    return gm


def convolution_back(hidden, gm, windows, gm_taps, inner, dilated, dilated_sum, small_sum):
    width = inner.shape[1]
    grad_second = None
    for k, piece in enumerate(gm_taps):
        term = dot_nt(piece, dilated[k * width : (k + 1) * width, :])
        grad_second = term if grad_second is None else grad_second + term
    dilated_sum[...] += dot_tn(windows(), gm())
    back = Back(hidden(), row(inner, 2), row(inner, 3))
    gv, gain, shift = back.grad(grad_second)
    gh = gv.astype(bf16)
    small_sum[0:8] += fold(gh.astype(f32))
    small_sum[8:16] += gain
    small_sum[16:24] += shift
    return gh


def stream_back(first, gh, narrow, wide_sum):
    gx, gain, shift = first.grad(dot_nt(gh, narrow[...]))
    wide_sum[0:8] += gain
    wide_sum[8:16] += shift
    return gx


def clear(*refs):
    for ref in refs:
        ref[...] = jnp.zeros_like(ref)


class Refs:
    def __init__(self, names, refs):
        for name, ref in zip(names, refs, strict=True):
            setattr(self, name, ref)


def whole(names, count, groups, residues, *refs):
    r = Refs(names, refs)
    place = Place()
    core = place.core
    rows, width = r.inputs.shape[1:]
    inner = r.narrow.shape[2]
    small_counts = SmallSum(place, *r.count_room)
    halos = [Halo(place, *room) for room in r.halo_rooms]
    outputs = Halves(place, count, r.block_output, *r.halves_room)
    grads = Halves(place, count, r.input_grad, *r.grads_room)
    outer, inner_p, joined, restore = r.outer_v, r.inner_v, r.joined_v, r.restore_v
    narrow = [joined.at[b, 0:width] for b in (0, 1)]
    dilated = [joined.at[b, width : width + KERNEL * inner] for b in (0, 1)]
    params = (
        (r.outer, lambda at: outer.at[at]),
        (r.inner, lambda at: inner_p.at[at]),
        (r.narrow, lambda at: joined.at[at, 0:width]),
        (r.dilated, lambda at: joined.at[at, width : width + KERNEL * inner]),
        (r.restore, lambda at: restore.at[at]),
    )
    parts = [(joined.at[1], r.restore_parts[0]), (r.joined_part, r.restore_parts[1])]
    totals = (r.narrow_total, r.dilated_total, r.restore_total)
    sets = [BlockSum(place, b, groups, parts[b], totals, r.sum_rooms[b]) for b in (0, 1)]
    seqs = [n if count % n == 0 else 1 for n in STEP_SEQS]
    stage_steps = [count // n for n in seqs]

    def local(k):
        src, dst = params[k]
        return pltpu.make_async_copy(src, dst(pl.ds(core, 1)), r.param_sems.at[0, k])

    def away(k):
        src, dst = params[k]
        to = dst(pl.ds(core, 1))
        return remote(src, to, r.param_sems.at[1, k], r.param_sems.at[2, k], place.other_core())

    def arrive(k, block):
        @pl.when(core == block)
        def _():
            local(k).wait()

        @pl.when(core != block)
        def _():
            away(k).wait_recv()

    def over(stage, body, ins, outs):
        n, steps = seqs[stage], stage_steps[stage]

        def spec(a, own):
            shape = (n, *a.shape[1:])
            if own:
                return pl.BlockSpec(shape, lambda i: (core * steps + i, 0, 0))
            return pl.BlockSpec(shape, lambda i: (i, 0, 0))

        def flat(*blocks):
            def reader(ref):
                return lambda: ref[...].reshape(n * rows, ref.shape[2])

            def writer(ref):
                def write(v):
                    ref[...] = v.astype(ref.dtype).reshape(ref.shape)

                return write

            cut = len(ins)
            body(pl.program_id(0), *map(reader, blocks[:cut]), *map(writer, blocks[cut:]))

        pipe = pltpu.emit_pipeline(
            flat,
            grid=(steps,),
            in_specs=[spec(a, a is r.inputs or a is r.cotangent) for a in ins],
            out_specs=[spec(a, False) for a in outs],
        )
        pipe(*ins, *outs)

    def each(stage, i):
        n = seqs[stage]
        return [(i * n + j, slice(j * rows, (j + 1) * rows)) for j in range(n)]

    def surround(stage, halo, pads, i, values):
        for j, (at, part) in enumerate(each(stage, i)):
            halo.around(pads.at[j], at, values[part])

    def tapped(stage, pads, d, direction):
        found = [taps(pads.at[j], rows, d, direction) for j in range(seqs[stage])]
        return [jnp.concatenate(pieces, axis=0) for pieces in zip(*found)]

    def windows_of(stage, pads, d):
        return jnp.concatenate(tapped(stage, pads, d, 1), axis=1)

    def take(stage, halo, i):
        for at, _ in each(stage, i):
            halo.take(at)

    def send(stage, sender, i, values):
        for at, part in each(stage, i):
            sender.send(at, values[part])

    def seed_of(stage, i, cot):
        return jnp.concatenate([seeded(cot[part], flags_of(at)) for at, part in each(stage, i)], axis=0)

    def flags_of(i):
        masked = jnp.sum(small_counts.total[small_counts.stages][1:2, :], axis=1, keepdims=True)
        return r.flags[core * count + i] * (residues / masked)

    place.greet(place.line() + place.partners())
    for k in range(len(params)):
        local(k).start()
        away(k).start()
    small_counts.total[1] = r.counts[...]
    for halo in halos:
        halo.begin()
    clear(r.narrow_sum, r.dilated_sum, r.restore_sum)
    clear(*r.wide_sums, *r.bias_sums, *r.upper_sums, *r.small_sums)
    for k in range(3):
        arrive(k, 0)

    def count_step(k):
        if k > 1:
            small_counts.end(k - 1)
        small_counts.start(k)

    def first(i, x, act_out, hidden_out, second_out):
        for k in range(1, min(small_counts.stages, stage_steps[0])):

            @pl.when(i == k)
            def _():
                count_step(k)

        act = norm_act(x().astype(f32), row(outer.at[0], 0), row(outer.at[0], 1))
        act_out(act)
        hidden = dot(act, narrow[0][...]) + row(inner_p.at[0], 0)
        hidden_out(hidden)
        second = norm_act(hidden, row(inner_p.at[0], 2), row(inner_p.at[0], 3))
        second_out(second)
        send(0, halos[0], i, second)

    over(0, first, [r.inputs], [r.first0, r.hidden0, r.second0])
    for k in range(stage_steps[0], small_counts.stages):
        count_step(k)
    small_counts.end(small_counts.stages - 1)
    r.counts_out[...] = small_counts.total[small_counts.stages]
    for k in range(len(params)):
        away(k).wait_send()
        arrive(k, 1)
        if k >= 3:
            arrive(k, 0)

    def second(i, x, second_in, mixed_out, middle_out, hidden_out, second_out):
        take(1, halos[0], i)
        surround(1, halos[0], r.pads, i, second_in())
        windows = windows_of(1, r.pads, FIRST_DILATION)
        mixed = dot(windows, dilated[0][...]) + row(inner_p.at[0], 1)
        mixed_out(mixed)
        third = norm_act(mixed, row(inner_p.at[0], 4), row(inner_p.at[0], 5))
        y = x().astype(f32) + (dot(third, restore[0]) + row(outer.at[0], 2))
        middle_out(y)
        act = norm_act(y, row(outer.at[1], 0), row(outer.at[1], 1))
        hidden = dot(act, narrow[1][...]) + row(inner_p.at[1], 0)
        hidden_out(hidden)
        second = norm_act(hidden, row(inner_p.at[1], 2), row(inner_p.at[1], 3))
        second_out(second)
        send(1, halos[1], i, second)

    over(1, second, [r.inputs, r.second0], [r.mixed0, r.middle, r.hidden1, r.second1])

    def turn(i, second_in, cot, third_out, gm_out):
        take(2, halos[1], i)
        surround(2, halos[1], r.pads, i, second_in())
        windows = windows_of(2, r.pads, SECOND_DILATION)
        mixed = dot(windows, dilated[1][...]) + row(inner_p.at[1], 1)
        back = Back(mixed, row(inner_p.at[1], 4), row(inner_p.at[1], 5))
        third_out(back.act)
        grad_low = seed_of(2, i, cot()).astype(bf16)
        gm = block_out_back(back, grad_low, restore.at[1], r.restore_sum, r.bias_sums[1], r.upper_sums[1])
        gm_out(gm)
        send(2, halos[2], i, gm)

    over(2, turn, [r.second1, r.cotangent], [r.third1, r.gm1])
    write_restore(r.restore_parts[1], r.restore_sum)
    clear(r.restore_sum)

    spans = [(steps, n * time) for steps, n, time in zip(stage_steps[3:], seqs[3:], SEQ_TIMES)]
    fifth, sixth = stage_steps[3], stage_steps[3] + stage_steps[4]
    ends = sixth + stage_steps[5]
    begins = [(1, 0, 0)]
    begins += [(1, g, fifth) for g in range(1, len(groups))]
    begins += [(0, 0, fifth + stage_steps[4] // 3)]
    begins += [(0, g, sixth) for g in range(1, len(groups))]
    due = plan(place, groups, inner, begins, spans)

    def beside(base, steps, i):
        for k in range(steps):
            if base + k in due:

                @pl.when(i == k)
                def _():
                    for block, g, t in due[base + k]:
                        sets[block].step(g, t)

    def between(i, middle, cot, hidden, second_in, gm, mixed, gx_out, gm_out):
        beside(0, stage_steps[3], i)
        take(3, halos[2], i)
        surround(3, halos[2], r.gm_pads, i, gm())
        surround(3, halos[1], r.pads, i, second_in())
        gh = convolution_back(
            hidden,
            gm,
            lambda: windows_of(3, r.pads, SECOND_DILATION),
            tapped(3, r.gm_pads, SECOND_DILATION, -1),
            inner_p.at[1],
            dilated[1],
            r.dilated_sum,
            r.small_sums[1],
        )
        first = Back(middle().astype(f32), row(outer.at[1], 0), row(outer.at[1], 1))
        r.narrow_sum[...] += dot_tn(first.act, gh)
        gx = seed_of(3, i, cot()) + stream_back(first, gh, narrow[1], r.wide_sums[1])
        gx_out(gx)
        back = Back(mixed(), row(inner_p.at[0], 4), row(inner_p.at[0], 5))
        gm = block_out_back(back, gx.astype(bf16), restore.at[0], r.restore_sum, r.bias_sums[0], r.upper_sums[0])
        gm_out(gm)
        send(3, halos[3], i, gm)

    over(3, between, [r.middle, r.cotangent, r.hidden1, r.second1, r.gm1, r.mixed0], [r.gx1, r.gm0])
    write_joined(r.joined_part, r.narrow_sum, r.dilated_sum)
    write_restore(r.restore_parts[0], r.restore_sum)
    clear(r.narrow_sum, r.dilated_sum)

    def inward(i, act, hidden, second_in, gm, gh_out):
        beside(fifth, stage_steps[4], i)
        take(4, halos[3], i)
        surround(4, halos[3], r.gm_pads, i, gm())
        surround(4, halos[0], r.pads, i, second_in())
        gh = convolution_back(
            hidden,
            gm,
            lambda: windows_of(4, r.pads, FIRST_DILATION),
            tapped(4, r.gm_pads, FIRST_DILATION, -1),
            inner_p.at[0],
            dilated[0],
            r.dilated_sum,
            r.small_sums[0],
        )
        gh_out(gh)
        r.narrow_sum[...] += dot_tn(act(), gh)

    over(4, inward, [r.first0, r.hidden0, r.second0, r.gm0], [r.gh0])
    write_joined(joined.at[1], r.narrow_sum, r.dilated_sum)

    def last(i, x, gx_in, gh, middle, third):
        beside(sixth, stage_steps[5], i)
        y = middle().astype(f32) + (dot(third(), restore[1]) + row(outer.at[1], 2))
        send(5, outputs, i, y.astype(bf16))
        first = Back(x().astype(f32), row(outer.at[0], 0), row(outer.at[0], 1))
        gx = gx_in().astype(f32) + stream_back(first, gh(), narrow[0], r.wide_sums[0])
        send(5, grads, i, gx.astype(bf16))

    over(5, last, [r.inputs, r.gx1, r.gh0, r.middle, r.third1], [])

    small = SmallSum(place, *r.small_room)
    small.total[0] = jnp.zeros_like(small.total[0])
    for b in (0, 1):
        gather_small(small.total, b, r.bias_sums[b], r.upper_sums[b], r.wide_sums[b], r.small_sums[b])
    after = sorted(at for at in due if at >= ends)
    for t in range(max(len(after), small.stages + 1)):
        if t < len(after):
            for block, g, k in due[after[t]]:
                sets[block].step(g, k)
        if 0 < t <= small.stages:
            small.end(t - 1)
        if t < small.stages:
            small.start(t)
    r.small_out[...] = small.total[small.stages]
    outputs.end()
    grads.end()


def write_restore(part, total):
    inner, wide = total.shape
    for j in range(wide // inner):
        at = j * inner
        part[at : at + inner, :] = total[:, j * inner : (j + 1) * inner].astype(bf16)


def write_joined(part, narrow_sum, dilated_sum):
    cut, deep = narrow_sum.shape[0], dilated_sum.shape[0]
    part[:cut, :] = narrow_sum[...].astype(bf16)
    part[cut : cut + deep, :] = dilated_sum[...].astype(bf16)


def shards(
    inputs,
    cotangent,
    mask_flags,
    residue_types,
    predicted,
    outer_params,
    narrow,
    dilated,
    restore,
    inner_params,
):
    core = lax.axis_index("pipe")
    chip_seqs, rows, width = inputs.shape
    inner = narrow.shape[-1]
    count = chip_seqs // 2
    half = width // 2
    levels = bits_of(lax.axis_size("seq")) + bits_of(lax.axis_size("dp"))
    type_ids = jnp.arange(TYPES, dtype=jnp.int32)
    matches = residue_types[:, :, None] == type_ids
    right_flags = mask_flags * (predicted == residue_types).astype(jnp.int32)
    right_counts = jnp.sum(jnp.where(matches, right_flags[:, :, None], 0), axis=(0, 1))
    masked_counts = jnp.sum(jnp.where(matches, mask_flags[:, :, None], 0), axis=(0, 1))
    counts = jnp.stack([right_counts, masked_counts]).astype(f32)
    counts = jnp.pad(counts, ((0, 8 - 2), (0, 128 - TYPES)))

    flags = mask_flags.astype(f32)[:, None, :]
    groups = groups_of(inner, width)
    residues = float(chip_seqs * lax.axis_size("dp") * LENGTH)
    deep = KERNEL * inner
    any_space, vmem = pl.BlockSpec(memory_space=pl.ANY), pl.BlockSpec(memory_space=pltpu.VMEM)
    args = [
        ("inputs", inputs, any_space),
        ("cotangent", cotangent, any_space),
        ("flags", flags, vmem),
        ("counts", counts, vmem),
        ("outer", outer_params, any_space),
        ("inner", inner_params, any_space),
        ("narrow", narrow, any_space),
        ("dilated", dilated.reshape(1, deep, inner), any_space),
        ("restore", restore, any_space),
    ]
    results = [
        ("block_output", (chip_seqs, rows, half), bf16, any_space),
        ("input_grad", (chip_seqs, rows, half), bf16, any_space),
        ("narrow_total", (width, inner), bf16, any_space),
        ("dilated_total", (deep, inner), bf16, any_space),
        ("restore_total", (inner, width), bf16, any_space),
        ("small_out", (32, inner), f32, vmem),
        ("counts_out", (8, 128), f32, vmem),
        ("third1", (count, rows, inner), bf16, any_space),
        ("first0", (count, rows, width), bf16, any_space),
        ("gh0", (count, rows, inner), bf16, any_space),
        ("hidden0", (count, rows, inner), f32, any_space),
        ("hidden1", (count, rows, inner), f32, any_space),
        ("mixed0", (count, rows, inner), f32, any_space),
        ("middle", (count, rows, width), KEPT, any_space),
        ("gx1", (count, rows, width), KEPT, any_space),
        ("second0", (count, rows, inner), bf16, any_space),
        ("second1", (count, rows, inner), bf16, any_space),
        ("gm0", (count, rows, inner), bf16, any_space),
        ("gm1", (count, rows, inner), bf16, any_space),
    ]

    def twice(a):
        return pltpu.VMEM((2, *a.shape[1:]), a.dtype)

    def sums(*shape):
        return pltpu.VMEM(shape, f32)

    scratch = [
        ("outer_v", twice(outer_params)),
        ("inner_v", twice(inner_params)),
        ("joined_v", pltpu.VMEM((2, width + deep, inner), bf16)),
        ("restore_v", twice(restore)),
        ("param_sems", pltpu.SemaphoreType.DMA((3, 5))),
        ("count_room", SmallSum.scratch(8, 128, levels)),
        ("small_room", SmallSum.scratch(32, inner, levels)),
        ("halo_rooms", [Halo.scratch(count, inner) for _ in range(4)]),
        ("halves_room", Halves.scratch(count, rows, half)),
        ("grads_room", Halves.scratch(count, rows, half)),
        ("pads", sums(max(STEP_SEQS), rows + 2 * REACH, inner)),
        ("gm_pads", sums(max(STEP_SEQS[3:5]), rows + 2 * REACH, inner)),
        ("narrow_sum", sums(width, inner)),
        ("dilated_sum", sums(deep, inner)),
        ("restore_sum", sums(inner, width)),
        ("wide_sums", [sums(16, width)] * 2),
        ("bias_sums", [sums(8, width)] * 2),
        ("upper_sums", [sums(24, inner)] * 2),
        ("small_sums", [sums(24, inner)] * 2),
        ("restore_parts", [pltpu.VMEM((width, inner), bf16)] * 2),
        ("joined_part", pltpu.VMEM((width + deep, inner), bf16)),
        ("sum_rooms", [BlockSum.scratch(groups, inner, levels) for _ in range(2)]),
    ]
    names = [a[0] for a in args] + [a[0] for a in results] + [a[0] for a in scratch]
    outs = pl.pallas_call(
        functools.partial(whole, names, count, groups, residues),
        out_shape=[jax.ShapeDtypeStruct(shape, dtype) for _, shape, dtype, _ in results],
        in_specs=[a[2] for a in args],
        out_specs=[a[3] for a in results],
        scratch_shapes=[a[1] for a in scratch],
        compiler_params=pltpu.CompilerParams(
            vmem_limit_bytes=VMEM_LIMIT, collective_id=0, has_side_effects=True
        ),
        name="whole",
    )(*[a[1] for a in args])
    block_output, input_grad, narrow_total, dilated_total, restore_total, smalls, counts = outs[:7]
    accuracy = counts[:2, :TYPES].astype(jnp.int32)
    smalls = lax.dynamic_slice_in_dim(smalls, core * 16, 16, 0)
    narrow_total = narrow_total.astype(f32)
    dilated_total = dilated_total.astype(f32)
    restore_total = restore_total.astype(f32)
    outer_total = smalls[: 3 * width // inner].reshape(3, width)
    inner_total = smalls[3 * width // inner :][:6]

    return (
        block_output,
        input_grad,
        outer_total[None],
        narrow_total[None],
        dilated_total.reshape(1, KERNEL, inner, inner),
        restore_total[None],
        inner_total[None],
        accuracy,
    )


def solution(mesh):
    in_specs = (
        P("dp", "seq", None),
        P("dp", "seq", None),
        P("dp", "seq"),
        P("dp", "seq"),
        P("dp", "seq"),
        P("pipe", None, None),
        P("pipe", None, None),
        P("pipe", None, None, None),
        P("pipe", None, None),
        P("pipe", None, None),
    )
    out_specs = (
        P("dp", "seq", "pipe"),
        P("dp", "seq", "pipe"),
        P("pipe", None, None),
        P("pipe", None, None),
        P("pipe", None, None, None),
        P("pipe", None, None),
        P("pipe", None, None),
        P(),
    )
    return jax.shard_map(shards, mesh=mesh, in_specs=in_specs, out_specs=out_specs, check_vma=False)
```

```python
import functools

import jax
import jax.numpy as jnp
from jax import lax
from jax.experimental import pallas as pl
from jax.experimental.pallas import tpu as pltpu
from jax.sharding import PartitionSpec as P

KERNEL = 5
FIRST_DILATION = 2
SECOND_DILATION = 4
TYPES = 30
LENGTH = 1024
REACH = 8
EPSILON = 1e-05
VMEM_LIMIT = 63 << 20

f32 = jnp.float32
bf16 = jnp.bfloat16
KEPT = bf16
STEP_SEQS = (2, 2, 2, 1, 2, 2)

ROOT_HALF = 0.7071067811865476
INV_ROOT_2PI = 0.3989422804014327
EXP2_SCALE = -0.5 * 1.4426950408889634


def normalized(v):
    scale = 1.0 / v.shape[-1]
    centered = v - jnp.sum(v, axis=-1, keepdims=True) * scale
    spread = jnp.sum(centered * centered, axis=-1, keepdims=True) * scale
    r = lax.rsqrt(spread + EPSILON)
    return centered * r, r


def upper(u):
    return 0.5 * lax.erf(u * ROOT_HALF) + 0.5


def norm_act(v, g, s):
    n, _ = normalized(v)
    u = n * g + s
    return (u * upper(u)).astype(bf16)


def fold(v):
    rows, width = v.shape
    return jnp.sum(v.reshape(rows // 8, 8, width), axis=0)


class Back:
    def __init__(self, v, g, s):
        self.n, self.r = normalized(v)
        self.g = g
        u = self.n * g + s
        phi = upper(u)
        self.act = (u * phi).astype(bf16)
        self.slope = phi + u * (INV_ROOT_2PI * jnp.exp2(u * u * EXP2_SCALE))

    def grad(self, e):
        p = e * self.slope
        pn = p * self.n
        scale = 1.0 / p.shape[-1]
        pg = p * self.g
        a = jnp.sum(pg, axis=-1, keepdims=True) * scale
        b = jnp.sum(pn * self.g, axis=-1, keepdims=True) * scale
        return self.r * (pg - a - self.n * b), fold(pn), fold(p)


def dot(a, b):
    return jnp.dot(a, b, preferred_element_type=f32)


def dot_nt(a, b):
    return lax.dot_general(a, b, (((1,), (1,)), ((), ())), preferred_element_type=f32)


def dot_tn(a, b):
    return lax.dot_general(a, b, (((0,), (0,)), ((), ())), preferred_element_type=f32)


def fill(pad, low, values, high):
    rows = values.shape[0]
    pad[0:REACH, :] = low.astype(f32)
    pad[REACH : REACH + rows, :] = values.astype(f32)
    pad[REACH + rows :, :] = high.astype(f32)


def taps(pad, rows, d, direction):
    pieces = []
    for k in range(KERNEL):
        start = REACH + direction * (k - KERNEL // 2) * d
        pieces.append(pad[start : start + rows, :].astype(bf16))
    return pieces


def row(ref, i):
    return ref[i : i + 1, :]


def inner_row(ref, i):
    half = ref.shape[1] // 2
    return ref[3 + i // 2 : 4 + i // 2, i % 2 * half : (i % 2 + 1) * half]


def column(flags):
    return jnp.transpose(jnp.broadcast_to(flags, (128, flags.shape[1])))


def seeded(cot, flags):
    col = column(flags)
    return cot.astype(f32) * jnp.concatenate([col] * (cot.shape[1] // 128), axis=1)


MESH = pl.DeviceIdType.MESH
UNIT = 16


def bits_of(count):
    return count.bit_length() - 1


def mixed_by(core, first, second):
    return first + core * (second - first)


class Place:
    def __init__(self):
        self.core = lax.axis_index("pipe")
        self.seq = lax.axis_index("seq")
        self.dp = lax.axis_index("dp")
        seq_bits = bits_of(lax.axis_size("seq"))
        dp_bits = bits_of(lax.axis_size("dp"))
        order = list(range(seq_bits))
        cut = seq_bits // 2
        turned = order[cut:] + order[:cut]
        self.stages = [("seq", a, b) for a, b in zip(order, turned)]
        self.stages += [("dp", a, a) for a in range(dp_bits)]

    def bit(self, stage):
        axis, a, b = self.stages[stage]
        spot = self.seq if axis == "seq" else self.dp
        return mixed_by(self.core, (spot // (1 << a)) % 2, (spot // (1 << b)) % 2)

    def peer(self, stage):
        axis, a, b = self.stages[stage]
        spot = self.seq if axis == "seq" else self.dp
        hop = mixed_by(self.core, 1 << a, 1 << b) * (1 - 2 * self.bit(stage))
        return {axis: spot + hop}

    def other_core(self):
        return {"pipe": 1 - self.core}

    def partners(self):
        return [self.other_core()] + [self.peer(s) for s in range(len(self.stages))]

    def line(self):
        n = lax.axis_size("seq")
        return [{"seq": (self.seq + 1) % n}, {"seq": (self.seq + n - 1) % n}]

    def greet(self, friends):
        barrier = pltpu.get_barrier_semaphore()
        for friend in friends:
            pl.semaphore_signal(barrier, inc=1, device_id=friend, device_id_type=MESH)
        pl.semaphore_wait(barrier, len(friends))


def remote(src, dst, send_sem, recv_sem, device):
    return pltpu.make_async_remote_copy(
        src_ref=src,
        dst_ref=dst,
        send_sem=send_sem,
        recv_sem=recv_sem,
        device_id=device,
        device_id_type=MESH,
    )


class Halo:
    def __init__(self, place, edges, halo, sems):
        self.place, self.edges, self.halo, self.sems = place, edges, halo, sems
        self.has_low = place.seq > 0
        self.has_high = place.seq < lax.axis_size("seq") - 1

    @staticmethod
    def scratch(count, width):
        return [
            pltpu.VMEM((2, count, REACH, width), bf16),
            pltpu.VMEM((2, count, REACH, width), bf16),
            pltpu.SemaphoreType.DMA((4, count)),
        ]

    def up(self, i):
        device = {"seq": self.place.seq + 1}
        sems = self.sems
        return remote(self.edges.at[1, i], self.halo.at[0, i], sems.at[0, i], sems.at[1, i], device)

    def down(self, i):
        device = {"seq": self.place.seq - 1}
        sems = self.sems
        return remote(self.edges.at[0, i], self.halo.at[1, i], sems.at[2, i], sems.at[3, i], device)

    def begin(self):
        @pl.when(jnp.logical_not(self.has_low))
        def _():
            self.halo[0] = jnp.zeros_like(self.halo[0])

        @pl.when(jnp.logical_not(self.has_high))
        def _():
            self.halo[1] = jnp.zeros_like(self.halo[1])

    def send(self, i, values):
        self.edges[0, i] = values[:REACH]
        self.edges[1, i] = values[values.shape[0] - REACH :]

        @pl.when(self.has_high)
        def _():
            self.up(i).start()

        @pl.when(self.has_low)
        def _():
            self.down(i).start()

    def take(self, i):
        @pl.when(self.has_low)
        def _():
            self.down(i).wait_send()
            self.up(i).wait_recv()

        @pl.when(self.has_high)
        def _():
            self.up(i).wait_send()
            self.down(i).wait_recv()

    def around(self, pad, i, values):
        fill(pad, self.halo[0, i], values, self.halo[1, i])


class Halves:
    def __init__(self, place, count, out, own, other, sems, arrivals):
        self.place, self.count, self.out = place, count, out
        self.own, self.other, self.sems, self.arrivals = own, other, sems, arrivals

    @staticmethod
    def scratch(count, rows, half):
        return [
            pltpu.VMEM((2, rows, half), bf16),
            pltpu.VMEM((2, rows, half), bf16),
            pltpu.SemaphoreType.DMA((2, 2)),
            pltpu.SemaphoreType.DMA((count,)),
        ]

    def local(self, i, slot):
        to = self.place.core * self.count + i
        return pltpu.make_async_copy(self.own.at[slot], self.out.at[to], self.sems.at[0, slot])

    def away(self, i, slot):
        to = self.place.core * self.count + i
        return remote(
            self.other.at[slot],
            self.out.at[to],
            self.sems.at[1, slot],
            self.arrivals.at[i],
            self.place.other_core(),
        )

    def release(self, i, slot):
        self.local(i, slot).wait()
        self.away(i, slot).wait_send()

    def send(self, i, values):
        slot = i % 2
        half = values.shape[1] // 2
        left, right = values[:, :half], values[:, half:]

        @pl.when(i >= 2)
        def _():
            self.release(i - 2, slot)

        first = self.place.core == 0
        self.own[slot] = jnp.where(first, left, right)
        self.other[slot] = jnp.where(first, right, left)
        self.local(i, slot).start()
        self.away(i, slot).start()

    def end(self):
        for i in range(max(0, self.count - 2), self.count):
            self.release(i, i % 2)

        def body(i, carry):
            self.away(i, 0).wait_recv()
            return carry

        lax.fori_loop(0, self.count, body, 0)


def groups_of(inner, width):
    joined = width + KERNEL * inner
    half = joined // 2
    out, at = [(width // 2, 0, width // 2)], 0
    while at < half:
        rows = min(width // 2, half - at)
        out.append((rows, at, half))
        at += rows
    return out


class BlockSum:
    def __init__(self, place, block, groups, part, out, room):
        self.place, self.block, self.parts, self.out = place, block, part, out
        self.groups, sizes = groups, [g[0] for g in groups]
        self.sizes = sizes
        self.theirs, self.sbuf, self.rbuf, self.res = room[:4]
        self.core_sems, self.send_sems, self.recv_sems, self.out_sems = room[4:]
        self.levels = len(place.stages)
        self.starts = [sum(sizes[:g]) for g in range(len(sizes))]
        sent = [sum(self.lengths(n, self.levels)[1:]) for n in sizes]
        self.bases = [sum(sent[:g]) for g in range(len(sizes))]

    @staticmethod
    def lengths(rows, levels):
        out = [rows]
        for _ in range(levels):
            last = out[-1]
            out.append(last // 2 if last % (2 * UNIT) == 0 else last)
        return out

    @staticmethod
    def scratch(groups, width, levels):
        sizes = [g[0] for g in groups]
        rows, groups = sum(sizes), len(sizes)
        sent = sum(sum(BlockSum.lengths(n, levels)[1:]) for n in sizes)
        dma = pltpu.SemaphoreType.DMA
        return [
            pltpu.VMEM((rows, width), bf16),
            pltpu.VMEM((sent, width), bf16),
            pltpu.VMEM((sent, width), bf16),
            pltpu.VMEM((rows, width), bf16),
            dma((groups, 2)),
            dma((groups, 2 * levels)),
            dma((groups, 2 * levels)),
            dma((groups, 3)),
        ]

    def spots(self, g):
        lengths = self.lengths(self.sizes[g], self.levels)
        start, out = self.starts[g], []
        for s in range(self.levels):
            out.append((start, lengths[s]))
            if lengths[s + 1] < lengths[s]:
                start = start + self.place.bit(s) * lengths[s + 1]
        out.append((start, lengths[-1]))
        return out

    def base(self, g, s):
        return self.bases[g] + sum(self.lengths(self.sizes[g], self.levels)[1 : s + 1])

    def value(self, g, s, start, n):
        lengths, spots = self.lengths(self.sizes[g], self.levels), self.spots(g)
        terms = [
            (self.part(g), self.row(g, self.place.core) + (start - self.starts[g])),
            (self.theirs, start),
        ]
        for k in range(s):
            at = self.base(g, k) + (start - spots[k + 1][0])
            if lengths[k + 1] == lengths[k]:
                terms = [(self.sbuf, at)]
            terms.append((self.rbuf, at))
        total = None
        for ref, at in terms:
            term = ref[pl.ds(pl.multiple_of(at, UNIT), n), :].astype(f32)
            total = term if total is None else total + term
        return total

    def part(self, g):
        return self.parts[0 if g > 0 else 1]

    def row(self, g, half):
        _, at, stride = self.groups[g]
        return at + half * stride

    def core_copy(self, g):
        n = self.sizes[g]
        source = pl.multiple_of(self.row(g, 1 - self.place.core), UNIT)
        return remote(
            self.part(g).at[pl.ds(source, n)],
            self.theirs.at[pl.ds(self.starts[g], n)],
            self.core_sems.at[g, 0],
            self.core_sems.at[g, 1],
            self.place.other_core(),
        )

    def down(self, g, s):
        n = self.lengths(self.sizes[g], self.levels)[s + 1]
        at = pl.ds(self.base(g, s), n)
        return remote(
            self.sbuf.at[at],
            self.rbuf.at[at],
            self.send_sems.at[g, s],
            self.recv_sems.at[g, s],
            self.place.peer(s),
        )

    def start_down(self, g, s):
        start, rows = self.spots(g)[s]
        n = self.lengths(self.sizes[g], self.levels)[s + 1]
        if n < rows:
            start = start + (1 - self.place.bit(s)) * n
        base = self.base(g, s)
        self.sbuf[base : base + n, :] = self.value(g, s, start, n).astype(bf16)
        self.down(g, s).start()

    def up(self, g, s):
        lengths = self.lengths(self.sizes[g], self.levels)
        if lengths[s] == lengths[s + 1]:
            return None
        start, n = self.spots(g)[s + 1]
        at = pl.ds(pl.multiple_of(start, UNIT), n)
        return remote(
            self.res.at[at],
            self.res.at[at],
            self.send_sems.at[g, self.levels + s],
            self.recv_sems.at[g, self.levels + s],
            self.place.peer(s),
        )

    def target(self, g, half):
        n, at = self.sizes[g], self.row(g, half)
        narrow, dilated, restore = self.out
        if g == 0:
            return restore.at[:, pl.ds(at, n)]
        top = narrow.shape[0]
        return narrow.at[pl.ds(at, n)] if at < top else dilated.at[pl.ds(at - top, n)]

    def keep(self, g, half):
        at = pl.ds(self.starts[g], self.sizes[g])
        return pltpu.make_async_copy(self.res.at[at], self.target(g, half), self.out_sems.at[g, 0])

    def give(self, g, half):
        at = pl.ds(self.starts[g], self.sizes[g])
        return remote(
            self.res.at[at],
            self.target(g, half),
            self.out_sems.at[g, 1],
            self.out_sems.at[g, 2],
            self.place.other_core(),
        )

    def steps(self):
        return 2 * self.levels + 3

    def step(self, g, t):
        core, levels = self.place.core, self.levels
        if t == 0:
            self.core_copy(g).start()
        if t == 1:
            self.core_copy(g).wait()
        if 2 <= t < 2 + levels:
            self.down(g, t - 2).wait()
        if 1 <= t < 1 + levels:
            self.start_down(g, t - 1)
        if t == 1 + levels:
            start, n = self.spots(g)[levels]
            at = pl.ds(pl.multiple_of(start, UNIT), n)
            self.res[at, :] = self.value(g, levels, start, n).astype(bf16)
        if 2 + levels <= t < 2 + 2 * levels:
            copy = self.up(g, 2 * levels + 1 - t)
            if copy is not None:
                copy.wait()
        if 1 + levels <= t < 1 + 2 * levels:
            copy = self.up(g, 2 * levels - t)
            if copy is not None:
                copy.start()
        if t == 1 + 2 * levels:
            for half in (0, 1):

                @pl.when(core == half)
                def _():
                    if half == self.block:
                        self.keep(g, half).start()
                    else:
                        self.give(g, half).start()

        if t == 2 + 2 * levels:
            for half in (0, 1):

                @pl.when(core == half)
                def _():
                    if half == self.block:
                        self.keep(g, half).wait()
                        self.give(g, 1 - half).wait_recv()
                    else:
                        self.give(g, half).wait_send()


SEQ_TIMES = (5.0, 2.1, 2.5)
AFTER_TIME = 0.7
LATENCY = 3.5
CHIP_RATE = 1.0e5
CORE_RATE = 5.0e5


def plan(place, groups, width, begins, spans):
    levels = len(place.stages)
    times, now = [], 0.0
    for steps, length in (*spans, (400, AFTER_TIME)):
        for _ in range(steps):
            times.append(now)
            now += length

    def sent(g, t):
        rows = groups[g][0]
        lengths = BlockSum.lengths(rows, levels)
        size = 2 * width
        if t in (0, 2 * levels + 1):
            return "pipe", rows * size / CORE_RATE
        s = t - 1 if t <= levels else 2 * levels - t
        axis, bit, _ = place.stages[s]
        flows = 1 if axis == "seq" else 2 << bit
        if t > levels and lengths[s] == lengths[s + 1]:
            flows = 0
        return axis, lengths[s + 1] * size * flows / CHIP_RATE

    due, free = {}, {}
    ready = {(block, g): times[at] for block, g, at in begins}
    tick = dict.fromkeys(ready, 0)
    for k, now in enumerate(times):
        for key in [key for key in ready if ready[key] <= now]:
            t = tick[key]
            due.setdefault(k, []).append((*key, t))
            tick[key] += 1
            if t == 2 * levels + 2:
                del ready[key]
                continue
            link, busy = sent(key[1], t)
            free[link] = max(free.get(link, 0.0), now) + busy
            ready[key] = free[link] + LATENCY
    assert not ready
    return due


class SmallSum:
    def __init__(self, place, total, arrived, sems):
        self.place, self.total, self.arrived, self.sems = place, total, arrived, sems
        self.stages = len(place.stages) + 1

    @staticmethod
    def scratch(rows, width, levels):
        return [
            pltpu.VMEM((levels + 2, rows, width), f32),
            pltpu.VMEM((levels + 1, rows, width), f32),
            pltpu.SemaphoreType.DMA((levels + 1, 2)),
        ]

    def copy(self, s):
        device = self.place.other_core() if s == 0 else self.place.peer(s - 1)
        return remote(
            self.total.at[s], self.arrived.at[s], self.sems.at[s, 0], self.sems.at[s, 1], device
        )

    def start(self, s):
        self.copy(s).start()

    def end(self, s):
        self.copy(s).wait()
        self.total[s + 1] = self.total[s] + self.arrived[s]


def gather_small(total, block, bias_ref, upper_ref, wide_ref, small_ref):
    half = total.shape[-1]
    rows = []
    for ref in (wide_ref, bias_ref):
        for k in range(ref.shape[0] // 8):
            for lane in range(0, ref.shape[1], half):
                rows.append((ref, k, lane))
    for ref, k in ((small_ref, 0), (upper_ref, 0), (small_ref, 1), (small_ref, 2), (upper_ref, 1), (upper_ref, 2)):
        rows.append((ref, k, 0))
    for j, (ref, k, lane) in enumerate(rows):
        piece = ref[8 * k : 8 * k + 8, lane : lane + half]
        total[0, 16 * block + j : 16 * block + j + 1, :] = jnp.sum(piece, axis=0, keepdims=True)


def block_out_back(back, grad_low, restore, restore_sum, bias_sum, upper_sum):
    restore_sum[...] += dot_tn(back.act, grad_low)
    bias_sum[...] += fold(grad_low.astype(f32))
    gv, gain, shift = back.grad(dot_nt(grad_low, restore[...]))
    gm = gv.astype(bf16)
    upper_sum[0:8] += fold(gm.astype(f32))
    upper_sum[8:16] += gain
    upper_sum[16:24] += shift
    return gm


def convolution_back(hidden, gm, windows, gm_taps, inner, dilated, dilated_sum, small_sum):
    width = dilated.shape[1]
    grad_second = None
    for k, piece in enumerate(gm_taps):
        term = dot_nt(piece, dilated[k * width : (k + 1) * width, :])
        grad_second = term if grad_second is None else grad_second + term
    dilated_sum[...] += dot_tn(windows(), gm())
    back = Back(hidden(), inner_row(inner, 2), inner_row(inner, 3))
    gv, gain, shift = back.grad(grad_second)
    gh = gv.astype(bf16)
    small_sum[0:8] += fold(gh.astype(f32))
    small_sum[8:16] += gain
    small_sum[16:24] += shift
    return gh


def stream_back(first, gh, narrow, wide_sum):
    gx, gain, shift = first.grad(dot_nt(gh, narrow[...]))
    wide_sum[0:8] += gain
    wide_sum[8:16] += shift
    return gx


def clear(*refs):
    for ref in refs:
        ref[...] = jnp.zeros_like(ref)


class Refs:
    def __init__(self, names, refs):
        for name, ref in zip(names, refs, strict=True):
            setattr(self, name, ref)


def whole(names, count, groups, residues, *refs):
    r = Refs(names, refs)
    place = Place()
    core = place.core
    rows, width = r.inputs.shape[1:]
    inner = r.narrow.shape[2]
    small_counts = SmallSum(place, *r.count_room)
    halos = [Halo(place, *room) for room in r.halo_rooms]
    outputs = Halves(place, count, r.block_output, *r.halves_room)
    grads = Halves(place, count, r.input_grad, *r.grads_room)
    outer, joined, restore = r.outer_v, r.joined_v, r.restore_v
    narrow = [joined.at[b, 0:width] for b in (0, 1)]
    dilated = [joined.at[b, width : width + KERNEL * inner] for b in (0, 1)]
    params = (
        (r.outer, lambda at: outer.at[at]),
        (r.narrow, lambda at: joined.at[at, 0:width]),
        (r.dilated, lambda at: joined.at[at, width : width + KERNEL * inner]),
        (r.restore, lambda at: restore.at[at]),
    )
    parts = [(joined.at[1], r.restore_parts[0]), (r.joined_part, r.restore_parts[1])]
    totals = (r.narrow_total, r.dilated_total, r.restore_total)
    sets = [BlockSum(place, b, groups, parts[b], totals, r.sum_rooms[b]) for b in (0, 1)]
    seqs = [n if count % n == 0 else 1 for n in STEP_SEQS]
    stage_steps = [count // n for n in seqs]

    def local(k):
        src, dst = params[k]
        return pltpu.make_async_copy(src, dst(pl.ds(core, 1)), r.param_sems.at[0, k])

    def away(k):
        src, dst = params[k]
        to = dst(pl.ds(core, 1))
        return remote(src, to, r.param_sems.at[1, k], r.param_sems.at[2, k], place.other_core())

    def arrive(k, block):
        @pl.when(core == block)
        def _():
            local(k).wait()

        @pl.when(core != block)
        def _():
            away(k).wait_recv()

    def over(stage, body, ins, outs):
        n, steps = seqs[stage], stage_steps[stage]

        def spec(a, own):
            shape = (n, *a.shape[1:])
            if own:
                return pl.BlockSpec(shape, lambda i: (core * steps + i, 0, 0))
            return pl.BlockSpec(shape, lambda i: (i, 0, 0))

        def flat(*blocks):
            def reader(ref):
                return lambda: ref[...].reshape(n * rows, ref.shape[2])

            def writer(ref):
                def write(v):
                    ref[...] = v.astype(ref.dtype).reshape(ref.shape)

                return write

            cut = len(ins)
            body(pl.program_id(0), *map(reader, blocks[:cut]), *map(writer, blocks[cut:]))

        pipe = pltpu.emit_pipeline(
            flat,
            grid=(steps,),
            in_specs=[spec(a, a is r.inputs or a is r.cotangent) for a in ins],
            out_specs=[spec(a, False) for a in outs],
        )
        pipe(*ins, *outs)

    def each(stage, i):
        n = seqs[stage]
        return [(i * n + j, slice(j * rows, (j + 1) * rows)) for j in range(n)]

    def surround(stage, halo, pads, i, values):
        for j, (at, part) in enumerate(each(stage, i)):
            halo.around(pads.at[j], at, values[part])

    def tapped(stage, pads, d, direction):
        found = [taps(pads.at[j], rows, d, direction) for j in range(seqs[stage])]
        return [jnp.concatenate(pieces, axis=0) for pieces in zip(*found)]

    def windows_of(stage, pads, d):
        return jnp.concatenate(tapped(stage, pads, d, 1), axis=1)

    def take(stage, halo, i):
        for at, _ in each(stage, i):
            halo.take(at)

    def send(stage, sender, i, values):
        for at, part in each(stage, i):
            sender.send(at, values[part])

    def seed_of(stage, i, cot):
        return jnp.concatenate([seeded(cot[part], flags_of(at)) for at, part in each(stage, i)], axis=0)

    def flags_of(i):
        masked = jnp.sum(small_counts.total[small_counts.stages][1:2, :], axis=1, keepdims=True)
        return r.flags[core * count + i] * (residues / masked)

    place.greet(place.line() + place.partners())
    for k in range(len(params)):
        local(k).start()
        away(k).start()
    small_counts.total[1] = r.counts[...]
    for halo in halos:
        halo.begin()
    clear(r.narrow_sum, r.dilated_sum, r.restore_sum)
    clear(*r.wide_sums, *r.bias_sums, *r.upper_sums, *r.small_sums)
    for k in range(2):
        arrive(k, 0)

    def count_step(k):
        if k > 1:
            small_counts.end(k - 1)
        small_counts.start(k)

    def first(i, x, act_out, hidden_out, second_out):
        for k in range(1, min(small_counts.stages, stage_steps[0])):

            @pl.when(i == k)
            def _():
                count_step(k)

        act = norm_act(x().astype(f32), row(outer.at[0], 0), row(outer.at[0], 1))
        act_out(act)
        hidden = dot(act, narrow[0][...]) + inner_row(outer.at[0], 0)
        hidden_out(hidden)
        second = norm_act(hidden, inner_row(outer.at[0], 2), inner_row(outer.at[0], 3))
        second_out(second)
        send(0, halos[0], i, second)

    over(0, first, [r.inputs], [r.first0, r.hidden0, r.second0])
    for k in range(stage_steps[0], small_counts.stages):
        count_step(k)
    small_counts.end(small_counts.stages - 1)
    r.counts_out[...] = small_counts.total[small_counts.stages]
    for k in range(len(params)):
        away(k).wait_send()
        arrive(k, 1)
        if k >= 2:
            arrive(k, 0)

    def second(i, x, second_in, mixed_out, middle_out, hidden_out, second_out):
        take(1, halos[0], i)
        surround(1, halos[0], r.pads, i, second_in())
        windows = windows_of(1, r.pads, FIRST_DILATION)
        mixed = dot(windows, dilated[0][...]) + inner_row(outer.at[0], 1)
        mixed_out(mixed)
        third = norm_act(mixed, inner_row(outer.at[0], 4), inner_row(outer.at[0], 5))
        y = x().astype(f32) + (dot(third, restore[0]) + row(outer.at[0], 2))
        middle_out(y)
        act = norm_act(y, row(outer.at[1], 0), row(outer.at[1], 1))
        hidden = dot(act, narrow[1][...]) + inner_row(outer.at[1], 0)
        hidden_out(hidden)
        second = norm_act(hidden, inner_row(outer.at[1], 2), inner_row(outer.at[1], 3))
        second_out(second)
        send(1, halos[1], i, second)

    over(1, second, [r.inputs, r.second0], [r.mixed0, r.middle, r.hidden1, r.second1])

    def turn(i, second_in, cot, third_out, gm_out):
        take(2, halos[1], i)
        surround(2, halos[1], r.pads, i, second_in())
        windows = windows_of(2, r.pads, SECOND_DILATION)
        mixed = dot(windows, dilated[1][...]) + inner_row(outer.at[1], 1)
        back = Back(mixed, inner_row(outer.at[1], 4), inner_row(outer.at[1], 5))
        third_out(back.act)
        grad_low = seed_of(2, i, cot()).astype(bf16)
        gm = block_out_back(back, grad_low, restore.at[1], r.restore_sum, r.bias_sums[1], r.upper_sums[1])
        gm_out(gm)
        send(2, halos[2], i, gm)

    over(2, turn, [r.second1, r.cotangent], [r.third1, r.gm1])
    write_restore(r.restore_parts[1], r.restore_sum)
    clear(r.restore_sum)

    spans = [(steps, n * time) for steps, n, time in zip(stage_steps[3:], seqs[3:], SEQ_TIMES)]
    fifth, sixth = stage_steps[3], stage_steps[3] + stage_steps[4]
    ends = sixth + stage_steps[5]
    begins = [(1, 0, 0)]
    begins += [(1, g, fifth) for g in range(1, len(groups))]
    begins += [(0, 0, fifth + stage_steps[4] // 3)]
    begins += [(0, g, sixth) for g in range(1, len(groups))]
    due = plan(place, groups, inner, begins, spans)

    def beside(base, steps, i):
        for k in range(steps):
            if base + k in due:

                @pl.when(i == k)
                def _():
                    for block, g, t in due[base + k]:
                        sets[block].step(g, t)

    def between(i, middle, cot, hidden, second_in, gm, mixed, gx_out, gm_out):
        beside(0, stage_steps[3], i)
        take(3, halos[2], i)
        surround(3, halos[2], r.gm_pads, i, gm())
        surround(3, halos[1], r.pads, i, second_in())
        gh = convolution_back(
            hidden,
            gm,
            lambda: windows_of(3, r.pads, SECOND_DILATION),
            tapped(3, r.gm_pads, SECOND_DILATION, -1),
            outer.at[1],
            dilated[1],
            r.dilated_sum,
            r.small_sums[1],
        )
        first = Back(middle().astype(f32), row(outer.at[1], 0), row(outer.at[1], 1))
        r.narrow_sum[...] += dot_tn(first.act, gh)
        gx = seed_of(3, i, cot()) + stream_back(first, gh, narrow[1], r.wide_sums[1])
        gx_out(gx)
        back = Back(mixed(), inner_row(outer.at[0], 4), inner_row(outer.at[0], 5))
        gm = block_out_back(back, gx.astype(bf16), restore.at[0], r.restore_sum, r.bias_sums[0], r.upper_sums[0])
        gm_out(gm)
        send(3, halos[3], i, gm)

    over(3, between, [r.middle, r.cotangent, r.hidden1, r.second1, r.gm1, r.mixed0], [r.gx1, r.gm0])
    write_joined(r.joined_part, r.narrow_sum, r.dilated_sum)
    write_restore(r.restore_parts[0], r.restore_sum)
    clear(r.narrow_sum, r.dilated_sum)

    def inward(i, act, hidden, second_in, gm, gh_out):
        beside(fifth, stage_steps[4], i)
        take(4, halos[3], i)
        surround(4, halos[3], r.gm_pads, i, gm())
        surround(4, halos[0], r.pads, i, second_in())
        gh = convolution_back(
            hidden,
            gm,
            lambda: windows_of(4, r.pads, FIRST_DILATION),
            tapped(4, r.gm_pads, FIRST_DILATION, -1),
            outer.at[0],
            dilated[0],
            r.dilated_sum,
            r.small_sums[0],
        )
        gh_out(gh)
        r.narrow_sum[...] += dot_tn(act(), gh)

    over(4, inward, [r.first0, r.hidden0, r.second0, r.gm0], [r.gh0])
    write_joined(joined.at[1], r.narrow_sum, r.dilated_sum)

    def last(i, x, gx_in, gh, middle, third):
        beside(sixth, stage_steps[5], i)
        y = middle().astype(f32) + (dot(third(), restore[1]) + row(outer.at[1], 2))
        send(5, outputs, i, y.astype(bf16))
        first = Back(x().astype(f32), row(outer.at[0], 0), row(outer.at[0], 1))
        gx = gx_in().astype(f32) + stream_back(first, gh(), narrow[0], r.wide_sums[0])
        send(5, grads, i, gx.astype(bf16))

    over(5, last, [r.inputs, r.gx1, r.gh0, r.middle, r.third1], [])

    small = SmallSum(place, *r.small_room)
    small.total[0] = jnp.zeros_like(small.total[0])
    for b in (0, 1):
        gather_small(small.total, b, r.bias_sums[b], r.upper_sums[b], r.wide_sums[b], r.small_sums[b])
    after = sorted(at for at in due if at >= ends)
    for t in range(max(len(after), small.stages + 1)):
        if t < len(after):
            for block, g, k in due[after[t]]:
                sets[block].step(g, k)
        if 0 < t <= small.stages:
            small.end(t - 1)
        if t < small.stages:
            small.start(t)
    r.small_out[...] = small.total[small.stages]
    outputs.end()
    grads.end()


def write_restore(part, total):
    inner, wide = total.shape
    for j in range(wide // inner):
        at = j * inner
        part[at : at + inner, :] = total[:, j * inner : (j + 1) * inner].astype(bf16)


def write_joined(part, narrow_sum, dilated_sum):
    cut, deep = narrow_sum.shape[0], dilated_sum.shape[0]
    part[:cut, :] = narrow_sum[...].astype(bf16)
    part[cut : cut + deep, :] = dilated_sum[...].astype(bf16)


def shards(
    inputs,
    cotangent,
    mask_flags,
    residue_types,
    predicted,
    outer_params,
    narrow,
    dilated,
    restore,
    inner_params,
):
    core = lax.axis_index("pipe")
    chip_seqs, rows, width = inputs.shape
    inner = narrow.shape[-1]
    count = chip_seqs // 2
    half = width // 2
    levels = bits_of(lax.axis_size("seq")) + bits_of(lax.axis_size("dp"))
    type_ids = jnp.arange(TYPES, dtype=jnp.int32)
    matches = residue_types[:, :, None] == type_ids
    right_flags = mask_flags * (predicted == residue_types).astype(jnp.int32)
    right_counts = jnp.sum(jnp.where(matches, right_flags[:, :, None], 0), axis=(0, 1))
    masked_counts = jnp.sum(jnp.where(matches, mask_flags[:, :, None], 0), axis=(0, 1))
    counts = jnp.stack([right_counts, masked_counts]).astype(f32)
    counts = jnp.pad(counts, ((0, 8 - 2), (0, 128 - TYPES)))

    flags = mask_flags.astype(f32)[:, None, :]
    groups = groups_of(inner, width)
    residues = float(chip_seqs * lax.axis_size("dp") * LENGTH)
    deep = KERNEL * inner
    any_space, vmem = pl.BlockSpec(memory_space=pl.ANY), pl.BlockSpec(memory_space=pltpu.VMEM)
    packed = jnp.concatenate([outer_params, inner_params.reshape(1, 3, width)], axis=1)
    packed = jnp.pad(packed, ((0, 0), (0, 2), (0, 0)))
    args = [
        ("inputs", inputs, any_space),
        ("cotangent", cotangent, any_space),
        ("flags", flags, vmem),
        ("counts", counts, vmem),
        ("outer", packed, any_space),
        ("narrow", narrow, any_space),
        ("dilated", dilated.reshape(1, deep, inner), any_space),
        ("restore", restore, any_space),
    ]
    results = [
        ("block_output", (chip_seqs, rows, half), bf16, any_space),
        ("input_grad", (chip_seqs, rows, half), bf16, any_space),
        ("narrow_total", (width, inner), bf16, any_space),
        ("dilated_total", (deep, inner), bf16, any_space),
        ("restore_total", (inner, width), bf16, any_space),
        ("small_out", (32, inner), f32, vmem),
        ("counts_out", (8, 128), f32, vmem),
        ("third1", (count, rows, inner), bf16, any_space),
        ("first0", (count, rows, width), bf16, any_space),
        ("gh0", (count, rows, inner), bf16, any_space),
        ("hidden0", (count, rows, inner), f32, any_space),
        ("hidden1", (count, rows, inner), f32, any_space),
        ("mixed0", (count, rows, inner), f32, any_space),
        ("middle", (count, rows, width), KEPT, any_space),
        ("gx1", (count, rows, width), KEPT, any_space),
        ("second0", (count, rows, inner), bf16, any_space),
        ("second1", (count, rows, inner), bf16, any_space),
        ("gm0", (count, rows, inner), bf16, any_space),
        ("gm1", (count, rows, inner), bf16, any_space),
    ]

    def twice(a):
        return pltpu.VMEM((2, *a.shape[1:]), a.dtype)

    def sums(*shape):
        return pltpu.VMEM(shape, f32)

    scratch = [
        ("outer_v", twice(packed)),
        ("joined_v", pltpu.VMEM((2, width + deep, inner), bf16)),
        ("restore_v", twice(restore)),
        ("param_sems", pltpu.SemaphoreType.DMA((3, 5))),
        ("count_room", SmallSum.scratch(8, 128, levels)),
        ("small_room", SmallSum.scratch(32, inner, levels)),
        ("halo_rooms", [Halo.scratch(count, inner) for _ in range(4)]),
        ("halves_room", Halves.scratch(count, rows, half)),
        ("grads_room", Halves.scratch(count, rows, half)),
        ("pads", sums(max(STEP_SEQS), rows + 2 * REACH, inner)),
        ("gm_pads", sums(max(STEP_SEQS[3:5]), rows + 2 * REACH, inner)),
        ("narrow_sum", sums(width, inner)),
        ("dilated_sum", sums(deep, inner)),
        ("restore_sum", sums(inner, width)),
        ("wide_sums", [sums(16, width)] * 2),
        ("bias_sums", [sums(8, width)] * 2),
        ("upper_sums", [sums(24, inner)] * 2),
        ("small_sums", [sums(24, inner)] * 2),
        ("restore_parts", [pltpu.VMEM((width, inner), bf16)] * 2),
        ("joined_part", pltpu.VMEM((width + deep, inner), bf16)),
        ("sum_rooms", [BlockSum.scratch(groups, inner, levels) for _ in range(2)]),
    ]
    names = [a[0] for a in args] + [a[0] for a in results] + [a[0] for a in scratch]
    outs = pl.pallas_call(
        functools.partial(whole, names, count, groups, residues),
        out_shape=[jax.ShapeDtypeStruct(shape, dtype) for _, shape, dtype, _ in results],
        in_specs=[a[2] for a in args],
        out_specs=[a[3] for a in results],
        scratch_shapes=[a[1] for a in scratch],
        compiler_params=pltpu.CompilerParams(
            vmem_limit_bytes=VMEM_LIMIT, collective_id=0, has_side_effects=True
        ),
        name="whole",
    )(*[a[1] for a in args])
    block_output, input_grad, narrow_total, dilated_total, restore_total, smalls, counts = outs[:7]
    accuracy = counts[:2, :TYPES].astype(jnp.int32)
    smalls = lax.dynamic_slice_in_dim(smalls, core * 16, 16, 0)
    narrow_total = narrow_total.astype(f32)
    dilated_total = dilated_total.astype(f32)
    restore_total = restore_total.astype(f32)
    outer_total = smalls[: 3 * width // inner].reshape(3, width)
    inner_total = smalls[3 * width // inner :][:6]

    return (
        block_output,
        input_grad,
        outer_total[None],
        narrow_total[None],
        dilated_total.reshape(1, KERNEL, inner, inner),
        restore_total[None],
        inner_total[None],
        accuracy,
    )


def solution(mesh):
    in_specs = (
        P("dp", "seq", None),
        P("dp", "seq", None),
        P("dp", "seq"),
        P("dp", "seq"),
        P("dp", "seq"),
        P("pipe", None, None),
        P("pipe", None, None),
        P("pipe", None, None, None),
        P("pipe", None, None),
        P("pipe", None, None),
    )
    out_specs = (
        P("dp", "seq", "pipe"),
        P("dp", "seq", "pipe"),
        P("pipe", None, None),
        P("pipe", None, None),
        P("pipe", None, None, None),
        P("pipe", None, None),
        P("pipe", None, None),
        P(),
    )
    return jax.shard_map(shards, mesh=mesh, in_specs=in_specs, out_specs=out_specs, check_vma=False)
```

```python
import functools

import jax
import jax.numpy as jnp
from jax import lax
from jax.experimental import pallas as pl
from jax.experimental.pallas import tpu as pltpu
from jax.sharding import PartitionSpec as P

KERNEL = 5
FIRST_DILATION = 2
SECOND_DILATION = 4
TYPES = 30
LENGTH = 1024
REACH = 8
EPSILON = 1e-05
VMEM_LIMIT = 63 << 20

f32 = jnp.float32
bf16 = jnp.bfloat16
KEPT = bf16
STEP_SEQS = (2, 2, 2, 1, 2, 2)

ROOT_HALF = 0.7071067811865476
INV_ROOT_2PI = 0.3989422804014327
EXP2_SCALE = -0.5 * 1.4426950408889634


def normalized(v):
    scale = 1.0 / v.shape[-1]
    centered = v - jnp.sum(v, axis=-1, keepdims=True) * scale
    spread = jnp.sum(centered * centered, axis=-1, keepdims=True) * scale
    r = lax.rsqrt(spread + EPSILON)
    return centered * r, r


def upper(u):
    return 0.5 * lax.erf(u * ROOT_HALF) + 0.5


def norm_act(v, g, s):
    n, _ = normalized(v)
    u = n * g + s
    return (u * upper(u)).astype(bf16)


def fold(v):
    rows, width = v.shape
    return jnp.sum(v.reshape(rows // 8, 8, width), axis=0)


class Back:
    def __init__(self, v, g, s):
        self.n, self.r = normalized(v)
        self.g = g
        u = self.n * g + s
        phi = upper(u)
        self.act = (u * phi).astype(bf16)
        self.slope = phi + u * (INV_ROOT_2PI * jnp.exp2(u * u * EXP2_SCALE))

    def grad(self, e):
        p = e * self.slope
        pn = p * self.n
        scale = 1.0 / p.shape[-1]
        pg = p * self.g
        a = jnp.sum(pg, axis=-1, keepdims=True) * scale
        b = jnp.sum(pn * self.g, axis=-1, keepdims=True) * scale
        return self.r * (pg - a - self.n * b), fold(pn), fold(p)


def dot(a, b):
    return jnp.dot(a, b, preferred_element_type=f32)


def dot_nt(a, b):
    return lax.dot_general(a, b, (((1,), (1,)), ((), ())), preferred_element_type=f32)


def dot_tn(a, b):
    return lax.dot_general(a, b, (((0,), (0,)), ((), ())), preferred_element_type=f32)


def fill(pad, low, values, high):
    rows = values.shape[0]
    pad[0:REACH, :] = low.astype(f32)
    pad[REACH : REACH + rows, :] = values.astype(f32)
    pad[REACH + rows :, :] = high.astype(f32)


def taps(pad, rows, d, direction):
    pieces = []
    for k in range(KERNEL):
        start = REACH + direction * (k - KERNEL // 2) * d
        pieces.append(pad[start : start + rows, :].astype(bf16))
    return pieces


def row(ref, i):
    return ref[i : i + 1, :]


def inner_row(ref, i):
    half = ref.shape[1] // 2
    return ref[3 + i // 2 : 4 + i // 2, i % 2 * half : (i % 2 + 1) * half]


def column(flags):
    return jnp.transpose(jnp.broadcast_to(flags, (128, flags.shape[1])))


def seeded(cot, flags):
    col = column(flags)
    return cot.astype(f32) * jnp.concatenate([col] * (cot.shape[1] // 128), axis=1)


MESH = pl.DeviceIdType.MESH
UNIT = 16


def bits_of(count):
    return count.bit_length() - 1


def mixed_by(core, first, second):
    return first + core * (second - first)


class Place:
    def __init__(self):
        self.core = lax.axis_index("pipe")
        self.seq = lax.axis_index("seq")
        self.dp = lax.axis_index("dp")
        seq_bits = bits_of(lax.axis_size("seq"))
        dp_bits = bits_of(lax.axis_size("dp"))
        order = list(range(seq_bits))
        cut = seq_bits // 2
        turned = order[cut:] + order[:cut]
        self.stages = [("seq", a, b) for a, b in zip(order, turned)]
        self.stages += [("dp", a, a) for a in range(dp_bits)]

    def bit(self, stage):
        axis, a, b = self.stages[stage]
        spot = self.seq if axis == "seq" else self.dp
        return mixed_by(self.core, (spot // (1 << a)) % 2, (spot // (1 << b)) % 2)

    def peer(self, stage):
        axis, a, b = self.stages[stage]
        spot = self.seq if axis == "seq" else self.dp
        hop = mixed_by(self.core, 1 << a, 1 << b) * (1 - 2 * self.bit(stage))
        return {axis: spot + hop}

    def other_core(self):
        return {"pipe": 1 - self.core}

    def partners(self):
        return [self.other_core()] + [self.peer(s) for s in range(len(self.stages))]

    def line(self):
        n = lax.axis_size("seq")
        return [{"seq": (self.seq + 1) % n}, {"seq": (self.seq + n - 1) % n}]

    def greet(self, friends):
        barrier = pltpu.get_barrier_semaphore()
        for friend in friends:
            pl.semaphore_signal(barrier, inc=1, device_id=friend, device_id_type=MESH)
        pl.semaphore_wait(barrier, len(friends))


def remote(src, dst, send_sem, recv_sem, device):
    return pltpu.make_async_remote_copy(
        src_ref=src,
        dst_ref=dst,
        send_sem=send_sem,
        recv_sem=recv_sem,
        device_id=device,
        device_id_type=MESH,
    )


class Halo:
    def __init__(self, place, edges, halo, sems):
        self.place, self.edges, self.halo, self.sems = place, edges, halo, sems
        self.has_low = place.seq > 0
        self.has_high = place.seq < lax.axis_size("seq") - 1

    @staticmethod
    def scratch(count, width):
        return [
            pltpu.VMEM((2, count, REACH, width), bf16),
            pltpu.VMEM((2, count, REACH, width), bf16),
            pltpu.SemaphoreType.DMA((4, count)),
        ]

    def up(self, i):
        device = {"seq": self.place.seq + 1}
        sems = self.sems
        return remote(self.edges.at[1, i], self.halo.at[0, i], sems.at[0, i], sems.at[1, i], device)

    def down(self, i):
        device = {"seq": self.place.seq - 1}
        sems = self.sems
        return remote(self.edges.at[0, i], self.halo.at[1, i], sems.at[2, i], sems.at[3, i], device)

    def begin(self):
        @pl.when(jnp.logical_not(self.has_low))
        def _():
            self.halo[0] = jnp.zeros_like(self.halo[0])

        @pl.when(jnp.logical_not(self.has_high))
        def _():
            self.halo[1] = jnp.zeros_like(self.halo[1])

    def send(self, i, values):
        self.edges[0, i] = values[:REACH]
        self.edges[1, i] = values[values.shape[0] - REACH :]

        @pl.when(self.has_high)
        def _():
            self.up(i).start()

        @pl.when(self.has_low)
        def _():
            self.down(i).start()

    def take(self, i):
        @pl.when(self.has_low)
        def _():
            self.down(i).wait_send()
            self.up(i).wait_recv()

        @pl.when(self.has_high)
        def _():
            self.up(i).wait_send()
            self.down(i).wait_recv()

    def around(self, pad, i, values):
        fill(pad, self.halo[0, i], values, self.halo[1, i])


class Halves:
    def __init__(self, place, count, out, own, other, sems, arrivals):
        self.place, self.count, self.out = place, count, out
        self.own, self.other, self.sems, self.arrivals = own, other, sems, arrivals

    @staticmethod
    def scratch(count, rows, half):
        return [
            pltpu.VMEM((2, rows, half), bf16),
            pltpu.VMEM((2, rows, half), bf16),
            pltpu.SemaphoreType.DMA((2, 2)),
            pltpu.SemaphoreType.DMA((count,)),
        ]

    def local(self, i, slot):
        to = self.place.core * self.count + i
        return pltpu.make_async_copy(self.own.at[slot], self.out.at[to], self.sems.at[0, slot])

    def away(self, i, slot):
        to = self.place.core * self.count + i
        return remote(
            self.other.at[slot],
            self.out.at[to],
            self.sems.at[1, slot],
            self.arrivals.at[i],
            self.place.other_core(),
        )

    def release(self, i, slot):
        self.local(i, slot).wait()
        self.away(i, slot).wait_send()

    def send(self, i, values):
        slot = i % 2
        half = values.shape[1] // 2
        left, right = values[:, :half], values[:, half:]

        @pl.when(i >= 2)
        def _():
            self.release(i - 2, slot)

        first = self.place.core == 0
        self.own[slot] = jnp.where(first, left, right)
        self.other[slot] = jnp.where(first, right, left)
        self.local(i, slot).start()
        self.away(i, slot).start()

    def end(self):
        for i in range(max(0, self.count - 2), self.count):
            self.release(i, i % 2)

        def body(i, carry):
            self.away(i, 0).wait_recv()
            return carry

        lax.fori_loop(0, self.count, body, 0)


def groups_of(inner, width):
    joined = width + KERNEL * inner
    half = joined // 2
    out, at = [(width // 2, 0, width // 2)], 0
    while at < half:
        rows = min(width // 2, half - at)
        out.append((rows, at, half))
        at += rows
    return out


class BlockSum:
    def __init__(self, place, block, groups, part, out, room):
        self.place, self.block, self.parts, self.out = place, block, part, out
        self.groups, sizes = groups, [g[0] for g in groups]
        self.sizes = sizes
        self.theirs, self.sbuf, self.rbuf, self.res = room[:4]
        self.core_sems, self.send_sems, self.recv_sems, self.out_sems = room[4:]
        self.levels = len(place.stages)
        self.starts = [sum(sizes[:g]) for g in range(len(sizes))]
        sent = [sum(self.lengths(n, self.levels)[1:]) for n in sizes]
        self.bases = [sum(sent[:g]) for g in range(len(sizes))]

    @staticmethod
    def lengths(rows, levels):
        out = [rows]
        for _ in range(levels):
            last = out[-1]
            out.append(last // 2 if last % (2 * UNIT) == 0 else last)
        return out

    @staticmethod
    def scratch(groups, width, levels):
        sizes = [g[0] for g in groups]
        rows, groups = sum(sizes), len(sizes)
        sent = sum(sum(BlockSum.lengths(n, levels)[1:]) for n in sizes)
        dma = pltpu.SemaphoreType.DMA
        return [
            pltpu.VMEM((rows, width), bf16),
            pltpu.VMEM((sent, width), bf16),
            pltpu.VMEM((sent, width), bf16),
            pltpu.VMEM((rows, width), bf16),
            dma((groups, 2)),
            dma((groups, 2 * levels)),
            dma((groups, 2 * levels)),
            dma((groups, 3)),
        ]

    def spots(self, g):
        lengths = self.lengths(self.sizes[g], self.levels)
        start, out = self.starts[g], []
        for s in range(self.levels):
            out.append((start, lengths[s]))
            if lengths[s + 1] < lengths[s]:
                start = start + self.place.bit(s) * lengths[s + 1]
        out.append((start, lengths[-1]))
        return out

    def base(self, g, s):
        return self.bases[g] + sum(self.lengths(self.sizes[g], self.levels)[1 : s + 1])

    def value(self, g, s, start, n):
        lengths, spots = self.lengths(self.sizes[g], self.levels), self.spots(g)
        terms = [
            (self.part(g), self.row(g, self.place.core) + (start - self.starts[g])),
            (self.theirs, start),
        ]
        for k in range(s):
            at = self.base(g, k) + (start - spots[k + 1][0])
            if lengths[k + 1] == lengths[k]:
                terms = [(self.sbuf, at)]
            terms.append((self.rbuf, at))
        total = None
        for ref, at in terms:
            term = ref[pl.ds(pl.multiple_of(at, UNIT), n), :].astype(f32)
            total = term if total is None else total + term
        return total

    def part(self, g):
        return self.parts[0 if g > 0 else 1]

    def row(self, g, half):
        _, at, stride = self.groups[g]
        return at + half * stride

    def core_copy(self, g):
        n = self.sizes[g]
        source = pl.multiple_of(self.row(g, 1 - self.place.core), UNIT)
        return remote(
            self.part(g).at[pl.ds(source, n)],
            self.theirs.at[pl.ds(self.starts[g], n)],
            self.core_sems.at[g, 0],
            self.core_sems.at[g, 1],
            self.place.other_core(),
        )

    def down(self, g, s):
        n = self.lengths(self.sizes[g], self.levels)[s + 1]
        at = pl.ds(self.base(g, s), n)
        return remote(
            self.sbuf.at[at],
            self.rbuf.at[at],
            self.send_sems.at[g, s],
            self.recv_sems.at[g, s],
            self.place.peer(s),
        )

    def start_down(self, g, s):
        start, rows = self.spots(g)[s]
        n = self.lengths(self.sizes[g], self.levels)[s + 1]
        if n < rows:
            start = start + (1 - self.place.bit(s)) * n
        base = self.base(g, s)
        self.sbuf[base : base + n, :] = self.value(g, s, start, n).astype(bf16)
        self.down(g, s).start()

    def up(self, g, s):
        lengths = self.lengths(self.sizes[g], self.levels)
        if lengths[s] == lengths[s + 1]:
            return None
        start, n = self.spots(g)[s + 1]
        at = pl.ds(pl.multiple_of(start, UNIT), n)
        return remote(
            self.res.at[at],
            self.res.at[at],
            self.send_sems.at[g, self.levels + s],
            self.recv_sems.at[g, self.levels + s],
            self.place.peer(s),
        )

    def target(self, g, half):
        n, at = self.sizes[g], self.row(g, half)
        narrow, dilated, restore = self.out
        if g == 0:
            return restore.at[:, pl.ds(at, n)]
        top = narrow.shape[0]
        return narrow.at[pl.ds(at, n)] if at < top else dilated.at[pl.ds(at - top, n)]

    def keep(self, g, half):
        at = pl.ds(self.starts[g], self.sizes[g])
        return pltpu.make_async_copy(self.res.at[at], self.target(g, half), self.out_sems.at[g, 0])

    def give(self, g, half):
        at = pl.ds(self.starts[g], self.sizes[g])
        return remote(
            self.res.at[at],
            self.target(g, half),
            self.out_sems.at[g, 1],
            self.out_sems.at[g, 2],
            self.place.other_core(),
        )

    def steps(self):
        return 2 * self.levels + 3

    def step(self, g, t):
        core, levels = self.place.core, self.levels
        if t == 0:
            self.core_copy(g).start()
        if t == 1:
            self.core_copy(g).wait()
        if 2 <= t < 2 + levels:
            self.down(g, t - 2).wait()
        if 1 <= t < 1 + levels:
            self.start_down(g, t - 1)
        if t == 1 + levels:
            start, n = self.spots(g)[levels]
            at = pl.ds(pl.multiple_of(start, UNIT), n)
            self.res[at, :] = self.value(g, levels, start, n).astype(bf16)
        if 2 + levels <= t < 2 + 2 * levels:
            copy = self.up(g, 2 * levels + 1 - t)
            if copy is not None:
                copy.wait()
        if 1 + levels <= t < 1 + 2 * levels:
            copy = self.up(g, 2 * levels - t)
            if copy is not None:
                copy.start()
        if t == 1 + 2 * levels:
            for half in (0, 1):

                @pl.when(core == half)
                def _():
                    if half == self.block:
                        self.keep(g, half).start()
                    else:
                        self.give(g, half).start()

        if t == 2 + 2 * levels:
            for half in (0, 1):

                @pl.when(core == half)
                def _():
                    if half == self.block:
                        self.keep(g, half).wait()
                        self.give(g, 1 - half).wait_recv()
                    else:
                        self.give(g, half).wait_send()


SEQ_TIMES = (5.0, 2.1, 2.5)
AFTER_TIME = 0.7
LATENCY = 3.5
CHIP_RATE = 1.0e5
CORE_RATE = 5.0e5


def plan(place, groups, width, begins, spans):
    levels = len(place.stages)
    times, now = [], 0.0
    for steps, length in (*spans, (400, AFTER_TIME)):
        for _ in range(steps):
            times.append(now)
            now += length

    def sent(g, t):
        rows = groups[g][0]
        lengths = BlockSum.lengths(rows, levels)
        size = 2 * width
        if t in (0, 2 * levels + 1):
            return "pipe", rows * size / CORE_RATE
        s = t - 1 if t <= levels else 2 * levels - t
        axis, bit, _ = place.stages[s]
        flows = 1 if axis == "seq" else 2 << bit
        if t > levels and lengths[s] == lengths[s + 1]:
            flows = 0
        return axis, lengths[s + 1] * size * flows / CHIP_RATE

    due, free = {}, {}
    ready = {(block, g): times[at] for block, g, at in begins}
    tick = dict.fromkeys(ready, 0)
    for k, now in enumerate(times):
        for key in [key for key in ready if ready[key] <= now]:
            t = tick[key]
            due.setdefault(k, []).append((*key, t))
            tick[key] += 1
            if t == 2 * levels + 2:
                del ready[key]
                continue
            link, busy = sent(key[1], t)
            free[link] = max(free.get(link, 0.0), now) + busy
            ready[key] = free[link] + LATENCY
    assert not ready
    return due


class SmallSum:
    def __init__(self, place, total, arrived, sems):
        self.place, self.total, self.arrived, self.sems = place, total, arrived, sems
        self.stages = len(place.stages) + 1

    @staticmethod
    def scratch(rows, width, levels):
        return [
            pltpu.VMEM((levels + 2, rows, width), f32),
            pltpu.VMEM((levels + 1, rows, width), f32),
            pltpu.SemaphoreType.DMA((levels + 1, 2)),
        ]

    def copy(self, s):
        device = self.place.other_core() if s == 0 else self.place.peer(s - 1)
        return remote(
            self.total.at[s], self.arrived.at[s], self.sems.at[s, 0], self.sems.at[s, 1], device
        )

    def start(self, s):
        self.copy(s).start()

    def end(self, s):
        self.copy(s).wait()
        self.total[s + 1] = self.total[s] + self.arrived[s]


def gather_small(total, block, bias_ref, upper_ref, wide_ref, small_ref):
    half = total.shape[-1]
    rows = []
    for ref in (wide_ref, bias_ref):
        for k in range(ref.shape[0] // 8):
            for lane in range(0, ref.shape[1], half):
                rows.append((ref, k, lane))
    for ref, k in ((small_ref, 0), (upper_ref, 0), (small_ref, 1), (small_ref, 2), (upper_ref, 1), (upper_ref, 2)):
        rows.append((ref, k, 0))
    for j, (ref, k, lane) in enumerate(rows):
        piece = ref[8 * k : 8 * k + 8, lane : lane + half]
        total[0, 16 * block + j : 16 * block + j + 1, :] = jnp.sum(piece, axis=0, keepdims=True)


def block_out_back(back, grad_low, restore, restore_sum, bias_sum, upper_sum):
    restore_sum[...] += dot_tn(back.act, grad_low)
    bias_sum[...] += fold(grad_low.astype(f32))
    gv, gain, shift = back.grad(dot_nt(grad_low, restore[...]))
    gm = gv.astype(bf16)
    upper_sum[0:8] += fold(gm.astype(f32))
    upper_sum[8:16] += gain
    upper_sum[16:24] += shift
    return gm


def convolution_back(hidden, gm, windows, gm_taps, inner, dilated, dilated_sum, small_sum):
    width = dilated.shape[1]
    grad_second = None
    for k, piece in enumerate(gm_taps):
        term = dot_nt(piece, dilated[k * width : (k + 1) * width, :])
        grad_second = term if grad_second is None else grad_second + term
    dilated_sum[...] += dot_tn(windows(), gm())
    back = Back(hidden(), inner_row(inner, 2), inner_row(inner, 3))
    gv, gain, shift = back.grad(grad_second)
    gh = gv.astype(bf16)
    small_sum[0:8] += fold(gh.astype(f32))
    small_sum[8:16] += gain
    small_sum[16:24] += shift
    return gh


def stream_back(first, gh, narrow, wide_sum):
    gx, gain, shift = first.grad(dot_nt(gh, narrow[...]))
    wide_sum[0:8] += gain
    wide_sum[8:16] += shift
    return gx


def clear(*refs):
    for ref in refs:
        ref[...] = jnp.zeros_like(ref)


class Refs:
    def __init__(self, names, refs):
        for name, ref in zip(names, refs, strict=True):
            setattr(self, name, ref)


def whole(names, count, groups, residues, *refs):
    r = Refs(names, refs)
    place = Place()
    core = place.core
    rows, width = r.inputs.shape[1:]
    inner = r.narrow.shape[2]
    small_counts = SmallSum(place, *r.count_room)
    halos = [Halo(place, *room) for room in r.halo_rooms]
    outputs = Halves(place, count, r.block_output, *r.halves_room)
    grads = Halves(place, count, r.input_grad, *r.grads_room)
    outer, joined, restore = r.outer_v, r.joined_v, r.restore_v
    narrow = [joined.at[b, 0:width] for b in (0, 1)]
    dilated = [joined.at[b, width : width + KERNEL * inner] for b in (0, 1)]
    params = (
        (r.outer, lambda at: outer.at[at]),
        (r.narrow, lambda at: joined.at[at, 0:width]),
        (r.dilated, lambda at: joined.at[at, width : width + KERNEL * inner]),
        (r.restore, lambda at: restore.at[at]),
    )
    parts = [(joined.at[1], r.restore_parts[0]), (r.joined_part, r.restore_parts[1])]
    totals = (r.narrow_total, r.dilated_total, r.restore_total)
    sets = [BlockSum(place, b, groups, parts[b], totals, r.sum_rooms[b]) for b in (0, 1)]
    seqs = [n if count % n == 0 else 1 for n in STEP_SEQS]
    stage_steps = [count // n for n in seqs]

    def local(k):
        src, dst = params[k]
        return pltpu.make_async_copy(src, dst(pl.ds(core, 1)), r.param_sems.at[0, k])

    def away(k):
        src, dst = params[k]
        to = dst(pl.ds(core, 1))
        return remote(src, to, r.param_sems.at[1, k], r.param_sems.at[2, k], place.other_core())

    def arrive(k, block):
        @pl.when(core == block)
        def _():
            local(k).wait()

        @pl.when(core != block)
        def _():
            away(k).wait_recv()

    def over(stage, body, ins, outs):
        n, steps = seqs[stage], stage_steps[stage]

        def spec(a, own):
            shape = (n, *a.shape[1:])
            if own:
                return pl.BlockSpec(shape, lambda i: (core * steps + i, 0, 0))
            return pl.BlockSpec(shape, lambda i: (i, 0, 0))

        def flat(*blocks):
            def reader(ref):
                return lambda: ref[...].reshape(n * rows, ref.shape[2])

            def writer(ref):
                def write(v):
                    ref[...] = v.astype(ref.dtype).reshape(ref.shape)

                return write

            cut = len(ins)
            body(pl.program_id(0), *map(reader, blocks[:cut]), *map(writer, blocks[cut:]))

        pipe = pltpu.emit_pipeline(
            flat,
            grid=(steps,),
            in_specs=[spec(a, a is r.inputs or a is r.cotangent) for a in ins],
            out_specs=[spec(a, False) for a in outs],
        )
        pipe(*ins, *outs)

    def each(stage, i):
        n = seqs[stage]
        return [(i * n + j, slice(j * rows, (j + 1) * rows)) for j in range(n)]

    def surround(stage, halo, pads, i, values):
        for j, (at, part) in enumerate(each(stage, i)):
            halo.around(pads.at[j], at, values[part])

    def tapped(stage, pads, d, direction):
        found = [taps(pads.at[j], rows, d, direction) for j in range(seqs[stage])]
        return [jnp.concatenate(pieces, axis=0) for pieces in zip(*found)]

    def windows_of(stage, pads, d):
        return jnp.concatenate(tapped(stage, pads, d, 1), axis=1)

    def take(stage, halo, i):
        for at, _ in each(stage, i):
            halo.take(at)

    def send(stage, sender, i, values):
        for at, part in each(stage, i):
            sender.send(at, values[part])

    def seed_of(stage, i, cot):
        return jnp.concatenate([seeded(cot[part], flags_of(at)) for at, part in each(stage, i)], axis=0)

    def flags_of(i):
        masked = jnp.sum(small_counts.total[small_counts.stages][1:2, :], axis=1, keepdims=True)
        return r.flags[core * count + i] * (residues / masked)

    place.greet(place.line() + place.partners())
    for k in range(len(params)):
        local(k).start()
        away(k).start()
    small_counts.total[1] = r.counts[...]
    for halo in halos:
        halo.begin()
    clear(r.narrow_sum, r.dilated_sum, r.restore_sum)
    clear(*r.wide_sums, *r.bias_sums, *r.upper_sums, *r.small_sums)
    for k in range(2):
        arrive(k, 0)

    def count_step(k):
        if k > 1:
            small_counts.end(k - 1)
        small_counts.start(k)

    def first(i, x, act_out, hidden_out, second_out):
        for k in range(1, min(small_counts.stages, stage_steps[0])):

            @pl.when(i == k)
            def _():
                count_step(k)

        act = norm_act(x().astype(f32), row(outer.at[0], 0), row(outer.at[0], 1))
        act_out(act)
        hidden = dot(act, narrow[0][...]) + inner_row(outer.at[0], 0)
        hidden_out(hidden)
        second = norm_act(hidden, inner_row(outer.at[0], 2), inner_row(outer.at[0], 3))
        second_out(second)
        send(0, halos[0], i, second)

    over(0, first, [r.inputs], [r.first0, r.hidden0, r.second0])
    for k in range(stage_steps[0], small_counts.stages):
        count_step(k)
    small_counts.end(small_counts.stages - 1)
    r.counts_out[...] = small_counts.total[small_counts.stages]
    for k in range(len(params)):
        away(k).wait_send()
        arrive(k, 1)
        if k >= 2:
            arrive(k, 0)

    def second(i, x, second_in, mixed_out, middle_out, hidden_out, second_out):
        take(1, halos[0], i)
        surround(1, halos[0], r.pads, i, second_in())
        windows = windows_of(1, r.pads, FIRST_DILATION)
        mixed = dot(windows, dilated[0][...]) + inner_row(outer.at[0], 1)
        mixed_out(mixed)
        third = norm_act(mixed, inner_row(outer.at[0], 4), inner_row(outer.at[0], 5))
        y = x().astype(f32) + (dot(third, restore[0]) + row(outer.at[0], 2))
        middle_out(y)
        act = norm_act(y, row(outer.at[1], 0), row(outer.at[1], 1))
        hidden = dot(act, narrow[1][...]) + inner_row(outer.at[1], 0)
        hidden_out(hidden)
        second = norm_act(hidden, inner_row(outer.at[1], 2), inner_row(outer.at[1], 3))
        second_out(second)
        send(1, halos[1], i, second)

    over(1, second, [r.inputs, r.second0], [r.mixed0, r.middle, r.hidden1, r.second1])

    def turn(i, second_in, cot, third_out, gm_out):
        take(2, halos[1], i)
        surround(2, halos[1], r.pads, i, second_in())
        windows = windows_of(2, r.pads, SECOND_DILATION)
        mixed = dot(windows, dilated[1][...]) + inner_row(outer.at[1], 1)
        back = Back(mixed, inner_row(outer.at[1], 4), inner_row(outer.at[1], 5))
        third_out(back.act)
        grad_low = seed_of(2, i, cot()).astype(bf16)
        gm = block_out_back(back, grad_low, restore.at[1], r.restore_sum, r.bias_sums[1], r.upper_sums[1])
        gm_out(gm)
        send(2, halos[2], i, gm)

    over(2, turn, [r.second1, r.cotangent], [r.third1, r.gm1])
    write_restore(r.restore_parts[1], r.restore_sum)
    clear(r.restore_sum)

    spans = [(steps, n * time) for steps, n, time in zip(stage_steps[3:], seqs[3:], SEQ_TIMES)]
    fifth, sixth = stage_steps[3], stage_steps[3] + stage_steps[4]
    ends = sixth + stage_steps[5]
    begins = [(1, 0, 0)]
    begins += [(1, g, fifth) for g in range(1, len(groups))]
    begins += [(0, 0, fifth)]
    begins += [(0, g, sixth) for g in range(1, len(groups))]
    due = plan(place, groups, inner, begins, spans)

    def beside(base, steps, i):
        for k in range(steps):
            if base + k in due:

                @pl.when(i == k)
                def _():
                    for block, g, t in due[base + k]:
                        sets[block].step(g, t)

    def between(i, middle, cot, hidden, second_in, gm, mixed, gx_out, gm_out):
        beside(0, stage_steps[3], i)
        take(3, halos[2], i)
        surround(3, halos[2], r.gm_pads, i, gm())
        surround(3, halos[1], r.pads, i, second_in())
        gh = convolution_back(
            hidden,
            gm,
            lambda: windows_of(3, r.pads, SECOND_DILATION),
            tapped(3, r.gm_pads, SECOND_DILATION, -1),
            outer.at[1],
            dilated[1],
            r.dilated_sum,
            r.small_sums[1],
        )
        first = Back(middle().astype(f32), row(outer.at[1], 0), row(outer.at[1], 1))
        r.narrow_sum[...] += dot_tn(first.act, gh)
        gx = seed_of(3, i, cot()) + stream_back(first, gh, narrow[1], r.wide_sums[1])
        gx_out(gx)
        back = Back(mixed(), inner_row(outer.at[0], 4), inner_row(outer.at[0], 5))
        gm = block_out_back(back, gx.astype(bf16), restore.at[0], r.restore_sum, r.bias_sums[0], r.upper_sums[0])
        gm_out(gm)
        send(3, halos[3], i, gm)

    over(3, between, [r.middle, r.cotangent, r.hidden1, r.second1, r.gm1, r.mixed0], [r.gx1, r.gm0])
    write_joined(r.joined_part, r.narrow_sum, r.dilated_sum)
    write_restore(r.restore_parts[0], r.restore_sum)
    clear(r.narrow_sum, r.dilated_sum)

    def inward(i, act, hidden, second_in, gm, gh_out):
        beside(fifth, stage_steps[4], i)
        take(4, halos[3], i)
        surround(4, halos[3], r.gm_pads, i, gm())
        surround(4, halos[0], r.pads, i, second_in())
        gh = convolution_back(
            hidden,
            gm,
            lambda: windows_of(4, r.pads, FIRST_DILATION),
            tapped(4, r.gm_pads, FIRST_DILATION, -1),
            outer.at[0],
            dilated[0],
            r.dilated_sum,
            r.small_sums[0],
        )
        gh_out(gh)
        r.narrow_sum[...] += dot_tn(act(), gh)

    over(4, inward, [r.first0, r.hidden0, r.second0, r.gm0], [r.gh0])
    write_joined(joined.at[1], r.narrow_sum, r.dilated_sum)

    def last(i, x, gx_in, gh, middle, third):
        beside(sixth, stage_steps[5], i)
        y = middle().astype(f32) + (dot(third(), restore[1]) + row(outer.at[1], 2))
        send(5, outputs, i, y.astype(bf16))
        first = Back(x().astype(f32), row(outer.at[0], 0), row(outer.at[0], 1))
        gx = gx_in().astype(f32) + stream_back(first, gh(), narrow[0], r.wide_sums[0])
        send(5, grads, i, gx.astype(bf16))

    over(5, last, [r.inputs, r.gx1, r.gh0, r.middle, r.third1], [])

    small = SmallSum(place, *r.small_room)
    small.total[0] = jnp.zeros_like(small.total[0])
    for b in (0, 1):
        gather_small(small.total, b, r.bias_sums[b], r.upper_sums[b], r.wide_sums[b], r.small_sums[b])
    after = sorted(at for at in due if at >= ends)
    for t in range(max(len(after), small.stages + 1)):
        if t < len(after):
            for block, g, k in due[after[t]]:
                sets[block].step(g, k)
        if 0 < t <= small.stages:
            small.end(t - 1)
        if t < small.stages:
            small.start(t)
    r.small_out[...] = small.total[small.stages]
    outputs.end()
    grads.end()


def write_restore(part, total):
    inner, wide = total.shape
    for j in range(wide // inner):
        at = j * inner
        part[at : at + inner, :] = total[:, j * inner : (j + 1) * inner].astype(bf16)


def write_joined(part, narrow_sum, dilated_sum):
    cut, deep = narrow_sum.shape[0], dilated_sum.shape[0]
    part[:cut, :] = narrow_sum[...].astype(bf16)
    part[cut : cut + deep, :] = dilated_sum[...].astype(bf16)


def shards(
    inputs,
    cotangent,
    mask_flags,
    residue_types,
    predicted,
    outer_params,
    narrow,
    dilated,
    restore,
    inner_params,
):
    core = lax.axis_index("pipe")
    chip_seqs, rows, width = inputs.shape
    inner = narrow.shape[-1]
    count = chip_seqs // 2
    half = width // 2
    levels = bits_of(lax.axis_size("seq")) + bits_of(lax.axis_size("dp"))
    type_ids = jnp.arange(TYPES, dtype=jnp.int32)
    matches = residue_types[:, :, None] == type_ids
    right_flags = mask_flags * (predicted == residue_types).astype(jnp.int32)
    right_counts = jnp.sum(jnp.where(matches, right_flags[:, :, None], 0), axis=(0, 1))
    masked_counts = jnp.sum(jnp.where(matches, mask_flags[:, :, None], 0), axis=(0, 1))
    counts = jnp.stack([right_counts, masked_counts]).astype(f32)
    counts = jnp.pad(counts, ((0, 8 - 2), (0, 128 - TYPES)))

    flags = mask_flags.astype(f32)[:, None, :]
    groups = groups_of(inner, width)
    residues = float(chip_seqs * lax.axis_size("dp") * LENGTH)
    deep = KERNEL * inner
    any_space, vmem = pl.BlockSpec(memory_space=pl.ANY), pl.BlockSpec(memory_space=pltpu.VMEM)
    packed = jnp.concatenate([outer_params, inner_params.reshape(1, 3, width)], axis=1)
    packed = jnp.pad(packed, ((0, 0), (0, 2), (0, 0)))
    args = [
        ("inputs", inputs, any_space),
        ("cotangent", cotangent, any_space),
        ("flags", flags, vmem),
        ("counts", counts, vmem),
        ("outer", packed, any_space),
        ("narrow", narrow, any_space),
        ("dilated", dilated.reshape(1, deep, inner), any_space),
        ("restore", restore, any_space),
    ]
    results = [
        ("block_output", (chip_seqs, rows, half), bf16, any_space),
        ("input_grad", (chip_seqs, rows, half), bf16, any_space),
        ("narrow_total", (width, inner), bf16, any_space),
        ("dilated_total", (deep, inner), bf16, any_space),
        ("restore_total", (inner, width), bf16, any_space),
        ("small_out", (32, inner), f32, vmem),
        ("counts_out", (8, 128), f32, vmem),
        ("third1", (count, rows, inner), bf16, any_space),
        ("first0", (count, rows, width), bf16, any_space),
        ("gh0", (count, rows, inner), bf16, any_space),
        ("hidden0", (count, rows, inner), f32, any_space),
        ("hidden1", (count, rows, inner), f32, any_space),
        ("mixed0", (count, rows, inner), f32, any_space),
        ("middle", (count, rows, width), KEPT, any_space),
        ("gx1", (count, rows, width), KEPT, any_space),
        ("second0", (count, rows, inner), bf16, any_space),
        ("second1", (count, rows, inner), bf16, any_space),
        ("gm0", (count, rows, inner), bf16, any_space),
        ("gm1", (count, rows, inner), bf16, any_space),
    ]

    def twice(a):
        return pltpu.VMEM((2, *a.shape[1:]), a.dtype)

    def sums(*shape):
        return pltpu.VMEM(shape, f32)

    scratch = [
        ("outer_v", twice(packed)),
        ("joined_v", pltpu.VMEM((2, width + deep, inner), bf16)),
        ("restore_v", twice(restore)),
        ("param_sems", pltpu.SemaphoreType.DMA((3, 5))),
        ("count_room", SmallSum.scratch(8, 128, levels)),
        ("small_room", SmallSum.scratch(32, inner, levels)),
        ("halo_rooms", [Halo.scratch(count, inner) for _ in range(4)]),
        ("halves_room", Halves.scratch(count, rows, half)),
        ("grads_room", Halves.scratch(count, rows, half)),
        ("pads", sums(max(STEP_SEQS), rows + 2 * REACH, inner)),
        ("gm_pads", sums(max(STEP_SEQS[3:5]), rows + 2 * REACH, inner)),
        ("narrow_sum", sums(width, inner)),
        ("dilated_sum", sums(deep, inner)),
        ("restore_sum", sums(inner, width)),
        ("wide_sums", [sums(16, width)] * 2),
        ("bias_sums", [sums(8, width)] * 2),
        ("upper_sums", [sums(24, inner)] * 2),
        ("small_sums", [sums(24, inner)] * 2),
        ("restore_parts", [pltpu.VMEM((width, inner), bf16)] * 2),
        ("joined_part", pltpu.VMEM((width + deep, inner), bf16)),
        ("sum_rooms", [BlockSum.scratch(groups, inner, levels) for _ in range(2)]),
    ]
    names = [a[0] for a in args] + [a[0] for a in results] + [a[0] for a in scratch]
    outs = pl.pallas_call(
        functools.partial(whole, names, count, groups, residues),
        out_shape=[jax.ShapeDtypeStruct(shape, dtype) for _, shape, dtype, _ in results],
        in_specs=[a[2] for a in args],
        out_specs=[a[3] for a in results],
        scratch_shapes=[a[1] for a in scratch],
        compiler_params=pltpu.CompilerParams(
            vmem_limit_bytes=VMEM_LIMIT, collective_id=0, has_side_effects=True
        ),
        name="whole",
    )(*[a[1] for a in args])
    block_output, input_grad, narrow_total, dilated_total, restore_total, smalls, counts = outs[:7]
    accuracy = counts[:2, :TYPES].astype(jnp.int32)
    smalls = lax.dynamic_slice_in_dim(smalls, core * 16, 16, 0)
    narrow_total = narrow_total.astype(f32)
    dilated_total = dilated_total.astype(f32)
    restore_total = restore_total.astype(f32)
    outer_total = smalls[: 3 * width // inner].reshape(3, width)
    inner_total = smalls[3 * width // inner :][:6]

    return (
        block_output,
        input_grad,
        outer_total[None],
        narrow_total[None],
        dilated_total.reshape(1, KERNEL, inner, inner),
        restore_total[None],
        inner_total[None],
        accuracy,
    )


def solution(mesh):
    in_specs = (
        P("dp", "seq", None),
        P("dp", "seq", None),
        P("dp", "seq"),
        P("dp", "seq"),
        P("dp", "seq"),
        P("pipe", None, None),
        P("pipe", None, None),
        P("pipe", None, None, None),
        P("pipe", None, None),
        P("pipe", None, None),
    )
    out_specs = (
        P("dp", "seq", "pipe"),
        P("dp", "seq", "pipe"),
        P("pipe", None, None),
        P("pipe", None, None),
        P("pipe", None, None, None),
        P("pipe", None, None),
        P("pipe", None, None),
        P(),
    )
    return jax.shard_map(shards, mesh=mesh, in_specs=in_specs, out_specs=out_specs, check_vma=False)
```
